256 devices in a mesh: gy: 16 (over z, core), gz: 16 (over x, y).
Axes of the slice: x: 4, y: 4, z: 8, core: 2. Of those that a mesh axis runs over, the one named last changes fastest.
Arguments:
- solution: float32 [2, 32, 512, 512], P(None, 'gz', 'gy'), may hold values from -6 to 6
- residual: float32 [2, 32, 512, 512], P(None, 'gz', 'gy'), may hold values from -32 to 32
- sensitivity: bfloat16 [2, 8, 32, 512, 512], P(None, None, 'gz', 'gy'), may hold values from -2 to 2
- sampling: int32 [512, 512], replicated, may hold values from 0 to 1
Outputs:
- new_solution: float32 [2, 32, 512, 512], P(None, 'gz', 'gy')
- new_residual: float32 [2, 32, 512, 512], P(None, 'gz', 'gy')
- new_direction: float32 [2, 32, 512, 512], P(None, 'gz', 'gy')
The draws below stay inside these ranges and needn't reach their ends.
All inputs are finite; a program needn't handle non-finite values.
Results may differ from the reference program's by a relative error of at most 0.0025.
Values sent between devices are 32-bit elements; how exact they have to be, the bound alone decides.
A program may use at most 128 MiB of HBM per device.

```python
import math
import jax
import jax.numpy as jnp
from jax import lax

ROWS = 512
COLS = 512
COILS = 8
NZ = 32


def draw_residual(key, part):
    key = jax.random.fold_in(key, 11)
    key_values, key_columns, key_waves, key_phase = jax.random.split(key, 4)
    zpos = jnp.arange(NZ, dtype=jnp.float32) / (NZ - 1)
    ypos = jnp.arange(ROWS, dtype=jnp.float32) / (ROWS - 1)
    row_index = jnp.arange(ROWS, dtype=jnp.float32) / ROWS
    col_index = jnp.arange(COLS, dtype=jnp.float32) / COLS
    column = jnp.exp(jax.random.uniform(key_columns, (COLS,), minval=-0.69, maxval=0.69))
    waves = jax.random.randint(key_waves, (2, 2, NZ), 0, 4).astype(jnp.float32)
    offset = jax.random.uniform(key_phase, (2, NZ), minval=-math.pi, maxval=math.pi)
    angle = 2.0 * math.pi * (waves[0][:, :, None, None] * row_index[None, None, :, None] + waves[1][:, :, None, None] * col_index[None, None, None, :]) + offset[:, :, None, None]
    wave = jnp.cos(angle)
    values = 0.8 * jnp.clip(jax.random.normal(key_values, (2, NZ, ROWS, COLS)), -4.0, 4.0) + wave
    level = 3.0 ** (zpos[:, None] + ypos[None, :]) / 3.0
    return values * level[None, :, :, None] * column


def draw_sensitivity(key, part):
    key = jax.random.fold_in(key, 23)
    key_noise, key_centre, key_slope, key_offset = jax.random.split(key, 4)
    zpos = jnp.arange(NZ, dtype=jnp.float32) / (NZ - 1)
    ypos = jnp.arange(ROWS, dtype=jnp.float32) / (ROWS - 1)
    xpos = jnp.arange(COLS, dtype=jnp.float32) / (COLS - 1)
    coil_angle = 2.0 * math.pi * jnp.arange(COILS, dtype=jnp.float32) / COILS + jax.random.uniform(key_centre, (COILS,), minval=-0.3, maxval=0.3)
    centre_y = 0.5 + 0.35 * jnp.cos(coil_angle)
    centre_x = 0.5 + 0.35 * jnp.sin(coil_angle)
    slopes = jax.random.uniform(key_slope, (2, COILS), minval=-1.0, maxval=1.0)
    offset = jax.random.uniform(key_offset, (COILS,), minval=-math.pi, maxval=math.pi)
    dist_y = ypos[None, :, None] - centre_y[:, None, None]
    dist_x = xpos[None, None, :] - centre_x[:, None, None]
    envelope = jnp.exp(-(dist_y * dist_y + dist_x * dist_x) / 0.18)
    phase = math.pi * (slopes[0][:, None, None] * ypos[None, :, None] + slopes[1][:, None, None] * xpos[None, None, :]) + offset[:, None, None]
    smooth_map = jnp.stack([envelope * jnp.cos(phase), envelope * jnp.sin(phase)])[:, :, None, :, :]
    shape = (2, COILS, NZ, ROWS, COLS)
    values = 0.45 * smooth_map + 0.15 * jnp.clip(jax.random.normal(key_noise, shape), -4.0, 4.0)
    level = 3.0 ** (0.5 * (zpos[:, None] + ypos[None, :])) / 1.7320508
    return (values * level[None, None, :, :, None]).astype(jnp.bfloat16)


def draw_sampling(key, part):
    key = jax.random.fold_in(key, 37)
    row_freq = jnp.arange(ROWS, dtype=jnp.int32)
    col_freq = jnp.arange(COLS, dtype=jnp.int32)
    row_dist = jnp.minimum(row_freq, ROWS - row_freq)
    col_dist = jnp.minimum(col_freq, COLS - col_freq)
    cycle = jnp.maximum((row_dist * 32 // ROWS)[:, None], (col_dist * 32 // COLS)[None, :])
    threshold = jnp.maximum(12 - 2 * cycle, 2)
    draws = jax.random.randint(key, (ROWS, COLS), 0, 12, dtype=jnp.int32)
    return (draws < threshold).astype(jnp.int32)


def steps_of(rng, dims, shards, least, top_value):
    def one(dim, parts):
        steps = jax.random.uniform(jax.random.fold_in(jax.random.fold_in(rng, 6), dim), (parts,), jnp.float32, least / len(shards), top_value / len(shards))
        return jnp.repeat(jnp.exp(steps), dims[dim] // parts).reshape((-1,) + (1,) * (len(dims) - dim - 1))

    loudness = one(*shards[0])
    for cut in shards[1:]:
        loudness = loudness * one(*cut)
    return loudness


def normal_values(rng, extent, deviation, reach, cuts=(), held_as=jnp.bfloat16):
    values = jax.random.normal(rng, extent, jnp.float32) * deviation
    if len(cuts) > 0:
        values = steps_of(rng, extent, cuts, -0.22, 0.18) * values
    return jnp.clip(values, min=-reach, max=reach).astype(held_as)


def setup_inputs(seed: int = 0) -> dict:
    streams_of = jax.random.split(jax.random.key(seed), 5)
    solution = normal_values(streams_of[0], (2, NZ, ROWS, COLS), 1.0, 6.0, ((1, 16), (2, 16)), jnp.float32)
    residual = draw_residual(jax.random.fold_in(streams_of[4], 71), 0)
    sensitivity = draw_sensitivity(jax.random.fold_in(streams_of[4], 71), 0)
    sampling = draw_sampling(jax.random.fold_in(streams_of[4], 71), 0)
    return {"solution": solution, "residual": residual, "sensitivity": sensitivity, "sampling": sampling}


TV_EPS = 0.1
TV_WEIGHT = 0.1
TIKHONOV = 0.1

def forward_diff(field, axis):
    length = field.shape[axis]
    ahead = lax.slice_in_dim(field, 1, length, axis=axis) - lax.slice_in_dim(field, 0, length - 1, axis=axis)
    zeros = jnp.zeros_like(lax.slice_in_dim(field, 0, 1, axis=axis))
    return jnp.concatenate([ahead, zeros], axis=axis)

def backward_div(flux, axis):
    length = flux.shape[axis]
    zeros = jnp.zeros_like(lax.slice_in_dim(flux, 0, 1, axis=axis))
    before = jnp.concatenate([zeros, lax.slice_in_dim(flux, 0, length - 1, axis=axis)], axis=axis)
    return before - flux

def reference(solution, residual, sensitivity, sampling):
    squares = jnp.zeros(solution.shape[1:], dtype=jnp.float32)
    for axis in (1, 2, 3):
        ahead = forward_diff(solution, axis)
        squares = squares + lax.optimization_barrier(jnp.sum(ahead * ahead, axis=0))
    weight = 1.0 / jnp.sqrt(squares + TV_EPS * TV_EPS)
    smooth = jnp.zeros_like(residual)
    for axis in (1, 2, 3):
        smooth = smooth + backward_div(weight[None] * forward_diff(residual, axis), axis)
    taken = sampling.astype(jnp.float32)
    field = residual[0] + 1j * residual[1]

    def coil_term(total, coil_map):
        coil_float = coil_map.astype(jnp.float32)
        coil_cplx = coil_float[0] + 1j * coil_float[1]
        spectrum = jnp.fft.fft2(coil_cplx * field)
        back = jnp.fft.ifft2(spectrum * taken)
        return (total + jnp.conj(coil_cplx) * back, None)
    total, unused = lax.scan(coil_term, jnp.zeros_like(field), jnp.swapaxes(sensitivity, 0, 1))
    returned = jnp.stack([jnp.real(total), jnp.imag(total)])
    applied = returned - TV_WEIGHT * smooth + TIKHONOV * residual
    norm_old = jnp.sum(residual * residual)
    alpha = norm_old / jnp.sum(residual * applied)
    new_solution = solution + alpha * residual
    new_residual = residual - alpha * applied
    norm_new = jnp.sum(new_residual * new_residual)
    new_direction = new_residual + norm_new / norm_old * residual
    return (new_solution, new_residual, new_direction)
```

```python
import functools

import jax
import jax.numpy as jnp
import ml_dtypes
import numpy as np
from jax import lax
from jax.experimental import pallas as pl
from jax.experimental.pallas import tpu as pltpu
from jax.sharding import PartitionSpec as P

TV_EPS = 0.1
TV_WEIGHT = 0.1
TIKHONOV = 0.1
MESH = pl.DeviceIdType.MESH
F32 = jnp.float32
BF16 = jnp.bfloat16
LANES = 128
NX = 4


def split(x):
    high = x.astype(BF16)
    return high, (x - high.astype(F32)).astype(BF16)


def dot(a, b):
    return jnp.dot(a, b, preferred_element_type=F32)


def dot3(ah, al, bh, bl):
    return dot(ah, bh) + (dot(ah, bl) + dot(al, bh))


def total(x):
    rows = jnp.sum(x, axis=0, keepdims=True)
    n = rows.shape[1] // LANES
    return functools.reduce(jnp.add, [rows[:, i * LANES : (i + 1) * LANES] for i in range(n)])


def interleave(a, b):
    parts = []
    for i in range(a.shape[1] // LANES):
        parts += [a[:, i * LANES : (i + 1) * LANES], b[:, i * LANES : (i + 1) * LANES]]
    return jnp.concatenate(parts, axis=1)


def kernel(
    n, m, sol, res, sens, samp_in, g_in,
    out_app, out_scal,
    sbuf, relay, srecv, xrel, xall, vh, vl, yh, yl, samp, g,
    part, pair, tot, gath, fin, image, smooth,
    hz, hy_s, hy, qz_s, qz, qy_s, qy, ps1_s, ps1, ps2_s, ps2,
    csem, xls, xlr, zs, zr, xrs, xrr, xzs, xar, ms, os,
    prs, prr, gs, gr, fs, fr, hs, hr, p1s, p1r, p2s, p2r,
):
    y = lax.axis_index("gy")
    w = lax.axis_index("gz")
    z, core = y // 2, lax.rem(y, 2)
    x, yy = w // NX, lax.rem(w, NX)
    nz = n // 2
    slab, rows, cols = res.shape[1:]
    sib = 1 - core
    pos = (x, yy)
    odd = lax.rem(z, 2)
    lp = (1 - odd) * x + odd * yy
    sp = z // 2
    l = 2 * lp + core
    line = 2 * NX

    def dev(j, p, z_, core_):
        return (2 * z_ + core_, NX * x + p if j else NX * p + yy)

    def on_line(p, z_, core_):
        return (2 * z_ + core_, (1 - odd) * (NX * p + yy) + odd * (NX * x + p))

    def at_y(t):
        return (t, w)

    def at_z(t):
        return (y, t)

    def across(p, k):
        return (p, p + 1 - 2 * lax.rem(p, 2), lax.rem(p + 2, NX), NX - 1 - p)[k]

    def remote(src, dst, ssem, rsem, device):
        return pltpu.make_async_remote_copy(
            src_ref=src, dst_ref=dst, send_sem=ssem, recv_sem=rsem, device_id=device, device_id_type=MESH
        )

    def loop(lo, hi, f):
        def step(i, c):
            f(i)
            return c

        lax.fori_loop(lo, hi, step, 0)

    barrier = pltpu.get_barrier_semaphore()

    def hail(device):
        pl.semaphore_signal(barrier, inc=1, device_id=device, device_id_type=MESH)

    loop(1, n, lambda k: hail(at_y(lax.rem(y + k, n))))
    loop(1, m, lambda k: hail(at_z(lax.rem(w + k, m))))
    for j in range(slab):
        loop(1, NX, lambda k: hail(dev(j, lax.rem(pos[j] + k, NX), z, sib)))
        hail(dev(j, lax.rem(pos[j] + z, NX), slab * pos[j] + j, core))

    def from_self(j):
        return jnp.logical_and(lax.rem(z, NX) == 0, slab * pos[j] + j == z)

    loads = [
        pltpu.make_async_copy(a, b, csem.at[i]) for i, (a, b) in enumerate([(g_in, g), (samp_in, samp)])
    ]
    for c in loads:
        c.start()

    def widen(c):
        for j in range(slab):
            sbuf[c, j, 0] = sens[0, c, j].astype(F32)
            sbuf[c, j, 1] = sens[1, c, j].astype(F32)

    loop(0, line, widen)

    up_y, down_y = lax.rem(y + 1, n), lax.rem(y + n - 1, n)
    up_z, down_z = lax.rem(w + 1, m), lax.rem(w + m - 1, m)
    for f, field in enumerate((sol, res)):
        for p in range(2):
            for s in range(slab):
                i = f * 2 * slab + p * slab + s
                hy_s[i : i + 1, :] = field[p, s, 0:1, :]

    pl.semaphore_wait(barrier, n + m - 2 + slab * NX)

    moved = lax.rem(z, NX) != 0

    def res_over(j):
        return remote(res.at[:, j], xrel.at[j], xrs.at[j], xrr.at[j], dev(j, lax.rem(pos[j] + z, NX), z, core))

    for j in range(slab):
        @pl.when(moved)
        def _():
            res_over(j).start()

        @pl.when(jnp.logical_not(moved))
        def _():
            xrel[j] = res[:, j]

    steps = [(0, 1), (1, 0), (3, 0), (1, 1), (3, 1), (2, 0), (2, 1)]

    def partner(j, step):
        p = across(pos[j], step[0])
        c = sib if step[1] else core
        return p, c, 2 * p + c

    def maps_over(j, step):
        p, c, t = partner(j, step)
        me = 2 * pos[j] + core
        return remote(sbuf.at[t, j], relay.at[j, me], xls.at[line * j + t], xlr.at[line * j + me], dev(j, p, z, c))

    for step in steps:
        for j in range(slab):
            maps_over(j, step).start()

    halo1 = [
        remote(sol.at[:, 0], hz.at[0], hs.at[0], hr.at[0], at_z(down_z)),
        remote(res.at[:, 0], hz.at[1], hs.at[1], hr.at[1], at_z(down_z)),
        remote(hy_s, hy, hs.at[2], hr.at[2], at_y(down_y)),
    ]
    for h in halo1:
        h.start()

    def pass_on(src, j, t):
        zt = slab * (t // 2) + j
        slot = 2 * z + lax.rem(t, 2)
        cp = remote(src, srecv.at[slot], zs.at[line * j + t], zr.at[slot], dev(0, x, zt, core))
        return zt, slot, cp

    def forward_maps(src, j, t):
        zt, slot, cp = pass_on(src, j, t)

        @pl.when(zt != z)
        def _():
            cp.start()

        @pl.when(zt == z)
        def _():
            srecv[slot] = src[...]

    for j in range(slab):
        t = 2 * pos[j] + core
        forward_maps(sbuf.at[t, j], j, t)

    def forward_res(j):
        zt = slab * lax.rem(pos[j] + NX - lax.rem(z, NX), NX) + j
        return zt, remote(xrel.at[j], xall.at[y], xzs.at[j], xar.at[y], dev(0, x, zt, core))

    for j in range(slab):
        @pl.when(moved)
        def _():
            res_over(j).wait_recv()

        zt, cp = forward_res(j)

        @pl.when(zt != z)
        def _():
            cp.start()

        @pl.when(zt == z)
        def _():
            xall[y] = xrel[j]

    def relay_maps(step):
        for j in range(slab):
            _, _, t = partner(j, step)
            remote(sbuf.at[t, j], relay.at[j, t], xls.at[line * j + t], xlr.at[line * j + t], dev(j, pos[j], z, sib)).wait_recv()
            forward_maps(relay.at[j, t], j, t)

    for step in steps[:3]:
        relay_maps(step)

    first = lax.rem(lp + NX - lax.rem(sp, NX), NX)

    def hand(slot, i, k):
        p = lax.rem(lp + k, NX)
        return remote(xall.at[slot], xall.at[slot], ms.at[i * NX + k], xar.at[slot], on_line(p, z, core))

    def to_other(zz):
        slot = 2 * zz + core
        return remote(xall.at[slot], xall.at[slot], os.at[zz], xar.at[slot], on_line(lp, z, sib))

    for i in range(nz // NX):
        zz = first + NX * i
        slot = 2 * zz + core

        @pl.when(zz != z)
        def _():
            remote(xrel.at[0], xall.at[slot], xzs.at[0], xar.at[slot], dev(0, x, zz, core)).wait_recv()

        for k in range(1, NX):
            hand(slot, i, k).start()
        to_other(zz).start()

    for step in steps[3:]:
        relay_maps(step)

    for h in halo1:
        h.wait_recv()
    row = lax.broadcasted_iota(jnp.int32, (rows, cols), 0)
    col = lax.broadcasted_iota(jnp.int32, (rows, cols), 1)
    keep_y = jnp.logical_or(row < rows - 1, y < n - 1)
    keep_z = jnp.full((rows, cols), w, jnp.int32) < m - 1

    def ahead(f, field, p, s):
        v = field[p, s]
        dx = jnp.where(col == cols - 1, 0.0, pltpu.roll(v, cols - 1, 1) - v)
        i = f * 2 * slab + p * slab + s
        nxt = jnp.where(row == rows - 1, jnp.broadcast_to(hy[i : i + 1, :], (rows, cols)), pltpu.roll(v, rows - 1, 0))
        dy = jnp.where(keep_y, nxt - v, 0.0)
        if s + 1 < slab:
            dz = field[p, s + 1] - v
        else:
            dz = jnp.where(keep_z, hz[f, p] - v, 0.0)
        return dx, dy, dz

    qy_s[...] = jnp.zeros_like(qy_s)
    for s in range(slab):
        sq = jnp.zeros((rows, cols), F32)
        for p in range(2):
            for d in ahead(0, sol, p, s):
                sq = sq + d * d
        weight = 1.0 / jnp.sqrt(sq + TV_EPS * TV_EPS)
        for p in range(2):
            dx, dy, dz = (weight * d for d in ahead(1, res, p, s))
            before_x = jnp.where(col == 0, 0.0, pltpu.roll(dx, 1, 1))
            before_y = jnp.where(row == 0, 0.0, pltpu.roll(dy, 1, 0))
            here = (before_x - dx) + (before_y - dy) - dz
            if s > 0:
                here = here + qz_s[p]
            smooth[p, s] = here
            qz_s[p] = dz
            i = p * slab + s
            qy_s[i : i + 1, :] = dy[rows - 1 : rows, :]
    halo2 = [
        remote(qz_s, qz, hs.at[3], hr.at[3], at_z(up_z)),
        remote(qy_s, qy, hs.at[4], hr.at[4], at_y(up_y)),
    ]
    for h in halo2:
        h.start()

    for k in range(1, NX):
        for i in range(nz // NX):
            zz = lax.rem(first + k, NX) + NX * i
            slot = 2 * zz + core
            remote(xall.at[slot], xall.at[slot], ms.at[0], xar.at[slot], on_line(lax.rem(lp + k, NX), z, core)).wait_recv()
            to_other(zz).start()

    per = 4
    tile = per * rows
    groups = n // per
    loads[0].wait()

    def ready(s):
        zz = s // 2

        @pl.when(zz != z)
        def _():
            remote(relay.at[0, 0], srecv.at[s], zs.at[0], zr.at[s], dev(0, x, zz, core)).wait_recv()

        @pl.when(lax.rem(s, 2) == sib)
        def _():
            remote(xall.at[s], xall.at[s], os.at[0], xar.at[s], on_line(lp, z, sib)).wait_recv()

    def forward_cols(i):
        q = lax.rem(y // per + groups - 1 - i, groups)
        for t in range(per):
            ready(q * per + t)
        block = []
        for t in range(per):
            sr, si = srecv[q * per + t, 0], srecv[q * per + t, 1]
            xr, xi = xall[q * per + t, 0], xall[q * per + t, 1]
            block.append(interleave(sr * xr - si * xi, -(sr * xi + si * xr)))
        ah, al = split(jnp.concatenate(block, axis=0))
        v = dot3(ah, al, g[0], g[1])
        at = pl.ds(pl.multiple_of(q * tile, tile), tile)
        vh[0, at], vl[0, at] = split(v[:, :cols])
        vh[1, at], vl[1, at] = split(-v[:, cols:])

    loop(0, groups, forward_cols)

    full = n * rows
    loads[1].wait()
    scale = 1.0 / (full * cols)

    def forward_rows(t):
        at = pl.ds(pl.multiple_of(2 * t * tile, 2 * tile), 2 * tile)
        h, l_ = g[0, at], g[1, at]
        v = dot3(h[:, :full], l_[:, :full], vh[0], vl[0]) + dot3(h[:, full:], l_[:, full:], vh[1], vl[1])
        k = pl.ds(pl.multiple_of(t * tile, tile), tile)
        taken = samp[k].astype(F32) * scale
        yh[0, k], yl[0, k] = split(v[:tile] * taken)
        yh[1, k], yl[1, k] = split(v[tile:] * -taken)

    loop(0, groups, forward_rows)

    def to_sib(zz):
        return remote(part.at[2 * zz + sib], pair.at[zz], prs.at[zz], prr.at[zz], on_line(lp, z, sib))

    def to_adder(zz):
        t = lax.rem(sp + zz, NX)
        return t, remote(tot.at[zz], gath.at[zz // NX, lp], gs.at[zz], gr.at[NX * (zz // NX) + lp], on_line(t, z, core))

    def add_pair(zz):
        to_sib(zz).wait_recv()
        tot[zz] = part[2 * zz + core] + pair[zz]
        t, cp = to_adder(zz)

        @pl.when(t != lp)
        def _():
            cp.start()

    def home(i):
        zz = first + NX * i
        return zz, remote(fin.at[i], image.at[odd], fs.at[i], fr.at[odd], on_line(sp, zz, core))

    def add_line(i):
        zz, cp = home(i)
        v = tot[zz]
        for k in range(1, NX):
            t = lax.rem(lp + k, NX)
            remote(tot.at[zz], gath.at[i, t], gs.at[zz], gr.at[NX * i + t], on_line(t, z, core)).wait_recv()
            v = v + gath[i, t]
        here = jnp.logical_and(sp == lp, zz == z)

        @pl.when(here)
        def _():
            image[odd] = v

        @pl.when(jnp.logical_not(here))
        def _():
            fin[i] = v
            cp.start()

    def inverse(q):
        at = pl.ds(pl.multiple_of(2 * q * tile, 2 * tile), 2 * tile)
        h, l_ = g[0, at], g[1, at]
        v = dot3(h[:, :full], l_[:, :full], yh[0], yl[0]) + dot3(h[:, full:], l_[:, full:], yh[1], yl[1])
        ah, al = split(interleave(v[:tile], -v[tile:]))
        v = dot3(ah, al, g[0], g[1])
        for t in range(per):
            s = q * per + t
            vr, vi = v[t * rows : (t + 1) * rows, :cols], v[t * rows : (t + 1) * rows, cols:]
            sr, si = srecv[s, 0], srecv[s, 1]
            part[s, 0] = sr * vr + si * vi
            part[s, 1] = sr * vi - si * vr
        for t in range(per // 2):
            to_sib(q * per // 2 + t).start()

        @pl.when(q > 0)
        def _():
            for t in range(per // 2):
                add_pair((q - 1) * per // 2 + t)

        @pl.when(q == groups - 1)
        def _():
            add_line(0)

    loop(0, groups, inverse)
    for t in range(per // 2):
        add_pair((groups - 1) * per // 2 + t)
    add_line(1)

    for h in halo2:
        h.wait_recv()
    at_zero = jnp.full((rows, cols), w, jnp.int32) > 0
    at_top = jnp.logical_and(row == 0, y > 0)
    for p in range(2):
        for s in range(slab):
            i = p * slab + s
            v = smooth[p, s] + jnp.where(at_top, jnp.broadcast_to(qy[i : i + 1, :], (rows, cols)), 0.0)
            if s == 0:
                v = v + jnp.where(at_zero, qz[p], 0.0)
            smooth[p, s] = v

    rr = jnp.zeros((1, LANES), F32)
    ra = jnp.zeros((1, LANES), F32)
    aa = jnp.zeros((1, LANES), F32)
    for s in range(slab):
        @pl.when(jnp.logical_not(from_self(s)))
        def _():
            remote(fin.at[0], image.at[s], fs.at[0], fr.at[s], dev(s, lax.rem(pos[s] + z, NX), slab * pos[s] + s, core)).wait_recv()

        for p in range(2):
            r = res[p, s]
            a = image[s, p] - TV_WEIGHT * smooth[p, s] + TIKHONOV * r
            out_app[p, s] = a
            rr, ra, aa = rr + total(r * r), ra + total(r * a), aa + total(a * a)

    def exchange(send, recv, ssem, rsem, me, size, where):
        recv[me] = send[...]

        def go(k):
            t = lax.rem(me + k, size)
            remote(send, recv.at[me], ssem, rsem, where(t)).start()

        loop(1, size, go)
        others = recv.at[pl.ds(0, size - 1)]
        remote(others, others, ssem, rsem, where(lax.rem(me + 1, size))).wait_recv()
        return functools.reduce(jnp.add, [recv[i] for i in range(size)])

    ps1_s[...] = jnp.zeros_like(ps1_s)
    ps1_s[0:1, :] = rr
    ps1_s[1:2, :] = ra
    ps1_s[2:3, :] = aa
    ps2_s[...] = exchange(ps1_s, ps1, p1s, p1r, y, n, at_y)
    sums = jnp.sum(exchange(ps2_s, ps2, p2s, p2r, w, m, at_z), axis=1, keepdims=True)
    norm_old, curvature, applied2 = sums[0:1], sums[1:2], sums[2:3]
    alpha = norm_old / curvature
    norm_new = jnp.maximum(alpha * alpha * applied2 - norm_old, 0.0)
    out_scal[0:1, :] = jnp.broadcast_to(alpha, (1, cols))
    out_scal[1:2, :] = jnp.broadcast_to(norm_new / norm_old, (1, cols))

    for recv, ssem, rsem, size, there in ((ps1, p1s, p1r, n, at_y(up_y)), (ps2, p2s, p2r, m, at_z(up_z))):
        others = recv.at[pl.ds(0, size - 1)]
        remote(others, others, ssem, rsem, there).wait_send()
    for h in halo1 + halo2:
        h.wait_send()
    for j in range(slab):
        @pl.when(moved)
        def _():
            res_over(j).wait_send()

        for step in steps:
            maps_over(j, step).wait_send()

        def sent_maps(t):
            zt, _, cp = pass_on(sbuf.at[0, j], j, t)

            @pl.when(zt != z)
            def _():
                cp.wait_send()

        loop(0, line, sent_maps)
        zt, cp = forward_res(j)

        @pl.when(zt != z)
        def _():
            cp.wait_send()

    for i in range(nz // NX):
        for k in range(1, NX):
            hand(2 * (first + NX * i) + core, i, k).wait_send()
        zz, cp = home(i)

        @pl.when(jnp.logical_not(jnp.logical_and(sp == lp, zz == z)))
        def _():
            cp.wait_send()

    def sent_sums(zz):
        to_other(zz).wait_send()
        to_sib(zz).wait_send()
        t, cp = to_adder(zz)

        @pl.when(t != lp)
        def _():
            cp.wait_send()

    loop(0, nz, sent_sums)


def matrix(length, rows):
    k = np.arange(length)
    angle = 2.0 * np.pi / length * (np.outer(k, k) % length)
    c, s = np.cos(angle), np.sin(angle)
    g = np.block([[c, s], [-s, c]])
    blocks = length // rows
    g = g.reshape(2, blocks, rows, 2 * length).transpose(1, 0, 2, 3).reshape(2 * length, 2 * length)
    g = g.astype(np.float32)
    h = g.astype(ml_dtypes.bfloat16)
    return np.stack([h, (g - h.astype(np.float32)).astype(ml_dtypes.bfloat16)])


def body(n, m, solution, residual, sensitivity, sampling):
    _, slab, rows, cols = solution.shape
    coils = sensitivity.shape[1]
    full = n * rows
    g = jnp.asarray(matrix(full, LANES))
    vmem = pl.BlockSpec(memory_space=pltpu.VMEM)
    hbm = pl.BlockSpec(memory_space=pl.ANY)
    dma = pltpu.SemaphoreType.DMA
    chunk = (2, rows, cols)

    def f32(*shape):
        return pltpu.VMEM(shape, F32)

    def bf16(*shape):
        return pltpu.VMEM(shape, BF16)

    applied, scal = pl.pallas_call(
        functools.partial(kernel, n, m),
        out_shape=(jax.ShapeDtypeStruct(solution.shape, F32), jax.ShapeDtypeStruct((2, cols), F32)),
        in_specs=[vmem, vmem, vmem, hbm, hbm],
        out_specs=(vmem, vmem),
        scratch_shapes=[
            f32(coils, slab, *chunk), f32(slab, 2 * NX, *chunk), f32(n, *chunk), f32(slab, *chunk), f32(n, *chunk),
            bf16(2, full, cols), bf16(2, full, cols), bf16(2, full, cols), bf16(2, full, cols),
            pltpu.VMEM(sampling.shape, sampling.dtype), bf16(*g.shape),
            f32(n, *chunk), f32(n // 2, *chunk), f32(n // 2, *chunk), f32(n // 2 // NX, NX, *chunk), f32(2, *chunk),
            f32(slab, *chunk), f32(*solution.shape),
            f32(2, *chunk), f32(8, cols), f32(8, cols), f32(*chunk), f32(*chunk), f32(8, cols), f32(8, cols),
            f32(8, LANES), f32(n, 8, LANES), f32(8, LANES), f32(m, 8, LANES),
            dma((2,)), dma((2 * NX * slab,)), dma((2 * NX * slab,)), dma((2 * NX * slab,)), dma((n,)), dma((slab,)), dma((slab,)),
            dma((slab,)), dma((n,)), dma((n // 2 // NX * NX,)), dma((n // 2,)),
            dma((n // 2,)), dma((n // 2,)), dma((n // 2,)), dma((n // 2,)), dma((n // 2 // NX,)), dma((slab,)),
            dma((5,)), dma((5,)), dma, dma, dma, dma,
        ],
        compiler_params=pltpu.CompilerParams(
            collective_id=0, has_side_effects=True, vmem_limit_bytes=56 * 1024 * 1024
        ),
        name="iteration",
    )(solution, residual, sensitivity, sampling, g)
    alpha, beta = scal[0], scal[1]
    new_residual = residual - alpha * applied
    return solution + alpha * residual, new_residual, new_residual + beta * residual


def solution(mesh):
    n, m = mesh.shape["gy"], mesh.shape["gz"]
    field = P(None, "gz", "gy", None)
    return jax.shard_map(
        functools.partial(body, n, m),
        mesh=mesh,
        in_specs=(field, field, P(None, None, "gz", "gy", None), P()),
        out_specs=(field, field, field),
        check_vma=False,
    )
```

```python
import functools

import jax
import jax.numpy as jnp
import ml_dtypes
import numpy as np
from jax import lax
from jax.experimental import pallas as pl
from jax.experimental.pallas import tpu as pltpu
from jax.sharding import PartitionSpec as P

TV_EPS = 0.1
TV_WEIGHT = 0.1
TIKHONOV = 0.1
MESH = pl.DeviceIdType.MESH
F32 = jnp.float32
BF16 = jnp.bfloat16
LANES = 128
NX = 4


def split(x):
    high = x.astype(BF16)
    return high, (x - high.astype(F32)).astype(BF16)


def dot(a, b):
    return jnp.dot(a, b, preferred_element_type=F32)


def dot3(ah, al, bh, bl):
    return dot(ah, bh) + (dot(ah, bl) + dot(al, bh))


def total(x):
    rows = jnp.sum(x, axis=0, keepdims=True)
    n = rows.shape[1] // LANES
    return functools.reduce(jnp.add, [rows[:, i * LANES : (i + 1) * LANES] for i in range(n)])


def interleave(a, b):
    parts = []
    for i in range(a.shape[1] // LANES):
        parts += [a[:, i * LANES : (i + 1) * LANES], b[:, i * LANES : (i + 1) * LANES]]
    return jnp.concatenate(parts, axis=1)


def part_of(v, i):
    return jnp.concatenate([v[:, (2 * b + i) * LANES : (2 * b + i + 1) * LANES] for b in range(v.shape[1] // LANES // 2)], axis=1)


def kernel(
    n, m, sol, res, sens, samp_in, g_in,
    out_app, out_alpha, out_beta,
    sbuf, relay, srecv, xrel, xall, vh, vl, yacc, yh, yl, samp, g,
    part, pair, tot, gath, fin, image, smooth, local, local_in,
    hz, hy_s, hy, qz_s, qz, qy_s, qy, ps1_s, ps1, ps2_s, ps2,
    csem, xls, xlr, zs, zr, xrs, xrr, xzs, xar, ms, os,
    prs, prr, gs, gr, fs, fr, hs, hr, ls, lr, p1s, p1r, p2s, p2r,
):
    y = lax.axis_index("gy")
    w = lax.axis_index("gz")
    z, core = y // 2, lax.rem(y, 2)
    x, yy = w // NX, lax.rem(w, NX)
    nz = n // 2
    slab, rows, cols = res.shape[1:]
    sib = 1 - core
    pos = (x, yy)
    odd = lax.rem(z, 2)
    lp = (1 - odd) * x + odd * yy
    sp = z // 2
    l = 2 * lp + core
    line = 2 * NX

    def dev(j, p, z_, core_):
        return (2 * z_ + core_, NX * x + p if j else NX * p + yy)

    def on_line(p, z_, core_):
        return (2 * z_ + core_, (1 - odd) * (NX * p + yy) + odd * (NX * x + p))

    def at_y(t):
        return (t, w)

    def at_z(t):
        return (y, t)

    def across(p, k):
        return (p, p + 1 - 2 * lax.rem(p, 2), lax.rem(p + 2, NX), NX - 1 - p)[k]

    def remote(src, dst, ssem, rsem, device):
        return pltpu.make_async_remote_copy(
            src_ref=src, dst_ref=dst, send_sem=ssem, recv_sem=rsem, device_id=device, device_id_type=MESH
        )

    def loop(lo, hi, f):
        def step(i, c):
            f(i)
            return c

        lax.fori_loop(lo, hi, step, 0)

    barrier = pltpu.get_barrier_semaphore()

    def hail(device):
        pl.semaphore_signal(barrier, inc=1, device_id=device, device_id_type=MESH)

    loop(1, n, lambda k: hail(at_y(lax.rem(y + k, n))))
    loop(1, m, lambda k: hail(at_z(lax.rem(w + k, m))))
    for j in range(slab):
        loop(1, NX, lambda k: hail(dev(j, lax.rem(pos[j] + k, NX), z, sib)))
        hail(dev(j, lax.rem(pos[j] + z, NX), slab * pos[j] + j, core))

    def from_self(j):
        return jnp.logical_and(lax.rem(z, NX) == 0, slab * pos[j] + j == z)

    loads = [
        pltpu.make_async_copy(a, b, csem.at[i]) for i, (a, b) in enumerate([(g_in, g), (samp_in, samp)])
    ]
    for c in loads:
        c.start()

    def widen(c):
        for j in range(slab):
            sbuf[c, j, 0] = sens[0, c, j].astype(F32)
            sbuf[c, j, 1] = sens[1, c, j].astype(F32)

    loop(0, line, widen)

    up_y, down_y = lax.rem(y + 1, n), lax.rem(y + n - 1, n)
    up_z, down_z = lax.rem(w + 1, m), lax.rem(w + m - 1, m)
    for f, field in enumerate((sol, res)):
        for p in range(2):
            for s in range(slab):
                i = f * 2 * slab + p * slab + s
                hy_s[i : i + 1, :] = field[p, s, 0:1, :]

    pl.semaphore_wait(barrier, n + m - 2 + slab * NX)

    moved = lax.rem(z, NX) != 0

    def res_over(j):
        return remote(res.at[:, j], xrel.at[j], xrs.at[j], xrr.at[j], dev(j, lax.rem(pos[j] + z, NX), z, core))

    for j in range(slab):
        @pl.when(moved)
        def _():
            res_over(j).start()

        @pl.when(jnp.logical_not(moved))
        def _():
            xrel[j] = res[:, j]

    steps = [(0, 1), (1, 0), (3, 0), (1, 1), (3, 1), (2, 0), (2, 1)]

    def partner(j, step):
        p = across(pos[j], step[0])
        c = sib if step[1] else core
        return p, c, 2 * p + c

    def maps_over(j, step):
        p, c, t = partner(j, step)
        me = 2 * pos[j] + core
        return remote(sbuf.at[t, j], relay.at[j, me], xls.at[line * j + t], xlr.at[line * j + me], dev(j, p, z, c))

    for step in steps:
        for j in range(slab):
            maps_over(j, step).start()

    halo1 = [
        remote(sol.at[:, 0], hz.at[0], hs.at[0], hr.at[0], at_z(down_z)),
        remote(res.at[:, 0], hz.at[1], hs.at[1], hr.at[1], at_z(down_z)),
        remote(hy_s, hy, hs.at[2], hr.at[2], at_y(down_y)),
    ]
    for h in halo1:
        h.start()

    def pass_on(src, j, t):
        zt = slab * (t // 2) + j
        slot = 2 * z + lax.rem(t, 2)
        cp = remote(src, srecv.at[slot], zs.at[line * j + t], zr.at[slot], dev(0, x, zt, core))
        return zt, slot, cp

    def forward_maps(src, j, t):
        zt, slot, cp = pass_on(src, j, t)

        @pl.when(zt != z)
        def _():
            cp.start()

        @pl.when(zt == z)
        def _():
            srecv[slot] = src[...]

    for j in range(slab):
        t = 2 * pos[j] + core
        forward_maps(sbuf.at[t, j], j, t)

    def forward_res(j):
        zt = slab * lax.rem(pos[j] + NX - lax.rem(z, NX), NX) + j
        return zt, remote(xrel.at[j], xall.at[y], xzs.at[j], xar.at[y], dev(0, x, zt, core))

    for j in range(slab):
        @pl.when(moved)
        def _():
            res_over(j).wait_recv()

        zt, cp = forward_res(j)

        @pl.when(zt != z)
        def _():
            cp.start()

        @pl.when(zt == z)
        def _():
            xall[y] = xrel[j]

    def relay_maps(step):
        for j in range(slab):
            _, _, t = partner(j, step)
            remote(sbuf.at[t, j], relay.at[j, t], xls.at[line * j + t], xlr.at[line * j + t], dev(j, pos[j], z, sib)).wait_recv()
            forward_maps(relay.at[j, t], j, t)

    for step in steps:
        relay_maps(step)

    first = lax.rem(lp + NX - lax.rem(sp, NX), NX)

    def hand(slot, i, k):
        p = lax.rem(lp + k, NX)
        return remote(xall.at[slot], xall.at[slot], ms.at[i * NX + k], xar.at[slot], on_line(p, z, core))

    def to_other(zz):
        slot = 2 * zz + core
        return remote(xall.at[slot], xall.at[slot], os.at[zz], xar.at[slot], on_line(lp, z, sib))

    for i in range(nz // NX):
        zz = first + NX * i
        slot = 2 * zz + core

        @pl.when(zz != z)
        def _():
            remote(xrel.at[0], xall.at[slot], xzs.at[0], xar.at[slot], dev(0, x, zz, core)).wait_recv()

        for k in range(1, NX):
            hand(slot, i, k).start()
        to_other(zz).start()

    for h in halo1:
        h.wait_recv()
    row = lax.broadcasted_iota(jnp.int32, (rows, cols), 0)
    col = lax.broadcasted_iota(jnp.int32, (rows, cols), 1)
    keep_y = jnp.logical_or(row < rows - 1, y < n - 1)
    keep_z = jnp.full((rows, cols), w, jnp.int32) < m - 1

    def ahead(f, field, p, s):
        v = field[p, s]
        dx = jnp.where(col == cols - 1, 0.0, pltpu.roll(v, cols - 1, 1) - v)
        i = f * 2 * slab + p * slab + s
        nxt = jnp.where(row == rows - 1, jnp.broadcast_to(hy[i : i + 1, :], (rows, cols)), pltpu.roll(v, rows - 1, 0))
        dy = jnp.where(keep_y, nxt - v, 0.0)
        if s + 1 < slab:
            dz = field[p, s + 1] - v
        else:
            dz = jnp.where(keep_z, hz[f, p] - v, 0.0)
        return dx, dy, dz

    qy_s[...] = jnp.zeros_like(qy_s)
    for s in range(slab):
        sq = jnp.zeros((rows, cols), F32)
        for p in range(2):
            for d in ahead(0, sol, p, s):
                sq = sq + d * d
        weight = 1.0 / jnp.sqrt(sq + TV_EPS * TV_EPS)
        for p in range(2):
            dx, dy, dz = (weight * d for d in ahead(1, res, p, s))
            before_x = jnp.where(col == 0, 0.0, pltpu.roll(dx, 1, 1))
            before_y = jnp.where(row == 0, 0.0, pltpu.roll(dy, 1, 0))
            here = (before_x - dx) + (before_y - dy) - dz
            if s > 0:
                here = here + qz_s[p]
            smooth[p, s] = here
            qz_s[p] = dz
            i = p * slab + s
            qy_s[i : i + 1, :] = dy[rows - 1 : rows, :]
    halo2 = [
        remote(qz_s, qz, hs.at[3], hr.at[3], at_z(up_z)),
        remote(qy_s, qy, hs.at[4], hr.at[4], at_y(up_y)),
    ]
    for h in halo2:
        h.start()

    for k in range(1, NX):
        for i in range(nz // NX):
            zz = lax.rem(first + k, NX) + NX * i
            slot = 2 * zz + core
            remote(xall.at[slot], xall.at[slot], ms.at[0], xar.at[slot], on_line(lax.rem(lp + k, NX), z, core)).wait_recv()
            to_other(zz).start()

    per = 4
    tile = per * rows
    groups = n // per

    def ready(s):
        zz = s // 2

        @pl.when(zz != z)
        def _():
            remote(relay.at[0, 0], srecv.at[s], zs.at[0], zr.at[s], dev(0, x, zz, core)).wait_recv()

        @pl.when(lax.rem(s, 2) == sib)
        def _():
            remote(xall.at[s], xall.at[s], os.at[0], xar.at[s], on_line(lp, z, sib)).wait_recv()

    at_zero = jnp.full((rows, cols), w, jnp.int32) > 0
    at_top = jnp.logical_and(row == 0, y > 0)

    def local_over(j):
        there = dev(j, lax.rem(pos[j] + z, NX), slab * pos[j] + j, core)
        return remote(local.at[j], local_in.at[z // NX], ls.at[j], lr.at[z // NX], there)

    def send_local():
        for h in halo2:
            h.wait_recv()
        for p in range(2):
            for s in range(slab):
                i = p * slab + s
                v = smooth[p, s] + jnp.where(at_top, jnp.broadcast_to(qy[i : i + 1, :], (rows, cols)), 0.0)
                if s == 0:
                    v = v + jnp.where(at_zero, qz[p], 0.0)
                local[s, p] = TIKHONOV * res[p, s] - TV_WEIGHT * v
        for j in range(slab):
            @pl.when(jnp.logical_not(from_self(j)))
            def _():
                local_over(j).start()

            @pl.when(from_self(j))
            def _():
                local_in[z // NX] = local[j]

    full = n * rows
    scale = 1.0 / (full * cols)
    yacc[...] = jnp.zeros_like(yacc)
    loads[0].wait()
    loads[1].wait()

    def forward(i):
        q = lax.rem(y // per + groups - 1 - i, groups)
        last = i == groups - 1

        @pl.when(last)
        def _():
            send_local()

        for t in range(per):
            ready(q * per + t)
        block = []
        for t in range(per):
            sr, si = srecv[q * per + t, 0], srecv[q * per + t, 1]
            xr, xi = xall[q * per + t, 0], xall[q * per + t, 1]
            block.append(interleave(sr * xr - si * xi, -(sr * xi + si * xr)))
        ah, al = split(jnp.concatenate(block, axis=0))
        v = dot3(ah, al, g[0], g[1])
        vh[:tile], vl[:tile] = split(part_of(v, 0))
        vh[tile:], vl[tile:] = split(-part_of(v, 1))

        def rows_tile(t):
            at = pl.ds(pl.multiple_of(2 * t * tile, 2 * tile), 2 * tile)
            k = pl.ds(pl.multiple_of(2 * q * tile, 2 * tile), 2 * tile)
            v = yacc[at] + dot3(g[0, at, k], g[1, at, k], vh[...], vl[...])

            @pl.when(jnp.logical_not(last))
            def _():
                yacc[at] = v

            @pl.when(last)
            def _():
                taken = samp[pl.ds(pl.multiple_of(t * tile, tile), tile)].astype(F32) * scale
                yh[at], yl[at] = split(v * jnp.concatenate([taken, -taken], axis=0))

        loop(0, groups, rows_tile)

    loop(0, groups, forward)

    def to_sib(zz):
        return remote(part.at[2 * zz + sib], pair.at[zz], prs.at[zz], prr.at[zz], on_line(lp, z, sib))

    def to_adder(zz):
        t = lax.rem(sp + zz, NX)
        return t, remote(tot.at[zz], gath.at[zz // NX, lp], gs.at[zz], gr.at[NX * (zz // NX) + lp], on_line(t, z, core))

    def add_pair(zz):
        to_sib(zz).wait_recv()
        tot[zz] = part[2 * zz + core] + pair[zz]
        t, cp = to_adder(zz)

        @pl.when(t != lp)
        def _():
            cp.start()

    def home(i):
        zz = first + NX * i
        return zz, remote(fin.at[i], image.at[odd], fs.at[i], fr.at[odd], on_line(sp, zz, core))

    def add_line(i):
        zz, cp = home(i)
        v = tot[zz]
        for k in range(1, NX):
            t = lax.rem(lp + k, NX)
            remote(tot.at[zz], gath.at[i, t], gs.at[zz], gr.at[NX * i + t], on_line(t, z, core)).wait_recv()
            v = v + gath[i, t]

        @pl.when(jnp.logical_not(jnp.logical_and(sp == lp, zz == z)))
        def _():
            remote(local.at[0], local_in.at[i], ls.at[0], lr.at[i], on_line(sp, zz, core)).wait_recv()

        v = v + local_in[i]
        for p in range(2):
            a, r = v[p], xall[2 * zz + core, p]
            ps1_s[0:1, :] += total(r * r)
            ps1_s[1:2, :] += total(r * a)
            ps1_s[2:3, :] += total(a * a)
        here = jnp.logical_and(sp == lp, zz == z)

        @pl.when(here)
        def _():
            image[odd] = v

        @pl.when(jnp.logical_not(here))
        def _():
            fin[i] = v
            cp.start()

    def inverse(q):
        at = pl.ds(pl.multiple_of(2 * q * tile, 2 * tile), 2 * tile)
        v = dot3(g[0, at], g[1, at], yh[...], yl[...])
        ah, al = split(interleave(v[:tile], -v[tile:]))
        v = dot3(ah, al, g[0], g[1])
        re, im = part_of(v, 0), part_of(v, 1)
        for t in range(per):
            s = q * per + t
            vr, vi = re[t * rows : (t + 1) * rows], im[t * rows : (t + 1) * rows]
            sr, si = srecv[s, 0], srecv[s, 1]
            part[s, 0] = sr * vr + si * vi
            part[s, 1] = sr * vi - si * vr
        for t in range(per // 2):
            to_sib(q * per // 2 + t).start()

        @pl.when(q > 0)
        def _():
            for t in range(per // 2):
                add_pair((q - 1) * per // 2 + t)

        @pl.when(q == groups - 1)
        def _():
            add_line(0)

    ps1_s[...] = jnp.zeros_like(ps1_s)
    loop(0, groups, inverse)
    for t in range(per // 2):
        add_pair((groups - 1) * per // 2 + t)
    add_line(1)

    def exchange(send, recv, ssem, rsem, me, size, where):
        recv[me] = send[...]

        def go(k):
            t = lax.rem(me + k, size)
            remote(send, recv.at[me], ssem, rsem, where(t)).start()

        loop(1, size, go)
        others = recv.at[pl.ds(0, size - 1)]
        remote(others, others, ssem, rsem, where(lax.rem(me + 1, size))).wait_recv()
        return functools.reduce(jnp.add, [recv[i] for i in range(size)])

    ps2_s[...] = exchange(ps1_s, ps1, p1s, p1r, y, n, at_y)
    sums = jnp.sum(exchange(ps2_s, ps2, p2s, p2r, w, m, at_z), axis=1, keepdims=True)
    norm_old, curvature, applied2 = sums[0:1], sums[1:2], sums[2:3]
    alpha = norm_old / curvature
    norm_new = jnp.maximum(alpha * alpha * applied2 - norm_old, 0.0)
    out_alpha[...] = jnp.broadcast_to(alpha, (1, cols))
    out_beta[...] = jnp.broadcast_to(norm_new / norm_old, (1, cols))

    for s in range(slab):
        @pl.when(jnp.logical_not(from_self(s)))
        def _():
            remote(fin.at[0], image.at[s], fs.at[0], fr.at[s], dev(s, lax.rem(pos[s] + z, NX), slab * pos[s] + s, core)).wait_recv()

        for p in range(2):
            out_app[p, s] = image[s, p]

    for recv, ssem, rsem, size, there in ((ps1, p1s, p1r, n, at_y(up_y)), (ps2, p2s, p2r, m, at_z(up_z))):
        others = recv.at[pl.ds(0, size - 1)]
        remote(others, others, ssem, rsem, there).wait_send()
    for h in halo1 + halo2:
        h.wait_send()
    for j in range(slab):
        @pl.when(moved)
        def _():
            res_over(j).wait_send()

        @pl.when(jnp.logical_not(from_self(j)))
        def _():
            local_over(j).wait_send()

        for step in steps:
            maps_over(j, step).wait_send()

        def sent_maps(t):
            zt, _, cp = pass_on(sbuf.at[0, j], j, t)

            @pl.when(zt != z)
            def _():
                cp.wait_send()

        loop(0, line, sent_maps)
        zt, cp = forward_res(j)

        @pl.when(zt != z)
        def _():
            cp.wait_send()

    for i in range(nz // NX):
        for k in range(1, NX):
            hand(2 * (first + NX * i) + core, i, k).wait_send()
        zz, cp = home(i)

        @pl.when(jnp.logical_not(jnp.logical_and(sp == lp, zz == z)))
        def _():
            cp.wait_send()

    def sent_sums(zz):
        to_other(zz).wait_send()
        to_sib(zz).wait_send()
        t, cp = to_adder(zz)

        @pl.when(t != lp)
        def _():
            cp.wait_send()

    loop(0, nz, sent_sums)


def matrix(length, rows):
    k = np.arange(length)
    angle = 2.0 * np.pi / length * (np.outer(k, k) % length)
    c, s = np.cos(angle), np.sin(angle)
    g = np.block([[c, s], [-s, c]])
    blocks = length // rows
    order = np.arange(2 * length).reshape(2, blocks, rows).transpose(1, 0, 2).reshape(-1)
    g = g[order][:, order]
    g = g.astype(np.float32)
    h = g.astype(ml_dtypes.bfloat16)
    return np.stack([h, (g - h.astype(np.float32)).astype(ml_dtypes.bfloat16)])


def body(n, m, solution, residual, sensitivity, sampling):
    _, slab, rows, cols = solution.shape
    coils = sensitivity.shape[1]
    full = n * rows
    g = jnp.asarray(matrix(full, LANES))
    vmem = pl.BlockSpec(memory_space=pltpu.VMEM)
    hbm = pl.BlockSpec(memory_space=pl.ANY)
    dma = pltpu.SemaphoreType.DMA
    chunk = (2, rows, cols)

    def f32(*shape):
        return pltpu.VMEM(shape, F32)

    def bf16(*shape):
        return pltpu.VMEM(shape, BF16)

    applied, alpha, beta = pl.pallas_call(
        functools.partial(kernel, n, m),
        out_shape=(jax.ShapeDtypeStruct(solution.shape, F32),) + 2 * (jax.ShapeDtypeStruct((1, cols), F32),),
        in_specs=[vmem, vmem, vmem, hbm, hbm],
        out_specs=(vmem, vmem, vmem),
        scratch_shapes=[
            f32(coils, slab, *chunk), f32(slab, 2 * NX, *chunk), f32(n, *chunk), f32(slab, *chunk), f32(n, *chunk),
            bf16(2 * LANES, cols), bf16(2 * LANES, cols), f32(2 * full, cols), bf16(2 * full, cols), bf16(2 * full, cols),
            pltpu.VMEM(sampling.shape, sampling.dtype), bf16(*g.shape),
            f32(n, *chunk), f32(n // 2, *chunk), f32(n // 2, *chunk), f32(n // 2 // NX, NX, *chunk), f32(2, *chunk),
            f32(slab, *chunk), f32(*solution.shape), f32(slab, *chunk), f32(n // 2 // NX, *chunk),
            f32(2, *chunk), f32(8, cols), f32(8, cols), f32(*chunk), f32(*chunk), f32(8, cols), f32(8, cols),
            f32(8, LANES), f32(n, 8, LANES), f32(8, LANES), f32(m, 8, LANES),
            dma((2,)), dma((2 * NX * slab,)), dma((2 * NX * slab,)), dma((2 * NX * slab,)), dma((n,)), dma((slab,)), dma((slab,)),
            dma((slab,)), dma((n,)), dma((n // 2 // NX * NX,)), dma((n // 2,)),
            dma((n // 2,)), dma((n // 2,)), dma((n // 2,)), dma((n // 2,)), dma((n // 2 // NX,)), dma((slab,)),
            dma((5,)), dma((5,)), dma((slab,)), dma((n // 2 // NX,)), dma, dma, dma, dma,
        ],
        compiler_params=pltpu.CompilerParams(
            collective_id=0, has_side_effects=True, vmem_limit_bytes=56 * 1024 * 1024
        ),
        name="iteration",
    )(solution, residual, sensitivity, sampling, g)
    alpha, beta = alpha[0], beta[0]
    new_residual = residual - alpha * applied
    return solution + alpha * residual, new_residual, new_residual + beta * residual


def solution(mesh):
    n, m = mesh.shape["gy"], mesh.shape["gz"]
    field = P(None, "gz", "gy", None)
    return jax.shard_map(
        functools.partial(body, n, m),
        mesh=mesh,
        in_specs=(field, field, P(None, None, "gz", "gy", None), P()),
        out_specs=(field, field, field),
        check_vma=False,
    )
```

```python
import functools

import jax
import jax.numpy as jnp
import ml_dtypes
import numpy as np
from jax import lax
from jax.experimental import pallas as pl
from jax.experimental.pallas import tpu as pltpu
from jax.sharding import PartitionSpec as P

TV_EPS = 0.1
TV_WEIGHT = 0.1
TIKHONOV = 0.1
MESH = pl.DeviceIdType.MESH
F32 = jnp.float32
BF16 = jnp.bfloat16
LANES = 128
NX = 4


def split(x):
    high = x.astype(BF16)
    return high, (x - high.astype(F32)).astype(BF16)


def dot(a, b):
    return jnp.dot(a, b, preferred_element_type=F32)


def dot3(ah, al, bh, bl):
    return dot(ah, bh) + (dot(ah, bl) + dot(al, bh))


def total(x):
    rows = jnp.sum(x, axis=0, keepdims=True)
    n = rows.shape[1] // LANES
    return functools.reduce(jnp.add, [rows[:, i * LANES : (i + 1) * LANES] for i in range(n)])


def interleave(a, b):
    parts = []
    for i in range(a.shape[1] // LANES):
        parts += [a[:, i * LANES : (i + 1) * LANES], b[:, i * LANES : (i + 1) * LANES]]
    return jnp.concatenate(parts, axis=1)


def part_of(v, i):
    return jnp.concatenate([v[:, (2 * b + i) * LANES : (2 * b + i + 1) * LANES] for b in range(v.shape[1] // LANES // 2)], axis=1)


def kernel(
    n, m, sol, res, sens, samp_in, g_in,
    out_app, out_alpha, out_beta,
    sbuf, relay, srecv, xrel, xall, vh, vl, yacc, yh, yl, samp, g,
    part, pair, tot, gath, fin, image, smooth, local, local_in,
    hz, hy_s, hy, qz_s, qz, qy_s, qy, ps1_s, ps1, ps2_s, ps2,
    csem, xls, xlr, zs, zr, xrs, xrr, xzs, xar, ms, os,
    prs, prr, gs, gr, fs, fr, hs, hr, ls, lr, p1s, p1r, p2s, p2r,
):
    y = lax.axis_index("gy")
    w = lax.axis_index("gz")
    z, core = y // 2, lax.rem(y, 2)
    x, yy = w // NX, lax.rem(w, NX)
    nz = n // 2
    slab, rows, cols = res.shape[1:]
    sib = 1 - core
    pos = (x, yy)
    odd = lax.rem(z, 2)
    lp = (1 - odd) * x + odd * yy
    sp = z // 2
    l = 2 * lp + core
    line = 2 * NX

    def dev(j, p, z_, core_):
        return (2 * z_ + core_, NX * x + p if j else NX * p + yy)

    def on_line(p, z_, core_):
        return (2 * z_ + core_, (1 - odd) * (NX * p + yy) + odd * (NX * x + p))

    def at_y(t):
        return (t, w)

    def at_z(t):
        return (y, t)

    def xor(a, b):
        return 2 * lax.rem(a // 2 + b // 2, 2) + lax.rem(a + b, 2)

    def remote(src, dst, ssem, rsem, device):
        return pltpu.make_async_remote_copy(
            src_ref=src, dst_ref=dst, send_sem=ssem, recv_sem=rsem, device_id=device, device_id_type=MESH
        )

    def loop(lo, hi, f):
        def step(i, c):
            f(i)
            return c

        lax.fori_loop(lo, hi, step, 0)

    barrier = pltpu.get_barrier_semaphore()

    def hail(device):
        pl.semaphore_signal(barrier, inc=1, device_id=device, device_id_type=MESH)

    loop(1, n, lambda k: hail(at_y(lax.rem(y + k, n))))
    loop(1, m, lambda k: hail(at_z(lax.rem(w + k, m))))
    for j in range(slab):
        loop(1, NX, lambda k: hail(dev(j, lax.rem(pos[j] + k, NX), z, sib)))
        hail(dev(j, xor(pos[j], sp), slab * pos[j] + j, core))

    def from_self(j):
        return jnp.logical_and(sp == 0, slab * pos[j] + j == z)

    loads = [
        pltpu.make_async_copy(a, b, csem.at[i]) for i, (a, b) in enumerate([(g_in, g), (samp_in, samp)])
    ]
    for c in loads:
        c.start()

    def widen(c):
        for j in range(slab):
            sbuf[c, j, 0] = sens[0, c, j].astype(F32)
            sbuf[c, j, 1] = sens[1, c, j].astype(F32)

    loop(0, line, widen)

    up_y, down_y = lax.rem(y + 1, n), lax.rem(y + n - 1, n)
    up_z, down_z = lax.rem(w + 1, m), lax.rem(w + m - 1, m)
    for f, field in enumerate((sol, res)):
        for p in range(2):
            for s in range(slab):
                i = f * 2 * slab + p * slab + s
                hy_s[i : i + 1, :] = field[p, s, 0:1, :]

    pl.semaphore_wait(barrier, n + m - 2 + slab * NX)

    moved = sp != 0

    def res_over(j):
        return remote(res.at[:, j], xrel.at[j], xrs.at[j], xrr.at[j], dev(j, xor(pos[j], sp), z, core))

    for j in range(slab):
        @pl.when(moved)
        def _():
            res_over(j).start()

        @pl.when(jnp.logical_not(moved))
        def _():
            xrel[j] = res[:, j]

    steps = [(k, c) for k in range(NX) for c in range(2)]

    def partner(j, step):
        p = xor(pos[j], xor(sp, step[0]))
        c = sib if step[1] else core
        return p, c, 2 * p + c

    def hops(step):
        return jnp.logical_or(sp != step[0], step[1] > 0)

    def maps_over(j, step):
        p, c, t = partner(j, step)
        me = 2 * pos[j] + core
        return remote(sbuf.at[t, j], relay.at[j, me], xls.at[line * j + t], xlr.at[line * j + me], dev(j, p, z, c))

    for step in steps:
        for j in range(slab):
            @pl.when(hops(step))
            def _():
                maps_over(j, step).start()

    halo1 = [
        remote(sol.at[:, 0], hz.at[0], hs.at[0], hr.at[0], at_z(down_z)),
        remote(res.at[:, 0], hz.at[1], hs.at[1], hr.at[1], at_z(down_z)),
        remote(hy_s, hy, hs.at[2], hr.at[2], at_y(down_y)),
    ]
    for h in halo1:
        h.start()

    def pass_on(src, j, t):
        zt = slab * (t // 2) + j
        slot = 2 * z + lax.rem(t, 2)
        cp = remote(src, srecv.at[slot], zs.at[line * j + t], zr.at[slot], dev(0, x, zt, core))
        return zt, slot, cp

    def forward_maps(src, j, t):
        zt, slot, cp = pass_on(src, j, t)

        @pl.when(zt != z)
        def _():
            cp.start()

        @pl.when(zt == z)
        def _():
            srecv[slot] = src[...]

    def forward_res(j):
        zt = slab * xor(pos[j], sp) + j
        return zt, remote(xrel.at[j], xall.at[y], xzs.at[j], xar.at[y], dev(0, x, zt, core))

    for j in range(slab):
        @pl.when(moved)
        def _():
            res_over(j).wait_recv()

        zt, cp = forward_res(j)

        @pl.when(zt != z)
        def _():
            cp.start()

        @pl.when(zt == z)
        def _():
            xall[y] = xrel[j]

    def relay_maps(step):
        for j in range(slab):
            p, c, t = partner(j, step)

            @pl.when(hops(step))
            def _():
                remote(sbuf.at[t, j], relay.at[j, t], xls.at[line * j + t], xlr.at[line * j + t], dev(j, p, z, c)).wait_recv()
                forward_maps(relay.at[j, t], j, t)

            @pl.when(jnp.logical_not(hops(step)))
            def _():
                forward_maps(sbuf.at[t, j], j, t)

    for step in steps:
        relay_maps(step)

    first = 2 * xor(lp, sp)

    def hand(slot, i, k):
        p = xor(lp, k)
        return remote(xall.at[slot], xall.at[slot], ms.at[i * NX + k], xar.at[slot], on_line(p, z, core))

    def to_other(zz):
        slot = 2 * zz + core
        return remote(xall.at[slot], xall.at[slot], os.at[zz], xar.at[slot], on_line(lp, z, sib))

    for i in range(nz // NX):
        zz = first + i
        slot = 2 * zz + core

        @pl.when(zz != z)
        def _():
            remote(xrel.at[0], xall.at[slot], xzs.at[0], xar.at[slot], dev(0, x, zz, core)).wait_recv()

        for k in range(1, NX):
            hand(slot, i, k).start()
        to_other(zz).start()

    for h in halo1:
        h.wait_recv()
    row = lax.broadcasted_iota(jnp.int32, (rows, cols), 0)
    col = lax.broadcasted_iota(jnp.int32, (rows, cols), 1)
    keep_y = jnp.logical_or(row < rows - 1, y < n - 1)
    keep_z = jnp.full((rows, cols), w, jnp.int32) < m - 1

    def ahead(f, field, p, s):
        v = field[p, s]
        dx = jnp.where(col == cols - 1, 0.0, pltpu.roll(v, cols - 1, 1) - v)
        i = f * 2 * slab + p * slab + s
        nxt = jnp.where(row == rows - 1, jnp.broadcast_to(hy[i : i + 1, :], (rows, cols)), pltpu.roll(v, rows - 1, 0))
        dy = jnp.where(keep_y, nxt - v, 0.0)
        if s + 1 < slab:
            dz = field[p, s + 1] - v
        else:
            dz = jnp.where(keep_z, hz[f, p] - v, 0.0)
        return dx, dy, dz

    qy_s[...] = jnp.zeros_like(qy_s)
    for s in range(slab):
        sq = jnp.zeros((rows, cols), F32)
        for p in range(2):
            for d in ahead(0, sol, p, s):
                sq = sq + d * d
        weight = 1.0 / jnp.sqrt(sq + TV_EPS * TV_EPS)
        for p in range(2):
            dx, dy, dz = (weight * d for d in ahead(1, res, p, s))
            before_x = jnp.where(col == 0, 0.0, pltpu.roll(dx, 1, 1))
            before_y = jnp.where(row == 0, 0.0, pltpu.roll(dy, 1, 0))
            here = (before_x - dx) + (before_y - dy) - dz
            if s > 0:
                here = here + qz_s[p]
            smooth[p, s] = here
            qz_s[p] = dz
            i = p * slab + s
            qy_s[i : i + 1, :] = dy[rows - 1 : rows, :]
    halo2 = [
        remote(qz_s, qz, hs.at[3], hr.at[3], at_z(up_z)),
        remote(qy_s, qy, hs.at[4], hr.at[4], at_y(up_y)),
    ]
    for h in halo2:
        h.start()

    for k in range(1, NX):
        for i in range(nz // NX):
            zz = 2 * xor(xor(lp, k), sp) + i
            slot = 2 * zz + core
            remote(xall.at[slot], xall.at[slot], ms.at[0], xar.at[slot], on_line(xor(lp, k), z, core)).wait_recv()
            to_other(zz).start()

    per = 4
    tile = per * rows
    groups = n // per

    def ready(s):
        zz = s // 2

        @pl.when(zz != z)
        def _():
            remote(relay.at[0, 0], srecv.at[s], zs.at[0], zr.at[s], dev(0, x, zz, core)).wait_recv()

        @pl.when(lax.rem(s, 2) == sib)
        def _():
            remote(xall.at[s], xall.at[s], os.at[0], xar.at[s], on_line(lp, z, sib)).wait_recv()

    at_zero = jnp.full((rows, cols), w, jnp.int32) > 0
    at_top = jnp.logical_and(row == 0, y > 0)

    def local_over(j):
        there = dev(j, xor(pos[j], sp), slab * pos[j] + j, core)
        return remote(local.at[j], local_in.at[odd], ls.at[j], lr.at[odd], there)

    def send_local():
        for h in halo2:
            h.wait_recv()
        for p in range(2):
            for s in range(slab):
                i = p * slab + s
                v = smooth[p, s] + jnp.where(at_top, jnp.broadcast_to(qy[i : i + 1, :], (rows, cols)), 0.0)
                if s == 0:
                    v = v + jnp.where(at_zero, qz[p], 0.0)
                local[s, p] = TIKHONOV * res[p, s] - TV_WEIGHT * v
        for j in range(slab):
            @pl.when(jnp.logical_not(from_self(j)))
            def _():
                local_over(j).start()

            @pl.when(from_self(j))
            def _():
                local_in[odd] = local[j]

    full = n * rows
    scale = 1.0 / (full * cols)
    yacc[...] = jnp.zeros_like(yacc)
    loads[0].wait()
    loads[1].wait()

    def forward(i):
        q = xor(xor(lp, sp), i)
        last = i == groups - 1

        @pl.when(last)
        def _():
            send_local()

        for t in range(per):
            ready(q * per + t)
        block = []
        for t in range(per):
            sr, si = srecv[q * per + t, 0], srecv[q * per + t, 1]
            xr, xi = xall[q * per + t, 0], xall[q * per + t, 1]
            block.append(interleave(sr * xr - si * xi, -(sr * xi + si * xr)))
        ah, al = split(jnp.concatenate(block, axis=0))
        v = dot3(ah, al, g[0], g[1])
        vh[:tile], vl[:tile] = split(part_of(v, 0))
        vh[tile:], vl[tile:] = split(-part_of(v, 1))

        def rows_tile(t):
            at = pl.ds(pl.multiple_of(2 * t * tile, 2 * tile), 2 * tile)
            k = pl.ds(pl.multiple_of(2 * q * tile, 2 * tile), 2 * tile)
            v = yacc[at] + dot3(g[0, at, k], g[1, at, k], vh[...], vl[...])

            @pl.when(jnp.logical_not(last))
            def _():
                yacc[at] = v

            @pl.when(last)
            def _():
                taken = samp[pl.ds(pl.multiple_of(t * tile, tile), tile)].astype(F32) * scale
                yh[at], yl[at] = split(v * jnp.concatenate([taken, -taken], axis=0))

        loop(0, groups, rows_tile)

    loop(0, groups, forward)

    def to_sib(zz):
        return remote(part.at[2 * zz + sib], pair.at[zz], prs.at[zz], prr.at[zz], on_line(lp, z, sib))

    def to_adder(zz):
        t = xor(sp, zz // 2)
        i = lax.rem(zz, 2)
        return t, remote(tot.at[zz], gath.at[i, lp], gs.at[zz], gr.at[NX * i + lp], on_line(t, z, core))

    def add_pair(zz):
        to_sib(zz).wait_recv()
        tot[zz] = part[2 * zz + core] + pair[zz]
        t, cp = to_adder(zz)

        @pl.when(t != lp)
        def _():
            cp.start()

    def home(i):
        zz = first + i
        return zz, remote(fin.at[i], image.at[odd], fs.at[i], fr.at[odd], on_line(sp, zz, core))

    def add_line(i):
        zz, cp = home(i)
        v = tot[zz]
        for k in range(1, NX):
            t = xor(lp, k)
            remote(tot.at[zz], gath.at[i, t], gs.at[zz], gr.at[NX * i + t], on_line(t, z, core)).wait_recv()
            v = v + gath[i, t]

        @pl.when(jnp.logical_not(jnp.logical_and(sp == lp, zz == z)))
        def _():
            remote(local.at[0], local_in.at[i], ls.at[0], lr.at[i], on_line(sp, zz, core)).wait_recv()

        v = v + local_in[i]
        for p in range(2):
            a, r = v[p], xall[2 * zz + core, p]
            ps1_s[0:1, :] += total(r * r)
            ps1_s[1:2, :] += total(r * a)
            ps1_s[2:3, :] += total(a * a)
        here = jnp.logical_and(sp == lp, zz == z)

        @pl.when(here)
        def _():
            image[odd] = v

        @pl.when(jnp.logical_not(here))
        def _():
            fin[i] = v
            cp.start()

    def block_at(i):
        return xor(xor(lp, sp), 2 + i - (i // 2) * (2 * i - 1))

    def inverse(i):
        q = block_at(i)
        at = pl.ds(pl.multiple_of(2 * q * tile, 2 * tile), 2 * tile)
        v = dot3(g[0, at], g[1, at], yh[...], yl[...])
        ah, al = split(interleave(v[:tile], -v[tile:]))
        v = dot3(ah, al, g[0], g[1])
        re, im = part_of(v, 0), part_of(v, 1)
        for t in range(per):
            s = q * per + t
            vr, vi = re[t * rows : (t + 1) * rows], im[t * rows : (t + 1) * rows]
            sr, si = srecv[s, 0], srecv[s, 1]
            part[s, 0] = sr * vr + si * vi
            part[s, 1] = sr * vi - si * vr
        for t in range(per // 2):
            to_sib(q * per // 2 + t).start()

        @pl.when(i > 0)
        def _():
            for t in range(per // 2):
                add_pair(block_at(i - 1) * per // 2 + t)

    ps1_s[...] = jnp.zeros_like(ps1_s)
    loop(0, groups, inverse)
    for t in range(per // 2):
        add_pair(first + t)
    for i in range(nz // NX):
        add_line(i)

    def exchange(send, recv, ssem, rsem, me, size, where):
        recv[me] = send[...]

        def go(k):
            t = lax.rem(me + k, size)
            remote(send, recv.at[me], ssem, rsem, where(t)).start()

        loop(1, size, go)
        others = recv.at[pl.ds(0, size - 1)]
        remote(others, others, ssem, rsem, where(lax.rem(me + 1, size))).wait_recv()
        return functools.reduce(jnp.add, [recv[i] for i in range(size)])

    ps2_s[...] = exchange(ps1_s, ps1, p1s, p1r, y, n, at_y)
    sums = jnp.sum(exchange(ps2_s, ps2, p2s, p2r, w, m, at_z), axis=1, keepdims=True)
    norm_old, curvature, applied2 = sums[0:1], sums[1:2], sums[2:3]
    alpha = norm_old / curvature
    norm_new = jnp.maximum(alpha * alpha * applied2 - norm_old, 0.0)
    out_alpha[...] = jnp.broadcast_to(alpha, (1, cols))
    out_beta[...] = jnp.broadcast_to(norm_new / norm_old, (1, cols))

    for s in range(slab):
        @pl.when(jnp.logical_not(from_self(s)))
        def _():
            remote(fin.at[0], image.at[s], fs.at[0], fr.at[s], dev(s, xor(pos[s], sp), slab * pos[s] + s, core)).wait_recv()

        for p in range(2):
            out_app[p, s] = image[s, p]

    for recv, ssem, rsem, size, there in ((ps1, p1s, p1r, n, at_y(up_y)), (ps2, p2s, p2r, m, at_z(up_z))):
        others = recv.at[pl.ds(0, size - 1)]
        remote(others, others, ssem, rsem, there).wait_send()
    for h in halo1 + halo2:
        h.wait_send()
    for j in range(slab):
        @pl.when(moved)
        def _():
            res_over(j).wait_send()

        @pl.when(jnp.logical_not(from_self(j)))
        def _():
            local_over(j).wait_send()

        for step in steps:
            @pl.when(hops(step))
            def _():
                maps_over(j, step).wait_send()

        def sent_maps(t):
            zt, _, cp = pass_on(sbuf.at[0, j], j, t)

            @pl.when(zt != z)
            def _():
                cp.wait_send()

        loop(0, line, sent_maps)
        zt, cp = forward_res(j)

        @pl.when(zt != z)
        def _():
            cp.wait_send()

    for i in range(nz // NX):
        for k in range(1, NX):
            hand(2 * (first + i) + core, i, k).wait_send()
        zz, cp = home(i)

        @pl.when(jnp.logical_not(jnp.logical_and(sp == lp, zz == z)))
        def _():
            cp.wait_send()

    def sent_sums(zz):
        to_other(zz).wait_send()
        to_sib(zz).wait_send()
        t, cp = to_adder(zz)

        @pl.when(t != lp)
        def _():
            cp.wait_send()

    loop(0, nz, sent_sums)


def matrix(length, rows):
    k = np.arange(length)
    angle = 2.0 * np.pi / length * (np.outer(k, k) % length)
    c, s = np.cos(angle), np.sin(angle)
    g = np.block([[c, s], [-s, c]])
    blocks = length // rows
    order = np.arange(2 * length).reshape(2, blocks, rows).transpose(1, 0, 2).reshape(-1)
    g = g[order][:, order]
    g = g.astype(np.float32)
    h = g.astype(ml_dtypes.bfloat16)
    return np.stack([h, (g - h.astype(np.float32)).astype(ml_dtypes.bfloat16)])


def body(n, m, solution, residual, sensitivity, sampling):
    _, slab, rows, cols = solution.shape
    coils = sensitivity.shape[1]
    full = n * rows
    g = jnp.asarray(matrix(full, LANES))
    vmem = pl.BlockSpec(memory_space=pltpu.VMEM)
    hbm = pl.BlockSpec(memory_space=pl.ANY)
    dma = pltpu.SemaphoreType.DMA
    chunk = (2, rows, cols)

    def f32(*shape):
        return pltpu.VMEM(shape, F32)

    def bf16(*shape):
        return pltpu.VMEM(shape, BF16)

    applied, alpha, beta = pl.pallas_call(
        functools.partial(kernel, n, m),
        out_shape=(jax.ShapeDtypeStruct(solution.shape, F32),) + 2 * (jax.ShapeDtypeStruct((1, cols), F32),),
        in_specs=[vmem, vmem, vmem, hbm, hbm],
        out_specs=(vmem, vmem, vmem),
        scratch_shapes=[
            f32(coils, slab, *chunk), f32(slab, 2 * NX, *chunk), f32(n, *chunk), f32(slab, *chunk), f32(n, *chunk),
            bf16(2 * LANES, cols), bf16(2 * LANES, cols), f32(2 * full, cols), bf16(2 * full, cols), bf16(2 * full, cols),
            pltpu.VMEM(sampling.shape, sampling.dtype), bf16(*g.shape),
            f32(n, *chunk), f32(n // 2, *chunk), f32(n // 2, *chunk), f32(n // 2 // NX, NX, *chunk), f32(2, *chunk),
            f32(slab, *chunk), f32(*solution.shape), f32(slab, *chunk), f32(n // 2 // NX, *chunk),
            f32(2, *chunk), f32(8, cols), f32(8, cols), f32(*chunk), f32(*chunk), f32(8, cols), f32(8, cols),
            f32(8, LANES), f32(n, 8, LANES), f32(8, LANES), f32(m, 8, LANES),
            dma((2,)), dma((2 * NX * slab,)), dma((2 * NX * slab,)), dma((2 * NX * slab,)), dma((n,)), dma((slab,)), dma((slab,)),
            dma((slab,)), dma((n,)), dma((n // 2 // NX * NX,)), dma((n // 2,)),
            dma((n // 2,)), dma((n // 2,)), dma((n // 2,)), dma((n // 2,)), dma((n // 2 // NX,)), dma((slab,)),
            dma((5,)), dma((5,)), dma((slab,)), dma((n // 2 // NX,)), dma, dma, dma, dma,
        ],
        compiler_params=pltpu.CompilerParams(
            collective_id=0, has_side_effects=True, vmem_limit_bytes=56 * 1024 * 1024
        ),
        name="iteration",
    )(solution, residual, sensitivity, sampling, g)
    alpha, beta = alpha[0], beta[0]
    new_residual = residual - alpha * applied
    return solution + alpha * residual, new_residual, new_residual + beta * residual


def solution(mesh):
    n, m = mesh.shape["gy"], mesh.shape["gz"]
    field = P(None, "gz", "gy", None)
    return jax.shard_map(
        functools.partial(body, n, m),
        mesh=mesh,
        in_specs=(field, field, P(None, None, "gz", "gy", None), P()),
        out_specs=(field, field, field),
        check_vma=False,
    )
```

```python
import functools

import jax
import jax.numpy as jnp
import ml_dtypes
import numpy as np
from jax import lax
from jax.experimental import pallas as pl
from jax.experimental.pallas import tpu as pltpu
from jax.sharding import PartitionSpec as P

TV_EPS = 0.1
TV_WEIGHT = 0.1
TIKHONOV = 0.1
MESH = pl.DeviceIdType.MESH
F32 = jnp.float32
BF16 = jnp.bfloat16
LANES = 128
NX = 4


def split(x):
    high = x.astype(BF16)
    return high, (x - high.astype(F32)).astype(BF16)


def dot(a, b):
    return jnp.dot(a, b, preferred_element_type=F32)


def dot3(ah, al, bh, bl):
    return dot(ah, bh) + (dot(ah, bl) + dot(al, bh))


def total(x):
    rows = jnp.sum(x, axis=0, keepdims=True)
    n = rows.shape[1] // LANES
    return functools.reduce(jnp.add, [rows[:, i * LANES : (i + 1) * LANES] for i in range(n)])


def interleave(a, b):
    parts = []
    for i in range(a.shape[1] // LANES):
        parts += [a[:, i * LANES : (i + 1) * LANES], b[:, i * LANES : (i + 1) * LANES]]
    return jnp.concatenate(parts, axis=1)


def part_of(v, i):
    return jnp.concatenate([v[:, (2 * b + i) * LANES : (2 * b + i + 1) * LANES] for b in range(v.shape[1] // LANES // 2)], axis=1)


def kernel(
    n, m, sol, res, sens, samp_in, g_in,
    out_app, out_alpha, out_beta,
    sbuf, relay, srecv, xrel, xall, vh, vl, yacc, yh, yl, samp, g,
    part, pair, tot, gath, fin, image, smooth, local, local_in,
    hz, hy_s, hy, qz_s, qz, qy_s, qy, ps1_s, ps1, ps2_s, ps2,
    csem, xls, xlr, zs, zr, xrs, xrr, xzs, xar, ms, os,
    prs, prr, gs, gr, fs, fr, hs, hr, ls, lr, p1s, p1r, p2s, p2r,
):
    y = lax.axis_index("gy")
    w = lax.axis_index("gz")
    z, core = y // 2, lax.rem(y, 2)
    x, yy = w // NX, lax.rem(w, NX)
    nz = n // 2
    slab, rows, cols = res.shape[1:]
    sib = 1 - core
    pos = (x, yy)
    odd = lax.rem(z, 2)
    lp = (1 - odd) * x + odd * yy
    sp = z // 2
    l = 2 * lp + core
    line = 2 * NX

    def dev(j, p, z_, core_):
        return (2 * z_ + core_, NX * x + p if j else NX * p + yy)

    def on_line(p, z_, core_):
        return (2 * z_ + core_, (1 - odd) * (NX * p + yy) + odd * (NX * x + p))

    def at_y(t):
        return (t, w)

    def at_z(t):
        return (y, t)

    other = (yy, x)

    def around(t):
        return lax.rem(t + 4 * NX, NX)

    def shift(j):
        return sp + other[j] + 2 * j

    def rows_at(k):
        return around(sp - x - yy - 2 * odd - k)

    def remote(src, dst, ssem, rsem, device):
        return pltpu.make_async_remote_copy(
            src_ref=src, dst_ref=dst, send_sem=ssem, recv_sem=rsem, device_id=device, device_id_type=MESH
        )

    def loop(lo, hi, f):
        def step(i, c):
            f(i)
            return c

        lax.fori_loop(lo, hi, step, 0)

    barrier = pltpu.get_barrier_semaphore()

    def hail(device):
        pl.semaphore_signal(barrier, inc=1, device_id=device, device_id_type=MESH)

    loop(1, n, lambda k: hail(at_y(lax.rem(y + k, n))))
    loop(1, m, lambda k: hail(at_z(lax.rem(w + k, m))))
    for j in range(slab):
        loop(1, NX, lambda k: hail(dev(j, lax.rem(pos[j] + k, NX), z, sib)))
        hail(dev(j, around(pos[j] - shift(j)), slab * pos[j] + j, core))

    def from_self(j):
        return jnp.logical_and(around(shift(j)) == 0, slab * pos[j] + j == z)

    loads = [
        pltpu.make_async_copy(a, b, csem.at[i]) for i, (a, b) in enumerate([(g_in, g), (samp_in, samp)])
    ]
    for c in loads:
        c.start()

    def widen(c):
        for j in range(slab):
            sbuf[c, j, 0] = sens[0, c, j].astype(F32)
            sbuf[c, j, 1] = sens[1, c, j].astype(F32)

    loop(0, line, widen)

    up_y, down_y = lax.rem(y + 1, n), lax.rem(y + n - 1, n)
    up_z, down_z = lax.rem(w + 1, m), lax.rem(w + m - 1, m)
    for f, field in enumerate((sol, res)):
        for p in range(2):
            for s in range(slab):
                i = f * 2 * slab + p * slab + s
                hy_s[i : i + 1, :] = field[p, s, 0:1, :]

    pl.semaphore_wait(barrier, n + m - 2 + slab * NX)

    def moved(j):
        return around(shift(j)) != 0

    def res_over(j):
        return remote(res.at[:, j], xrel.at[j], xrs.at[j], xrr.at[j], dev(j, around(pos[j] - shift(j)), z, core))

    for j in range(slab):
        @pl.when(moved(j))
        def _():
            res_over(j).start()

        @pl.when(jnp.logical_not(moved(j)))
        def _():
            xrel[j] = res[:, j]

    steps = [(k, c) for k in range(NX) for c in range(2)]

    def hops(j, step):
        return jnp.logical_or(around(shift(j) + step[0]) != 0, step[1] > 0)

    def maps_over(j, step):
        p = around(pos[j] - shift(j) - step[0])
        c = sib if step[1] else core
        t = 2 * p + c
        me = 2 * pos[j] + core
        return remote(sbuf.at[t, j], relay.at[j, me], xls.at[line * j + t], xlr.at[line * j + me], dev(j, p, z, c))

    for step in steps:
        for j in range(slab):
            @pl.when(hops(j, step))
            def _():
                maps_over(j, step).start()

    halo1 = [
        remote(sol.at[:, 0], hz.at[0], hs.at[0], hr.at[0], at_z(down_z)),
        remote(res.at[:, 0], hz.at[1], hs.at[1], hr.at[1], at_z(down_z)),
        remote(hy_s, hy, hs.at[2], hr.at[2], at_y(down_y)),
    ]
    for h in halo1:
        h.start()

    def pass_on(src, j, t):
        zt = slab * (t // 2) + j
        slot = 2 * z + lax.rem(t, 2)
        cp = remote(src, srecv.at[slot], zs.at[line * j + t], zr.at[slot], dev(0, x, zt, core))
        return zt, slot, cp

    def forward_maps(src, j, t):
        zt, slot, cp = pass_on(src, j, t)

        @pl.when(zt != z)
        def _():
            cp.start()

        @pl.when(zt == z)
        def _():
            srecv[slot] = src[...]

    def forward_res(j):
        zt = slab * around(pos[j] + shift(j)) + j
        return zt, remote(xrel.at[j], xall.at[y], xzs.at[j], xar.at[y], dev(0, x, zt, core))

    for j in range(slab):
        @pl.when(moved(j))
        def _():
            res_over(j).wait_recv()

        zt, cp = forward_res(j)

        @pl.when(zt != z)
        def _():
            cp.start()

        @pl.when(zt == z)
        def _():
            xall[y] = xrel[j]

    def relay_maps(step):
        for j in range(slab):
            p = around(pos[j] + shift(j) + step[0])
            c = sib if step[1] else core
            t = 2 * p + c

            @pl.when(hops(j, step))
            def _():
                remote(sbuf.at[t, j], relay.at[j, t], xls.at[line * j + t], xlr.at[line * j + t], dev(j, p, z, c)).wait_recv()
                forward_maps(relay.at[j, t], j, t)

            @pl.when(jnp.logical_not(hops(j, step)))
            def _():
                forward_maps(sbuf.at[t, j], j, t)

    for step in steps:
        relay_maps(step)

    first = 2 * rows_at(0)

    def hand(slot, i, k):
        p = around(lp + k)
        return remote(xall.at[slot], xall.at[slot], ms.at[i * NX + k], xar.at[slot], on_line(p, z, core))

    def to_other(zz):
        slot = 2 * zz + core
        return remote(xall.at[slot], xall.at[slot], os.at[zz], xar.at[slot], on_line(lp, z, sib))

    for i in range(nz // NX):
        zz = first + i
        slot = 2 * zz + core

        @pl.when(zz != z)
        def _():
            remote(xrel.at[0], xall.at[slot], xzs.at[0], xar.at[slot], dev(0, x, zz, core)).wait_recv()

        for k in range(1, NX):
            hand(slot, i, k).start()
        to_other(zz).start()

    for h in halo1:
        h.wait_recv()
    row = lax.broadcasted_iota(jnp.int32, (rows, cols), 0)
    col = lax.broadcasted_iota(jnp.int32, (rows, cols), 1)
    keep_y = jnp.logical_or(row < rows - 1, y < n - 1)
    keep_z = jnp.full((rows, cols), w, jnp.int32) < m - 1

    def ahead(f, field, p, s):
        v = field[p, s]
        dx = jnp.where(col == cols - 1, 0.0, pltpu.roll(v, cols - 1, 1) - v)
        i = f * 2 * slab + p * slab + s
        nxt = jnp.where(row == rows - 1, jnp.broadcast_to(hy[i : i + 1, :], (rows, cols)), pltpu.roll(v, rows - 1, 0))
        dy = jnp.where(keep_y, nxt - v, 0.0)
        if s + 1 < slab:
            dz = field[p, s + 1] - v
        else:
            dz = jnp.where(keep_z, hz[f, p] - v, 0.0)
        return dx, dy, dz

    qy_s[...] = jnp.zeros_like(qy_s)
    for s in range(slab):
        sq = jnp.zeros((rows, cols), F32)
        for p in range(2):
            for d in ahead(0, sol, p, s):
                sq = sq + d * d
        weight = 1.0 / jnp.sqrt(sq + TV_EPS * TV_EPS)
        for p in range(2):
            dx, dy, dz = (weight * d for d in ahead(1, res, p, s))
            before_x = jnp.where(col == 0, 0.0, pltpu.roll(dx, 1, 1))
            before_y = jnp.where(row == 0, 0.0, pltpu.roll(dy, 1, 0))
            here = (before_x - dx) + (before_y - dy) - dz
            if s > 0:
                here = here + qz_s[p]
            smooth[p, s] = here
            qz_s[p] = dz
            i = p * slab + s
            qy_s[i : i + 1, :] = dy[rows - 1 : rows, :]
    halo2 = [
        remote(qz_s, qz, hs.at[3], hr.at[3], at_z(up_z)),
        remote(qy_s, qy, hs.at[4], hr.at[4], at_y(up_y)),
    ]
    for h in halo2:
        h.start()

    for k in range(1, NX):
        for i in range(nz // NX):
            zz = 2 * rows_at(k) + i
            slot = 2 * zz + core
            remote(xall.at[slot], xall.at[slot], ms.at[0], xar.at[slot], on_line(around(lp + k), z, core)).wait_recv()
            to_other(zz).start()

    per = 4
    tile = per * rows
    groups = n // per

    def ready(s):
        zz = s // 2

        @pl.when(zz != z)
        def _():
            remote(relay.at[0, 0], srecv.at[s], zs.at[0], zr.at[s], dev(0, x, zz, core)).wait_recv()

        @pl.when(lax.rem(s, 2) == sib)
        def _():
            remote(xall.at[s], xall.at[s], os.at[0], xar.at[s], on_line(lp, z, sib)).wait_recv()

    at_zero = jnp.full((rows, cols), w, jnp.int32) > 0
    at_top = jnp.logical_and(row == 0, y > 0)

    def local_over(j):
        there = dev(j, around(pos[j] - shift(j)), slab * pos[j] + j, core)
        return remote(local.at[j], local_in.at[odd], ls.at[j], lr.at[odd], there)

    def send_local():
        for h in halo2:
            h.wait_recv()
        for p in range(2):
            for s in range(slab):
                i = p * slab + s
                v = smooth[p, s] + jnp.where(at_top, jnp.broadcast_to(qy[i : i + 1, :], (rows, cols)), 0.0)
                if s == 0:
                    v = v + jnp.where(at_zero, qz[p], 0.0)
                local[s, p] = TIKHONOV * res[p, s] - TV_WEIGHT * v
        for j in range(slab):
            @pl.when(jnp.logical_not(from_self(j)))
            def _():
                local_over(j).start()

            @pl.when(from_self(j))
            def _():
                local_in[odd] = local[j]

    full = n * rows
    scale = 1.0 / (full * cols)
    yacc[...] = jnp.zeros_like(yacc)
    loads[0].wait()
    loads[1].wait()

    def forward(i):
        q = rows_at(i)
        last = i == groups - 1

        @pl.when(last)
        def _():
            send_local()

        for t in range(per):
            ready(q * per + t)
        block = []
        for t in range(per):
            sr, si = srecv[q * per + t, 0], srecv[q * per + t, 1]
            xr, xi = xall[q * per + t, 0], xall[q * per + t, 1]
            block.append(interleave(sr * xr - si * xi, -(sr * xi + si * xr)))
        ah, al = split(jnp.concatenate(block, axis=0))
        v = dot3(ah, al, g[0], g[1])
        vh[:tile], vl[:tile] = split(part_of(v, 0))
        vh[tile:], vl[tile:] = split(-part_of(v, 1))

        def rows_tile(t):
            at = pl.ds(pl.multiple_of(2 * t * tile, 2 * tile), 2 * tile)
            k = pl.ds(pl.multiple_of(2 * q * tile, 2 * tile), 2 * tile)
            v = yacc[at] + dot3(g[0, at, k], g[1, at, k], vh[...], vl[...])

            @pl.when(jnp.logical_not(last))
            def _():
                yacc[at] = v

            @pl.when(last)
            def _():
                taken = samp[pl.ds(pl.multiple_of(t * tile, tile), tile)].astype(F32) * scale
                yh[at], yl[at] = split(v * jnp.concatenate([taken, -taken], axis=0))

        loop(0, groups, rows_tile)

    loop(0, groups, forward)

    def to_sib(zz):
        return remote(part.at[2 * zz + sib], pair.at[zz], prs.at[zz], prr.at[zz], on_line(lp, z, sib))

    def to_adder(zz):
        t = around(lp + rows_at(0) - zz // 2)
        i = lax.rem(zz, 2)
        return t, remote(tot.at[zz], gath.at[i, lp], gs.at[zz], gr.at[NX * i + lp], on_line(t, z, core))

    def add_pair(zz):
        to_sib(zz).wait_recv()
        tot[zz] = part[2 * zz + core] + pair[zz]
        t, cp = to_adder(zz)

        @pl.when(t != lp)
        def _():
            cp.start()

    def home(i):
        zz = first + i
        return zz, remote(fin.at[i], image.at[odd], fs.at[i], fr.at[odd], on_line(sp, zz, core))

    def add_line(i):
        zz, cp = home(i)
        v = tot[zz]
        for k in range(1, NX):
            t = around(lp + k)
            remote(tot.at[zz], gath.at[i, t], gs.at[zz], gr.at[NX * i + t], on_line(t, z, core)).wait_recv()
            v = v + gath[i, t]

        @pl.when(jnp.logical_not(jnp.logical_and(sp == lp, zz == z)))
        def _():
            remote(local.at[0], local_in.at[i], ls.at[0], lr.at[i], on_line(sp, zz, core)).wait_recv()

        v = v + local_in[i]
        for p in range(2):
            a, r = v[p], xall[2 * zz + core, p]
            ps1_s[0:1, :] += total(r * r)
            ps1_s[1:2, :] += total(r * a)
            ps1_s[2:3, :] += total(a * a)
        here = jnp.logical_and(sp == lp, zz == z)

        @pl.when(here)
        def _():
            image[odd] = v

        @pl.when(jnp.logical_not(here))
        def _():
            fin[i] = v
            cp.start()

    def block_at(i):
        return rows_at(2 + i - (i // 2) * (2 * i - 1))

    def inverse(i):
        q = block_at(i)
        at = pl.ds(pl.multiple_of(2 * q * tile, 2 * tile), 2 * tile)
        v = dot3(g[0, at], g[1, at], yh[...], yl[...])
        ah, al = split(interleave(v[:tile], -v[tile:]))
        v = dot3(ah, al, g[0], g[1])
        re, im = part_of(v, 0), part_of(v, 1)
        for t in range(per):
            s = q * per + t
            vr, vi = re[t * rows : (t + 1) * rows], im[t * rows : (t + 1) * rows]
            sr, si = srecv[s, 0], srecv[s, 1]
            part[s, 0] = sr * vr + si * vi
            part[s, 1] = sr * vi - si * vr
        for t in range(per // 2):
            to_sib(q * per // 2 + t).start()

        @pl.when(i > 0)
        def _():
            for t in range(per // 2):
                add_pair(block_at(i - 1) * per // 2 + t)

    ps1_s[...] = jnp.zeros_like(ps1_s)
    loop(0, groups, inverse)
    for t in range(per // 2):
        add_pair(first + t)
    for i in range(nz // NX):
        add_line(i)

    def exchange(send, recv, ssem, rsem, me, size, where):
        recv[me] = send[...]

        def go(k):
            t = lax.rem(me + k, size)
            remote(send, recv.at[me], ssem, rsem, where(t)).start()

        loop(1, size, go)
        others = recv.at[pl.ds(0, size - 1)]
        remote(others, others, ssem, rsem, where(lax.rem(me + 1, size))).wait_recv()
        return functools.reduce(jnp.add, [recv[i] for i in range(size)])

    ps2_s[...] = exchange(ps1_s, ps1, p1s, p1r, y, n, at_y)
    sums = jnp.sum(exchange(ps2_s, ps2, p2s, p2r, w, m, at_z), axis=1, keepdims=True)
    norm_old, curvature, applied2 = sums[0:1], sums[1:2], sums[2:3]
    alpha = norm_old / curvature
    norm_new = jnp.maximum(alpha * alpha * applied2 - norm_old, 0.0)
    out_alpha[...] = jnp.broadcast_to(alpha, (1, cols))
    out_beta[...] = jnp.broadcast_to(norm_new / norm_old, (1, cols))

    for s in range(slab):
        @pl.when(jnp.logical_not(from_self(s)))
        def _():
            remote(fin.at[0], image.at[s], fs.at[0], fr.at[s], dev(s, around(pos[s] - shift(s)), slab * pos[s] + s, core)).wait_recv()

        for p in range(2):
            out_app[p, s] = image[s, p]

    for recv, ssem, rsem, size, there in ((ps1, p1s, p1r, n, at_y(up_y)), (ps2, p2s, p2r, m, at_z(up_z))):
        others = recv.at[pl.ds(0, size - 1)]
        remote(others, others, ssem, rsem, there).wait_send()
    for h in halo1 + halo2:
        h.wait_send()
    for j in range(slab):
        @pl.when(moved(j))
        def _():
            res_over(j).wait_send()

        @pl.when(jnp.logical_not(from_self(j)))
        def _():
            local_over(j).wait_send()

        for step in steps:
            @pl.when(hops(j, step))
            def _():
                maps_over(j, step).wait_send()

        def sent_maps(t):
            zt, _, cp = pass_on(sbuf.at[0, j], j, t)

            @pl.when(zt != z)
            def _():
                cp.wait_send()

        loop(0, line, sent_maps)
        zt, cp = forward_res(j)

        @pl.when(zt != z)
        def _():
            cp.wait_send()

    for i in range(nz // NX):
        for k in range(1, NX):
            hand(2 * (first + i) + core, i, k).wait_send()
        zz, cp = home(i)

        @pl.when(jnp.logical_not(jnp.logical_and(sp == lp, zz == z)))
        def _():
            cp.wait_send()

    def sent_sums(zz):
        to_other(zz).wait_send()
        to_sib(zz).wait_send()
        t, cp = to_adder(zz)

        @pl.when(t != lp)
        def _():
            cp.wait_send()

    loop(0, nz, sent_sums)


def matrix(length, rows):
    k = np.arange(length)
    angle = 2.0 * np.pi / length * (np.outer(k, k) % length)
    c, s = np.cos(angle), np.sin(angle)
    g = np.block([[c, s], [-s, c]])
    blocks = length // rows
    order = np.arange(2 * length).reshape(2, blocks, rows).transpose(1, 0, 2).reshape(-1)
    g = g[order][:, order]
    g = g.astype(np.float32)
    h = g.astype(ml_dtypes.bfloat16)
    return np.stack([h, (g - h.astype(np.float32)).astype(ml_dtypes.bfloat16)])


def body(n, m, solution, residual, sensitivity, sampling):
    _, slab, rows, cols = solution.shape
    coils = sensitivity.shape[1]
    full = n * rows
    g = jnp.asarray(matrix(full, LANES))
    vmem = pl.BlockSpec(memory_space=pltpu.VMEM)
    hbm = pl.BlockSpec(memory_space=pl.ANY)
    dma = pltpu.SemaphoreType.DMA
    chunk = (2, rows, cols)

    def f32(*shape):
        return pltpu.VMEM(shape, F32)

    def bf16(*shape):
        return pltpu.VMEM(shape, BF16)

    applied, alpha, beta = pl.pallas_call(
        functools.partial(kernel, n, m),
        out_shape=(jax.ShapeDtypeStruct(solution.shape, F32),) + 2 * (jax.ShapeDtypeStruct((1, cols), F32),),
        in_specs=[vmem, vmem, vmem, hbm, hbm],
        out_specs=(vmem, vmem, vmem),
        scratch_shapes=[
            f32(coils, slab, *chunk), f32(slab, 2 * NX, *chunk), f32(n, *chunk), f32(slab, *chunk), f32(n, *chunk),
            bf16(2 * LANES, cols), bf16(2 * LANES, cols), f32(2 * full, cols), bf16(2 * full, cols), bf16(2 * full, cols),
            pltpu.VMEM(sampling.shape, sampling.dtype), bf16(*g.shape),
            f32(n, *chunk), f32(n // 2, *chunk), f32(n // 2, *chunk), f32(n // 2 // NX, NX, *chunk), f32(2, *chunk),
            f32(slab, *chunk), f32(*solution.shape), f32(slab, *chunk), f32(n // 2 // NX, *chunk),
            f32(2, *chunk), f32(8, cols), f32(8, cols), f32(*chunk), f32(*chunk), f32(8, cols), f32(8, cols),
            f32(8, LANES), f32(n, 8, LANES), f32(8, LANES), f32(m, 8, LANES),
            dma((2,)), dma((2 * NX * slab,)), dma((2 * NX * slab,)), dma((2 * NX * slab,)), dma((n,)), dma((slab,)), dma((slab,)),
            dma((slab,)), dma((n,)), dma((n // 2 // NX * NX,)), dma((n // 2,)),
            dma((n // 2,)), dma((n // 2,)), dma((n // 2,)), dma((n // 2,)), dma((n // 2 // NX,)), dma((slab,)),
            dma((5,)), dma((5,)), dma((slab,)), dma((n // 2 // NX,)), dma, dma, dma, dma,
        ],
        compiler_params=pltpu.CompilerParams(
            collective_id=0, has_side_effects=True, vmem_limit_bytes=56 * 1024 * 1024
        ),
        name="iteration",
    )(solution, residual, sensitivity, sampling, g)
    alpha, beta = alpha[0], beta[0]
    new_residual = residual - alpha * applied
    return solution + alpha * residual, new_residual, new_residual + beta * residual


def solution(mesh):
    n, m = mesh.shape["gy"], mesh.shape["gz"]
    field = P(None, "gz", "gy", None)
    return jax.shard_map(
        functools.partial(body, n, m),
        mesh=mesh,
        in_specs=(field, field, P(None, None, "gz", "gy", None), P()),
        out_specs=(field, field, field),
        check_vma=False,
    )
```

```python
import functools

import jax
import jax.numpy as jnp
import ml_dtypes
import numpy as np
from jax import lax
from jax.experimental import pallas as pl
from jax.experimental.pallas import tpu as pltpu
from jax.sharding import PartitionSpec as P

TV_EPS = 0.1
TV_WEIGHT = 0.1
TIKHONOV = 0.1
MESH = pl.DeviceIdType.MESH
F32 = jnp.float32
BF16 = jnp.bfloat16
LANES = 128
NX = 4


def split(x):
    high = x.astype(BF16)
    return high, (x - high.astype(F32)).astype(BF16)


def dot(a, b):
    return jnp.dot(a, b, preferred_element_type=F32)


def dot3(ah, al, bh, bl):
    return dot(ah, bh) + (dot(ah, bl) + dot(al, bh))


def total(x):
    rows = jnp.sum(x, axis=0, keepdims=True)
    n = rows.shape[1] // LANES
    return functools.reduce(jnp.add, [rows[:, i * LANES : (i + 1) * LANES] for i in range(n)])


def interleave(a, b):
    parts = []
    for i in range(a.shape[1] // LANES):
        parts += [a[:, i * LANES : (i + 1) * LANES], b[:, i * LANES : (i + 1) * LANES]]
    return jnp.concatenate(parts, axis=1)


def part_of(v, i):
    return jnp.concatenate([v[:, (2 * b + i) * LANES : (2 * b + i + 1) * LANES] for b in range(v.shape[1] // LANES // 2)], axis=1)


def kernel(
    n, m, sol_in, res_in, sens_in, samp_in, g_in,
    out_app, out_alpha, out_beta,
    sol, res, sens, sbuf, relay, srecv, xrel, xall, vh, vl, yacc, yh, yl, samp, g,
    part, pair, tot, gath, fin, image, smooth, local, local_in,
    hz, hy_s, hy, qz_s, qz, qy_s, qy, ps1_s, ps1, ps2_s, ps2,
    csem, xls, xlr, zs, zr, xrs, xrr, xzs, xar, ms, os,
    prs, prr, gs, gr, fs, fr, hs, hr, ls, lr, p1s, p1r, p2s, p2r,
):
    y = lax.axis_index("gy")
    w = lax.axis_index("gz")
    z, core = y // 2, lax.rem(y, 2)
    x, yy = w // NX, lax.rem(w, NX)
    nz = n // 2
    slab, rows, cols = res.shape[1:]
    sib = 1 - core
    pos = (x, yy)
    odd = lax.rem(z, 2)
    lp = (1 - odd) * x + odd * yy
    sp = z // 2
    l = 2 * lp + core
    line = 2 * NX

    def dev(j, p, z_, core_):
        return (2 * z_ + core_, NX * x + p if j else NX * p + yy)

    def on_line(p, z_, core_):
        return (2 * z_ + core_, (1 - odd) * (NX * p + yy) + odd * (NX * x + p))

    def at_y(t):
        return (t, w)

    def at_z(t):
        return (y, t)

    other = (yy, x)

    def around(t):
        return lax.rem(t + 4 * NX, NX)

    def shift(j):
        return sp + other[j] + 2 * j

    def rows_at(k):
        return around(sp - x - yy - 2 * odd - k)

    def remote(src, dst, ssem, rsem, device):
        return pltpu.make_async_remote_copy(
            src_ref=src, dst_ref=dst, send_sem=ssem, recv_sem=rsem, device_id=device, device_id_type=MESH
        )

    def loop(lo, hi, f):
        def step(i, c):
            f(i)
            return c

        lax.fori_loop(lo, hi, step, 0)

    loads = [
        pltpu.make_async_copy(a, b, csem.at[i])
        for i, (a, b) in enumerate([(sens_in, sens), (res_in, res), (sol_in, sol), (g_in, g), (samp_in, samp)])
    ]
    for c in loads:
        c.start()

    barrier = pltpu.get_barrier_semaphore()

    def hail(device):
        pl.semaphore_signal(barrier, inc=1, device_id=device, device_id_type=MESH)

    loop(1, n, lambda k: hail(at_y(lax.rem(y + k, n))))
    loop(1, m, lambda k: hail(at_z(lax.rem(w + k, m))))
    for j in range(slab):
        loop(1, NX, lambda k: hail(dev(j, lax.rem(pos[j] + k, NX), z, sib)))
        hail(dev(j, around(pos[j] - shift(j)), slab * pos[j] + j, core))

    def from_self(j):
        return jnp.logical_and(around(shift(j)) == 0, slab * pos[j] + j == z)

    def widen(c):
        for j in range(slab):
            sbuf[c, j, 0] = sens[0, c, j].astype(F32)
            sbuf[c, j, 1] = sens[1, c, j].astype(F32)

    loads[0].wait()
    loop(0, line, widen)
    loads[1].wait()
    loads[2].wait()

    up_y, down_y = lax.rem(y + 1, n), lax.rem(y + n - 1, n)
    up_z, down_z = lax.rem(w + 1, m), lax.rem(w + m - 1, m)
    for f, field in enumerate((sol, res)):
        for p in range(2):
            for s in range(slab):
                i = f * 2 * slab + p * slab + s
                hy_s[i : i + 1, :] = field[p, s, 0:1, :]

    pl.semaphore_wait(barrier, n + m - 2 + slab * NX)

    def pass_on(src, j, t):
        zt = slab * (t // 2) + j
        slot = 2 * z + lax.rem(t, 2)
        cp = remote(src, srecv.at[slot], zs.at[line * j + t], zr.at[slot], dev(0, x, zt, core))
        return zt, slot, cp

    def forward_maps(src, j, t):
        zt, slot, cp = pass_on(src, j, t)

        @pl.when(zt != z)
        def _():
            cp.start()

        @pl.when(zt == z)
        def _():
            srecv[slot] = src[...]

    def maps_over(j, p, c):
        t = 2 * p + c
        me = 2 * pos[j] + core
        return remote(sbuf.at[t, j], relay.at[j, me], xls.at[line * j + t], xlr.at[line * j + me], dev(j, p, z, c))

    for j in range(slab):
        t = 2 * pos[j] + core
        forward_maps(sbuf.at[t, j], j, t)
        maps_over(j, pos[j], sib).start()

    def moved(j):
        return around(shift(j)) != 0

    def res_over(j):
        return remote(res.at[:, j], xrel.at[j], xrs.at[j], xrr.at[j], dev(j, around(pos[j] - shift(j)), z, core))

    for j in range(slab):
        @pl.when(moved(j))
        def _():
            res_over(j).start()

        @pl.when(jnp.logical_not(moved(j)))
        def _():
            xrel[j] = res[:, j]

    steps = [(k, c) for k in range(NX) for c in (core, sib)]

    def hops(j, k):
        return around(shift(j) + k) != 0

    for k, c in steps:
        for j in range(slab):
            @pl.when(hops(j, k))
            def _():
                maps_over(j, around(pos[j] - shift(j) - k), c).start()

    halo1 = [
        remote(sol.at[:, 0], hz.at[0], hs.at[0], hr.at[0], at_z(down_z)),
        remote(res.at[:, 0], hz.at[1], hs.at[1], hr.at[1], at_z(down_z)),
        remote(hy_s, hy, hs.at[2], hr.at[2], at_y(down_y)),
    ]
    for h in halo1:
        h.start()

    def relay_maps(j, p, c):
        t = 2 * p + c
        remote(sbuf.at[t, j], relay.at[j, t], xls.at[line * j + t], xlr.at[line * j + t], dev(j, p, z, c)).wait_recv()
        forward_maps(relay.at[j, t], j, t)

    for j in range(slab):
        relay_maps(j, pos[j], sib)

    def forward_res(j):
        zt = slab * around(pos[j] + shift(j)) + j
        return zt, remote(xrel.at[j], xall.at[y], xzs.at[j], xar.at[y], dev(0, x, zt, core))

    for j in range(slab):
        @pl.when(moved(j))
        def _():
            res_over(j).wait_recv()

        zt, cp = forward_res(j)

        @pl.when(zt != z)
        def _():
            cp.start()

        @pl.when(zt == z)
        def _():
            xall[y] = xrel[j]

    for k, c in steps:
        for j in range(slab):
            @pl.when(hops(j, k))
            def _():
                relay_maps(j, around(pos[j] + shift(j) + k), c)

    first = 2 * rows_at(0)

    def hand(slot, i, k):
        p = around(lp + k)
        return remote(xall.at[slot], xall.at[slot], ms.at[i * NX + k], xar.at[slot], on_line(p, z, core))

    def to_other(zz):
        slot = 2 * zz + core
        return remote(xall.at[slot], xall.at[slot], os.at[zz], xar.at[slot], on_line(lp, z, sib))

    for i in range(nz // NX):
        zz = first + i
        slot = 2 * zz + core

        @pl.when(zz != z)
        def _():
            remote(xrel.at[0], xall.at[slot], xzs.at[0], xar.at[slot], dev(0, x, zz, core)).wait_recv()

        for k in range(1, NX):
            hand(slot, i, k).start()
        to_other(zz).start()

    for h in halo1:
        h.wait_recv()
    row = lax.broadcasted_iota(jnp.int32, (rows, cols), 0)
    col = lax.broadcasted_iota(jnp.int32, (rows, cols), 1)
    keep_y = jnp.logical_or(row < rows - 1, y < n - 1)
    keep_z = jnp.full((rows, cols), w, jnp.int32) < m - 1

    def ahead(f, field, p, s):
        v = field[p, s]
        dx = jnp.where(col == cols - 1, 0.0, pltpu.roll(v, cols - 1, 1) - v)
        i = f * 2 * slab + p * slab + s
        nxt = jnp.where(row == rows - 1, jnp.broadcast_to(hy[i : i + 1, :], (rows, cols)), pltpu.roll(v, rows - 1, 0))
        dy = jnp.where(keep_y, nxt - v, 0.0)
        if s + 1 < slab:
            dz = field[p, s + 1] - v
        else:
            dz = jnp.where(keep_z, hz[f, p] - v, 0.0)
        return dx, dy, dz

    qy_s[...] = jnp.zeros_like(qy_s)
    for s in range(slab):
        sq = jnp.zeros((rows, cols), F32)
        for p in range(2):
            for d in ahead(0, sol, p, s):
                sq = sq + d * d
        weight = 1.0 / jnp.sqrt(sq + TV_EPS * TV_EPS)
        for p in range(2):
            dx, dy, dz = (weight * d for d in ahead(1, res, p, s))
            before_x = jnp.where(col == 0, 0.0, pltpu.roll(dx, 1, 1))
            before_y = jnp.where(row == 0, 0.0, pltpu.roll(dy, 1, 0))
            here = (before_x - dx) + (before_y - dy) - dz
            if s > 0:
                here = here + qz_s[p]
            smooth[p, s] = here
            qz_s[p] = dz
            i = p * slab + s
            qy_s[i : i + 1, :] = dy[rows - 1 : rows, :]
    halo2 = [
        remote(qz_s, qz, hs.at[3], hr.at[3], at_z(up_z)),
        remote(qy_s, qy, hs.at[4], hr.at[4], at_y(up_y)),
    ]
    for h in halo2:
        h.start()

    for k in range(1, NX):
        for i in range(nz // NX):
            zz = 2 * rows_at(k) + i
            slot = 2 * zz + core
            remote(xall.at[slot], xall.at[slot], ms.at[0], xar.at[slot], on_line(around(lp + k), z, core)).wait_recv()
            to_other(zz).start()

    per = 4
    tile = per * rows
    groups = n // per

    def ready(s):
        zz = s // 2

        @pl.when(zz != z)
        def _():
            remote(relay.at[0, 0], srecv.at[s], zs.at[0], zr.at[s], dev(0, x, zz, core)).wait_recv()

        @pl.when(lax.rem(s, 2) == sib)
        def _():
            remote(xall.at[s], xall.at[s], os.at[0], xar.at[s], on_line(lp, z, sib)).wait_recv()

    at_zero = jnp.full((rows, cols), w, jnp.int32) > 0
    at_top = jnp.logical_and(row == 0, y > 0)

    def local_over(j):
        there = dev(j, around(pos[j] - shift(j)), slab * pos[j] + j, core)
        return remote(local.at[j], local_in.at[odd], ls.at[j], lr.at[odd], there)

    def send_local():
        for h in halo2:
            h.wait_recv()
        for p in range(2):
            for s in range(slab):
                i = p * slab + s
                v = smooth[p, s] + jnp.where(at_top, jnp.broadcast_to(qy[i : i + 1, :], (rows, cols)), 0.0)
                if s == 0:
                    v = v + jnp.where(at_zero, qz[p], 0.0)
                local[s, p] = TIKHONOV * res[p, s] - TV_WEIGHT * v
        for j in range(slab):
            @pl.when(jnp.logical_not(from_self(j)))
            def _():
                local_over(j).start()

            @pl.when(from_self(j))
            def _():
                local_in[odd] = local[j]

    full = n * rows
    scale = 1.0 / (full * cols)
    yacc[...] = jnp.zeros_like(yacc)
    loads[3].wait()
    loads[4].wait()

    def forward(i):
        q = rows_at(i)
        last = i == groups - 1

        @pl.when(last)
        def _():
            send_local()

        for t in range(per):
            ready(q * per + t)
        block = []
        for t in range(per):
            sr, si = srecv[q * per + t, 0], srecv[q * per + t, 1]
            xr, xi = xall[q * per + t, 0], xall[q * per + t, 1]
            block.append(interleave(sr * xr - si * xi, -(sr * xi + si * xr)))
        ah, al = split(jnp.concatenate(block, axis=0))
        v = dot3(ah, al, g[0], g[1])
        vh[:tile], vl[:tile] = split(part_of(v, 0))
        vh[tile:], vl[tile:] = split(-part_of(v, 1))

        def rows_tile(t):
            at = pl.ds(pl.multiple_of(2 * t * tile, 2 * tile), 2 * tile)
            k = pl.ds(pl.multiple_of(2 * q * tile, 2 * tile), 2 * tile)
            v = yacc[at] + dot3(g[0, at, k], g[1, at, k], vh[...], vl[...])

            @pl.when(jnp.logical_not(last))
            def _():
                yacc[at] = v

            @pl.when(last)
            def _():
                taken = samp[pl.ds(pl.multiple_of(t * tile, tile), tile)].astype(F32) * scale
                yh[at], yl[at] = split(v * jnp.concatenate([taken, -taken], axis=0))

        loop(0, groups, rows_tile)

    loop(0, groups, forward)

    def to_sib(zz):
        return remote(part.at[2 * zz + sib], pair.at[zz], prs.at[zz], prr.at[zz], on_line(lp, z, sib))

    def to_adder(zz):
        t = around(lp + rows_at(0) - zz // 2)
        i = lax.rem(zz, 2)
        return t, remote(tot.at[zz], gath.at[i, lp], gs.at[zz], gr.at[NX * i + lp], on_line(t, z, core))

    def add_pair(zz):
        to_sib(zz).wait_recv()
        tot[zz] = part[2 * zz + core] + pair[zz]
        t, cp = to_adder(zz)

        @pl.when(t != lp)
        def _():
            cp.start()

    def home(i):
        zz = first + i
        return zz, remote(fin.at[i], image.at[odd], fs.at[i], fr.at[odd], on_line(sp, zz, core))

    def add_line(i):
        zz, cp = home(i)
        v = tot[zz]
        for k in range(1, NX):
            t = around(lp + k)
            remote(tot.at[zz], gath.at[i, t], gs.at[zz], gr.at[NX * i + t], on_line(t, z, core)).wait_recv()
            v = v + gath[i, t]

        @pl.when(jnp.logical_not(jnp.logical_and(sp == lp, zz == z)))
        def _():
            remote(local.at[0], local_in.at[i], ls.at[0], lr.at[i], on_line(sp, zz, core)).wait_recv()

        v = v + local_in[i]
        for p in range(2):
            a, r = v[p], xall[2 * zz + core, p]
            ps1_s[0:1, :] += total(r * r)
            ps1_s[1:2, :] += total(r * a)
            ps1_s[2:3, :] += total(a * a)
        here = jnp.logical_and(sp == lp, zz == z)

        @pl.when(here)
        def _():
            image[odd] = v

        @pl.when(jnp.logical_not(here))
        def _():
            fin[i] = v
            cp.start()

    def block_at(i):
        return rows_at(2 + i - (i // 2) * (2 * i - 1))

    def inverse(i):
        q = block_at(i)
        at = pl.ds(pl.multiple_of(2 * q * tile, 2 * tile), 2 * tile)
        v = dot3(g[0, at], g[1, at], yh[...], yl[...])
        ah, al = split(interleave(v[:tile], -v[tile:]))
        v = dot3(ah, al, g[0], g[1])
        re, im = part_of(v, 0), part_of(v, 1)
        for t in range(per):
            s = q * per + t
            vr, vi = re[t * rows : (t + 1) * rows], im[t * rows : (t + 1) * rows]
            sr, si = srecv[s, 0], srecv[s, 1]
            part[s, 0] = sr * vr + si * vi
            part[s, 1] = sr * vi - si * vr
        for t in range(per // 2):
            to_sib(q * per // 2 + t).start()

        @pl.when(i > 0)
        def _():
            for t in range(per // 2):
                add_pair(block_at(i - 1) * per // 2 + t)

    ps1_s[...] = jnp.zeros_like(ps1_s)
    loop(0, groups, inverse)
    for t in range(per // 2):
        add_pair(first + t)
    for i in range(nz // NX):
        add_line(i)

    def exchange(send, recv, ssem, rsem, me, size, where):
        recv[me] = send[...]

        def go(k):
            t = lax.rem(me + k, size)
            remote(send, recv.at[me], ssem, rsem, where(t)).start()

        loop(1, size, go)
        others = recv.at[pl.ds(0, size - 1)]
        remote(others, others, ssem, rsem, where(lax.rem(me + 1, size))).wait_recv()
        return functools.reduce(jnp.add, [recv[i] for i in range(size)])

    ps2_s[...] = exchange(ps1_s, ps1, p1s, p1r, y, n, at_y)
    sums = jnp.sum(exchange(ps2_s, ps2, p2s, p2r, w, m, at_z), axis=1, keepdims=True)
    norm_old, curvature, applied2 = sums[0:1], sums[1:2], sums[2:3]
    alpha = norm_old / curvature
    norm_new = jnp.maximum(alpha * alpha * applied2 - norm_old, 0.0)
    out_alpha[...] = jnp.broadcast_to(alpha, (1, cols))
    out_beta[...] = jnp.broadcast_to(norm_new / norm_old, (1, cols))

    for s in range(slab):
        @pl.when(jnp.logical_not(from_self(s)))
        def _():
            remote(fin.at[0], image.at[s], fs.at[0], fr.at[s], dev(s, around(pos[s] - shift(s)), slab * pos[s] + s, core)).wait_recv()

        for p in range(2):
            out_app[p, s] = image[s, p]

    for recv, ssem, rsem, size, there in ((ps1, p1s, p1r, n, at_y(up_y)), (ps2, p2s, p2r, m, at_z(up_z))):
        others = recv.at[pl.ds(0, size - 1)]
        remote(others, others, ssem, rsem, there).wait_send()
    for h in halo1 + halo2:
        h.wait_send()
    for j in range(slab):
        @pl.when(moved(j))
        def _():
            res_over(j).wait_send()

        @pl.when(jnp.logical_not(from_self(j)))
        def _():
            local_over(j).wait_send()

        maps_over(j, pos[j], sib).wait_send()
        for k, c in steps:
            @pl.when(hops(j, k))
            def _():
                maps_over(j, around(pos[j] - shift(j) - k), c).wait_send()

        def sent_maps(t):
            zt, _, cp = pass_on(sbuf.at[0, j], j, t)

            @pl.when(zt != z)
            def _():
                cp.wait_send()

        loop(0, line, sent_maps)
        zt, cp = forward_res(j)

        @pl.when(zt != z)
        def _():
            cp.wait_send()

    for i in range(nz // NX):
        for k in range(1, NX):
            hand(2 * (first + i) + core, i, k).wait_send()
        zz, cp = home(i)

        @pl.when(jnp.logical_not(jnp.logical_and(sp == lp, zz == z)))
        def _():
            cp.wait_send()

    def sent_sums(zz):
        to_other(zz).wait_send()
        to_sib(zz).wait_send()
        t, cp = to_adder(zz)

        @pl.when(t != lp)
        def _():
            cp.wait_send()

    loop(0, nz, sent_sums)


def matrix(length, rows):
    k = np.arange(length)
    angle = 2.0 * np.pi / length * (np.outer(k, k) % length)
    c, s = np.cos(angle), np.sin(angle)
    g = np.block([[c, s], [-s, c]])
    blocks = length // rows
    order = np.arange(2 * length).reshape(2, blocks, rows).transpose(1, 0, 2).reshape(-1)
    g = g[order][:, order]
    g = g.astype(np.float32)
    h = g.astype(ml_dtypes.bfloat16)
    return np.stack([h, (g - h.astype(np.float32)).astype(ml_dtypes.bfloat16)])


def body(n, m, solution, residual, sensitivity, sampling):
    _, slab, rows, cols = solution.shape
    coils = sensitivity.shape[1]
    full = n * rows
    g = jnp.asarray(matrix(full, LANES))
    vmem = pl.BlockSpec(memory_space=pltpu.VMEM)
    hbm = pl.BlockSpec(memory_space=pl.ANY)
    dma = pltpu.SemaphoreType.DMA
    chunk = (2, rows, cols)

    def f32(*shape):
        return pltpu.VMEM(shape, F32)

    def bf16(*shape):
        return pltpu.VMEM(shape, BF16)

    applied, alpha, beta = pl.pallas_call(
        functools.partial(kernel, n, m),
        out_shape=(jax.ShapeDtypeStruct(solution.shape, F32),) + 2 * (jax.ShapeDtypeStruct((1, cols), F32),),
        in_specs=5 * [hbm],
        out_specs=(vmem, vmem, vmem),
        scratch_shapes=[
            f32(*solution.shape), f32(*residual.shape), bf16(*sensitivity.shape),
            f32(coils, slab, *chunk), f32(slab, 2 * NX, *chunk), f32(n, *chunk), f32(slab, *chunk), f32(n, *chunk),
            bf16(2 * LANES, cols), bf16(2 * LANES, cols), f32(2 * full, cols), bf16(2 * full, cols), bf16(2 * full, cols),
            pltpu.VMEM(sampling.shape, sampling.dtype), bf16(*g.shape),
            f32(n, *chunk), f32(n // 2, *chunk), f32(n // 2, *chunk), f32(n // 2 // NX, NX, *chunk), f32(2, *chunk),
            f32(slab, *chunk), f32(*solution.shape), f32(slab, *chunk), f32(n // 2 // NX, *chunk),
            f32(2, *chunk), f32(8, cols), f32(8, cols), f32(*chunk), f32(*chunk), f32(8, cols), f32(8, cols),
            f32(8, LANES), f32(n, 8, LANES), f32(8, LANES), f32(m, 8, LANES),
            dma((5,)), dma((2 * NX * slab,)), dma((2 * NX * slab,)), dma((2 * NX * slab,)), dma((n,)), dma((slab,)), dma((slab,)),
            dma((slab,)), dma((n,)), dma((n // 2 // NX * NX,)), dma((n // 2,)),
            dma((n // 2,)), dma((n // 2,)), dma((n // 2,)), dma((n // 2,)), dma((n // 2 // NX,)), dma((slab,)),
            dma((5,)), dma((5,)), dma((slab,)), dma((n // 2 // NX,)), dma, dma, dma, dma,
        ],
        compiler_params=pltpu.CompilerParams(
            collective_id=0, has_side_effects=True, vmem_limit_bytes=56 * 1024 * 1024
        ),
        name="iteration",
    )(solution, residual, sensitivity, sampling, g)
    alpha, beta = alpha[0], beta[0]
    new_residual = residual - alpha * applied
    return solution + alpha * residual, new_residual, new_residual + beta * residual


def solution(mesh):
    n, m = mesh.shape["gy"], mesh.shape["gz"]
    field = P(None, "gz", "gy", None)
    return jax.shard_map(
        functools.partial(body, n, m),
        mesh=mesh,
        in_specs=(field, field, P(None, None, "gz", "gy", None), P()),
        out_specs=(field, field, field),
        check_vma=False,
    )
```

```python
import functools

import jax
import jax.numpy as jnp
import ml_dtypes
import numpy as np
from jax import lax
from jax.experimental import pallas as pl
from jax.experimental.pallas import tpu as pltpu
from jax.sharding import PartitionSpec as P

TV_EPS = 0.1
TV_WEIGHT = 0.1
TIKHONOV = 0.1
MESH = pl.DeviceIdType.MESH
F32 = jnp.float32
BF16 = jnp.bfloat16
LANES = 128
NX = 4


def split(x):
    high = x.astype(BF16)
    return high, (x - high.astype(F32)).astype(BF16)


def dot(a, b):
    return jnp.dot(a, b, preferred_element_type=F32)


def dot3(ah, al, bh, bl):
    return dot(ah, bh) + (dot(ah, bl) + dot(al, bh))


def fold(x):
    parts = [
        x[r : r + 8, c : c + LANES] for r in range(0, x.shape[0], 8) for c in range(0, x.shape[1], LANES)
    ]
    return functools.reduce(jnp.add, parts)


def total(x):
    return jnp.sum(jnp.sum(x, axis=0, keepdims=True), axis=1, keepdims=True)


def interleave(a, b):
    parts = []
    for i in range(a.shape[1] // LANES):
        parts += [a[:, i * LANES : (i + 1) * LANES], b[:, i * LANES : (i + 1) * LANES]]
    return jnp.concatenate(parts, axis=1)


def part_of(v, i):
    return jnp.concatenate([v[:, (2 * b + i) * LANES : (2 * b + i + 1) * LANES] for b in range(v.shape[1] // LANES // 2)], axis=1)


def kernel(
    n, m, sol_in, res_in, sens_in, samp_in, g_in,
    out_app, out_alpha, out_beta,
    sol, res, sens, sbuf, relay, srecv, xrel, xall, vh, vl, yacc, yh, yl, samp, g,
    part, pair, tot, gath, fin, image, smooth, local, local_in,
    hz, hy_s, hy, qz_s, qz, qy_s, qy, ps1_s, ps1, ps2_s, ps2,
    csem, xls, xlr, zs, zr, xrs, xrr, xzs, xar, ms, os,
    prs, prr, gs, gr, fs, fr, hs, hr, ls, lr, p1s, p1r, p2s, p2r,
):
    y = lax.axis_index("gy")
    w = lax.axis_index("gz")
    z, core = y // 2, lax.rem(y, 2)
    x, yy = w // NX, lax.rem(w, NX)
    nz = n // 2
    slab, rows, cols = res.shape[1:]
    sib = 1 - core
    pos = (x, yy)
    odd = lax.rem(z, 2)
    lp = (1 - odd) * x + odd * yy
    sp = z // 2
    l = 2 * lp + core
    line = 2 * NX

    def dev(j, p, z_, core_):
        return (2 * z_ + core_, NX * x + p if j else NX * p + yy)

    def on_line(p, z_, core_):
        return (2 * z_ + core_, (1 - odd) * (NX * p + yy) + odd * (NX * x + p))

    def at_y(t):
        return (t, w)

    def at_z(t):
        return (y, t)

    other = (yy, x)

    def around(t):
        return lax.rem(t + 4 * NX, NX)

    def shift(j):
        return sp + other[j] + 2 * j

    def rows_at(k):
        return around(sp - x - yy - 2 * odd - k)

    def remote(src, dst, ssem, rsem, device):
        return pltpu.make_async_remote_copy(
            src_ref=src, dst_ref=dst, send_sem=ssem, recv_sem=rsem, device_id=device, device_id_type=MESH
        )

    def loop(lo, hi, f):
        def step(i, c):
            f(i)
            return c

        lax.fori_loop(lo, hi, step, 0)

    loads = [
        pltpu.make_async_copy(a, b, csem.at[i])
        for i, (a, b) in enumerate([(sens_in, sens), (res_in, res), (sol_in, sol), (g_in, g), (samp_in, samp)])
    ]
    for c in loads:
        c.start()

    barrier = pltpu.get_barrier_semaphore()

    def hail(device):
        pl.semaphore_signal(barrier, inc=1, device_id=device, device_id_type=MESH)

    loop(1, n, lambda k: hail(at_y(lax.rem(y + k, n))))
    loop(1, m, lambda k: hail(at_z(lax.rem(w + k, m))))
    for j in range(slab):
        loop(1, NX, lambda k: hail(dev(j, lax.rem(pos[j] + k, NX), z, sib)))
        hail(dev(j, around(pos[j] - shift(j)), slab * pos[j] + j, core))

    def from_self(j):
        return jnp.logical_and(around(shift(j)) == 0, slab * pos[j] + j == z)

    def widen(c):
        for j in range(slab):
            sbuf[c, j, 0] = sens[0, c, j].astype(F32)
            sbuf[c, j, 1] = sens[1, c, j].astype(F32)

    loads[0].wait()
    loop(0, line, widen)
    loads[1].wait()
    loads[2].wait()

    up_y, down_y = lax.rem(y + 1, n), lax.rem(y + n - 1, n)
    up_z, down_z = lax.rem(w + 1, m), lax.rem(w + m - 1, m)
    for f, field in enumerate((sol, res)):
        for p in range(2):
            for s in range(slab):
                i = f * 2 * slab + p * slab + s
                hy_s[i : i + 1, :] = field[p, s, 0:1, :]

    pl.semaphore_wait(barrier, n + m - 2 + slab * NX)

    def pass_on(src, j, t):
        zt = slab * (t // 2) + j
        slot = 2 * z + lax.rem(t, 2)
        cp = remote(src, srecv.at[slot], zs.at[line * j + t], zr.at[slot], dev(0, x, zt, core))
        return zt, slot, cp

    def forward_maps(src, j, t):
        zt, slot, cp = pass_on(src, j, t)

        @pl.when(zt != z)
        def _():
            cp.start()

        @pl.when(zt == z)
        def _():
            srecv[slot] = src[...]

    def maps_over(j, p, c):
        t = 2 * p + c
        me = 2 * pos[j] + core
        return remote(sbuf.at[t, j], relay.at[j, me], xls.at[line * j + t], xlr.at[line * j + me], dev(j, p, z, c))

    for j in range(slab):
        t = 2 * pos[j] + core
        forward_maps(sbuf.at[t, j], j, t)
        maps_over(j, pos[j], sib).start()

    def moved(j):
        return around(shift(j)) != 0

    def res_over(j):
        return remote(res.at[:, j], xrel.at[j], xrs.at[j], xrr.at[j], dev(j, around(pos[j] - shift(j)), z, core))

    for j in range(slab):
        @pl.when(moved(j))
        def _():
            res_over(j).start()

        @pl.when(jnp.logical_not(moved(j)))
        def _():
            xrel[j] = res[:, j]

    steps = [(k, c) for k in range(NX) for c in (core, sib)]

    def hops(j, k):
        return around(shift(j) + k) != 0

    for k, c in steps:
        for j in range(slab):
            @pl.when(hops(j, k))
            def _():
                maps_over(j, around(pos[j] - shift(j) - k), c).start()

    halo1 = [
        remote(sol.at[:, 0], hz.at[0], hs.at[0], hr.at[0], at_z(down_z)),
        remote(res.at[:, 0], hz.at[1], hs.at[1], hr.at[1], at_z(down_z)),
        remote(hy_s, hy, hs.at[2], hr.at[2], at_y(down_y)),
    ]
    for h in halo1:
        h.start()

    def relay_maps(j, p, c):
        t = 2 * p + c
        remote(sbuf.at[t, j], relay.at[j, t], xls.at[line * j + t], xlr.at[line * j + t], dev(j, p, z, c)).wait_recv()
        forward_maps(relay.at[j, t], j, t)

    for j in range(slab):
        relay_maps(j, pos[j], sib)

    def forward_res(j):
        zt = slab * around(pos[j] + shift(j)) + j
        return zt, remote(xrel.at[j], xall.at[y], xzs.at[j], xar.at[y], dev(0, x, zt, core))

    for j in range(slab):
        @pl.when(moved(j))
        def _():
            res_over(j).wait_recv()

        zt, cp = forward_res(j)

        @pl.when(zt != z)
        def _():
            cp.start()

        @pl.when(zt == z)
        def _():
            xall[y] = xrel[j]

    for k, c in steps:
        for j in range(slab):
            @pl.when(hops(j, k))
            def _():
                relay_maps(j, around(pos[j] + shift(j) + k), c)

    first = 2 * rows_at(0)

    def hand(slot, i, k):
        p = around(lp + k)
        return remote(xall.at[slot], xall.at[slot], ms.at[i * NX + k], xar.at[slot], on_line(p, z, core))

    def to_other(zz):
        slot = 2 * zz + core
        return remote(xall.at[slot], xall.at[slot], os.at[zz], xar.at[slot], on_line(lp, z, sib))

    for i in range(nz // NX):
        zz = first + i
        slot = 2 * zz + core

        @pl.when(zz != z)
        def _():
            remote(xrel.at[0], xall.at[slot], xzs.at[0], xar.at[slot], dev(0, x, zz, core)).wait_recv()

        for k in range(1, NX):
            hand(slot, i, k).start()
        to_other(zz).start()

    for h in halo1:
        h.wait_recv()
    row = lax.broadcasted_iota(jnp.int32, (rows, cols), 0)
    col = lax.broadcasted_iota(jnp.int32, (rows, cols), 1)
    keep_y = jnp.logical_or(row < rows - 1, y < n - 1)
    keep_z = jnp.full((rows, cols), w, jnp.int32) < m - 1

    def ahead(f, field, p, s):
        v = field[p, s]
        dx = jnp.where(col == cols - 1, 0.0, pltpu.roll(v, cols - 1, 1) - v)
        i = f * 2 * slab + p * slab + s
        nxt = jnp.where(row == rows - 1, jnp.broadcast_to(hy[i : i + 1, :], (rows, cols)), pltpu.roll(v, rows - 1, 0))
        dy = jnp.where(keep_y, nxt - v, 0.0)
        if s + 1 < slab:
            dz = field[p, s + 1] - v
        else:
            dz = jnp.where(keep_z, hz[f, p] - v, 0.0)
        return dx, dy, dz

    qy_s[...] = jnp.zeros_like(qy_s)
    for s in range(slab):
        sq = jnp.zeros((rows, cols), F32)
        for p in range(2):
            for d in ahead(0, sol, p, s):
                sq = sq + d * d
        weight = 1.0 / jnp.sqrt(sq + TV_EPS * TV_EPS)
        for p in range(2):
            dx, dy, dz = (weight * d for d in ahead(1, res, p, s))
            before_x = jnp.where(col == 0, 0.0, pltpu.roll(dx, 1, 1))
            before_y = jnp.where(row == 0, 0.0, pltpu.roll(dy, 1, 0))
            here = (before_x - dx) + (before_y - dy) - dz
            if s > 0:
                here = here + qz_s[p]
            smooth[p, s] = here
            qz_s[p] = dz
            i = p * slab + s
            qy_s[i : i + 1, :] = dy[rows - 1 : rows, :]
    halo2 = [
        remote(qz_s, qz, hs.at[3], hr.at[3], at_z(up_z)),
        remote(qy_s, qy, hs.at[4], hr.at[4], at_y(up_y)),
    ]
    for h in halo2:
        h.start()

    for k in range(1, NX):
        for i in range(nz // NX):
            zz = 2 * rows_at(k) + i
            slot = 2 * zz + core
            remote(xall.at[slot], xall.at[slot], ms.at[0], xar.at[slot], on_line(around(lp + k), z, core)).wait_recv()
            to_other(zz).start()

    per = 4
    tile = per * rows
    groups = n // per

    def ready(s):
        zz = s // 2

        @pl.when(zz != z)
        def _():
            remote(relay.at[0, 0], srecv.at[s], zs.at[0], zr.at[s], dev(0, x, zz, core)).wait_recv()

        @pl.when(lax.rem(s, 2) == sib)
        def _():
            remote(xall.at[s], xall.at[s], os.at[0], xar.at[s], on_line(lp, z, sib)).wait_recv()

    at_zero = jnp.full((rows, cols), w, jnp.int32) > 0
    at_top = jnp.logical_and(row == 0, y > 0)

    def local_over(j):
        there = dev(j, around(pos[j] - shift(j)), slab * pos[j] + j, core)
        return remote(local.at[j], local_in.at[odd], ls.at[j], lr.at[odd], there)

    def send_local():
        for h in halo2:
            h.wait_recv()
        for p in range(2):
            for s in range(slab):
                i = p * slab + s
                v = smooth[p, s] + jnp.where(at_top, jnp.broadcast_to(qy[i : i + 1, :], (rows, cols)), 0.0)
                if s == 0:
                    v = v + jnp.where(at_zero, qz[p], 0.0)
                local[s, p] = TIKHONOV * res[p, s] - TV_WEIGHT * v
        for j in range(slab):
            @pl.when(jnp.logical_not(from_self(j)))
            def _():
                local_over(j).start()

            @pl.when(from_self(j))
            def _():
                local_in[odd] = local[j]

    full = n * rows
    scale = 1.0 / (full * cols)
    yacc[...] = jnp.zeros_like(yacc)
    loads[3].wait()
    loads[4].wait()

    def forward(i):
        q = rows_at(i)
        last = i == groups - 1

        @pl.when(last)
        def _():
            send_local()

        for t in range(per):
            ready(q * per + t)
        block = []
        for t in range(per):
            sr, si = srecv[q * per + t, 0], srecv[q * per + t, 1]
            xr, xi = xall[q * per + t, 0], xall[q * per + t, 1]
            block.append(interleave(sr * xr - si * xi, -(sr * xi + si * xr)))
        ah, al = split(jnp.concatenate(block, axis=0))
        v = dot3(ah, al, g[0], g[1])
        vh[:tile], vl[:tile] = split(part_of(v, 0))
        vh[tile:], vl[tile:] = split(-part_of(v, 1))

        def rows_tile(t):
            at = pl.ds(pl.multiple_of(2 * t * tile, 2 * tile), 2 * tile)
            k = pl.ds(pl.multiple_of(2 * q * tile, 2 * tile), 2 * tile)
            v = yacc[at] + dot3(g[0, at, k], g[1, at, k], vh[...], vl[...])

            @pl.when(jnp.logical_not(last))
            def _():
                yacc[at] = v

            @pl.when(last)
            def _():
                taken = samp[pl.ds(pl.multiple_of(t * tile, tile), tile)].astype(F32) * scale
                yh[at], yl[at] = split(v * jnp.concatenate([taken, -taken], axis=0))

        loop(0, groups, rows_tile)

    loop(0, groups, forward)

    def to_sib(zz):
        return remote(part.at[2 * zz + sib], pair.at[zz], prs.at[zz], prr.at[zz], on_line(lp, z, sib))

    def to_adder(zz):
        t = around(lp + rows_at(0) - zz // 2)
        i = lax.rem(zz, 2)
        return t, remote(tot.at[zz], gath.at[i, lp], gs.at[zz], gr.at[NX * i + lp], on_line(t, z, core))

    def add_pair(zz):
        to_sib(zz).wait_recv()
        tot[zz] = part[2 * zz + core] + pair[zz]
        t, cp = to_adder(zz)

        @pl.when(t != lp)
        def _():
            cp.start()

    def home(i):
        zz = first + i
        return zz, remote(fin.at[i], image.at[odd], fs.at[i], fr.at[odd], on_line(sp, zz, core))

    def add_line(i, sums):
        zz = first + i
        v = tot[zz]
        for k in range(1, NX):
            t = around(lp + k)
            remote(tot.at[zz], gath.at[i, t], gs.at[zz], gr.at[NX * i + t], on_line(t, z, core)).wait_recv()
            v = v + gath[i, t]

        @pl.when(jnp.logical_not(jnp.logical_and(sp == lp, zz == z)))
        def _():
            remote(local.at[0], local_in.at[i], ls.at[0], lr.at[i], on_line(sp, zz, core)).wait_recv()

        v = v + local_in[i]
        for p in range(2):
            a, r = v[p], xall[2 * zz + core, p]
            for k, term in enumerate((r * r, r * a, a * a)):
                sums[k] = sums[k] + fold(term)
        here = jnp.logical_and(sp == lp, zz == z)

        @pl.when(here)
        def _():
            image[odd] = v

        @pl.when(jnp.logical_not(here))
        def _():
            fin[i] = v

    def block_at(i):
        return rows_at(2 + i - (i // 2) * (2 * i - 1))

    def inverse(i):
        q = block_at(i)
        at = pl.ds(pl.multiple_of(2 * q * tile, 2 * tile), 2 * tile)
        v = dot3(g[0, at], g[1, at], yh[...], yl[...])
        ah, al = split(interleave(v[:tile], -v[tile:]))
        v = dot3(ah, al, g[0], g[1])
        re, im = part_of(v, 0), part_of(v, 1)
        for t in range(per):
            s = q * per + t
            vr, vi = re[t * rows : (t + 1) * rows], im[t * rows : (t + 1) * rows]
            sr, si = srecv[s, 0], srecv[s, 1]
            part[s, 0] = sr * vr + si * vi
            part[s, 1] = sr * vi - si * vr
        for t in range(per // 2):
            to_sib(q * per // 2 + t).start()

        @pl.when(i > 0)
        def _():
            for t in range(per // 2):
                add_pair(block_at(i - 1) * per // 2 + t)

    loop(0, groups, inverse)
    for t in range(per // 2):
        add_pair(first + t)
    sums = [jnp.zeros((8, LANES), F32) for _ in range(3)]
    for i in range(nz // NX):
        add_line(i, sums)
    sums = [total(v) for v in sums]
    lane = lax.broadcasted_iota(jnp.int32, (1, LANES), 1)
    ps1_s[...] = jnp.where(lane == 0, sums[0], jnp.where(lane == 1, sums[1], sums[2]))

    def start_home():
        for i in range(nz // NX):
            zz, cp = home(i)

            @pl.when(jnp.logical_not(jnp.logical_and(sp == lp, zz == z)))
            def _():
                cp.start()

    def wait_home():
        for i in range(nz // NX):
            zz, cp = home(i)

            @pl.when(jnp.logical_not(jnp.logical_and(sp == lp, zz == z)))
            def _():
                cp.wait_send()

    def wait_sends():
        for h in halo1 + halo2:
            h.wait_send()
        for j in range(slab):
            @pl.when(moved(j))
            def _():
                res_over(j).wait_send()

            @pl.when(jnp.logical_not(from_self(j)))
            def _():
                local_over(j).wait_send()

            maps_over(j, pos[j], sib).wait_send()
            for k, c in steps:
                @pl.when(hops(j, k))
                def _():
                    maps_over(j, around(pos[j] - shift(j) - k), c).wait_send()

            def sent_maps(t):
                zt, _, cp = pass_on(sbuf.at[0, j], j, t)

                @pl.when(zt != z)
                def _():
                    cp.wait_send()

            loop(0, line, sent_maps)
            zt, cp = forward_res(j)

            @pl.when(zt != z)
            def _():
                cp.wait_send()

        for i in range(nz // NX):
            for k in range(1, NX):
                hand(2 * (first + i) + core, i, k).wait_send()

        def sent_sums(zz):
            to_other(zz).wait_send()
            to_sib(zz).wait_send()
            t, cp = to_adder(zz)

            @pl.when(t != lp)
            def _():
                cp.wait_send()

        loop(0, nz, sent_sums)

    def exchange(send, recv, ssem, rsem, me, size, where, meanwhile):
        recv[me] = send[...]

        def go(k):
            t = lax.rem(me + k, size)
            remote(send, recv.at[me], ssem, rsem, where(t)).start()

        loop(1, size, go)
        for f in meanwhile:
            f()
        others = recv.at[pl.ds(0, size - 1)]
        remote(others, others, ssem, rsem, where(lax.rem(me + 1, size))).wait_recv()
        return functools.reduce(jnp.add, [recv[i] for i in range(size)])

    ps2_s[...] = exchange(ps1_s, ps1, p1s, p1r, y, n, at_y, (start_home, wait_sends))
    sums = exchange(ps2_s, ps2, p2s, p2r, w, m, at_z, (wait_home,))
    norm_old, curvature, applied2 = sums[:, 0:1], sums[:, 1:2], sums[:, 2:3]
    alpha = norm_old / curvature
    norm_new = jnp.maximum(alpha * alpha * applied2 - norm_old, 0.0)
    out_alpha[...] = jnp.broadcast_to(alpha, (1, cols))
    out_beta[...] = jnp.broadcast_to(norm_new / norm_old, (1, cols))

    for s in range(slab):
        @pl.when(jnp.logical_not(from_self(s)))
        def _():
            remote(fin.at[0], image.at[s], fs.at[0], fr.at[s], dev(s, around(pos[s] - shift(s)), slab * pos[s] + s, core)).wait_recv()

        for p in range(2):
            out_app[p, s] = image[s, p]

    for recv, ssem, rsem, size, there in ((ps1, p1s, p1r, n, at_y(up_y)), (ps2, p2s, p2r, m, at_z(up_z))):
        others = recv.at[pl.ds(0, size - 1)]
        remote(others, others, ssem, rsem, there).wait_send()


def matrix(length, rows):
    k = np.arange(length)
    angle = 2.0 * np.pi / length * (np.outer(k, k) % length)
    c, s = np.cos(angle), np.sin(angle)
    g = np.block([[c, s], [-s, c]])
    blocks = length // rows
    order = np.arange(2 * length).reshape(2, blocks, rows).transpose(1, 0, 2).reshape(-1)
    g = g[order][:, order]
    g = g.astype(np.float32)
    h = g.astype(ml_dtypes.bfloat16)
    return np.stack([h, (g - h.astype(np.float32)).astype(ml_dtypes.bfloat16)])


def body(n, m, solution, residual, sensitivity, sampling):
    _, slab, rows, cols = solution.shape
    coils = sensitivity.shape[1]
    full = n * rows
    g = jnp.asarray(matrix(full, LANES))
    vmem = pl.BlockSpec(memory_space=pltpu.VMEM)
    hbm = pl.BlockSpec(memory_space=pl.ANY)
    dma = pltpu.SemaphoreType.DMA
    chunk = (2, rows, cols)

    def f32(*shape):
        return pltpu.VMEM(shape, F32)

    def bf16(*shape):
        return pltpu.VMEM(shape, BF16)

    applied, alpha, beta = pl.pallas_call(
        functools.partial(kernel, n, m),
        out_shape=(jax.ShapeDtypeStruct(solution.shape, F32),) + 2 * (jax.ShapeDtypeStruct((1, cols), F32),),
        in_specs=5 * [hbm],
        out_specs=(vmem, vmem, vmem),
        scratch_shapes=[
            f32(*solution.shape), f32(*residual.shape), bf16(*sensitivity.shape),
            f32(coils, slab, *chunk), f32(slab, 2 * NX, *chunk), f32(n, *chunk), f32(slab, *chunk), f32(n, *chunk),
            bf16(2 * LANES, cols), bf16(2 * LANES, cols), f32(2 * full, cols), bf16(2 * full, cols), bf16(2 * full, cols),
            pltpu.VMEM(sampling.shape, sampling.dtype), bf16(*g.shape),
            f32(n, *chunk), f32(n // 2, *chunk), f32(n // 2, *chunk), f32(n // 2 // NX, NX, *chunk), f32(2, *chunk),
            f32(slab, *chunk), f32(*solution.shape), f32(slab, *chunk), f32(n // 2 // NX, *chunk),
            f32(2, *chunk), f32(8, cols), f32(8, cols), f32(*chunk), f32(*chunk), f32(8, cols), f32(8, cols),
            f32(1, LANES), f32(n, 1, LANES), f32(1, LANES), f32(m, 1, LANES),
            dma((5,)), dma((2 * NX * slab,)), dma((2 * NX * slab,)), dma((2 * NX * slab,)), dma((n,)), dma((slab,)), dma((slab,)),
            dma((slab,)), dma((n,)), dma((n // 2 // NX * NX,)), dma((n // 2,)),
            dma((n // 2,)), dma((n // 2,)), dma((n // 2,)), dma((n // 2,)), dma((n // 2 // NX,)), dma((slab,)),
            dma((5,)), dma((5,)), dma((slab,)), dma((n // 2 // NX,)), dma, dma, dma, dma,
        ],
        compiler_params=pltpu.CompilerParams(
            collective_id=0, has_side_effects=True, vmem_limit_bytes=56 * 1024 * 1024
        ),
        name="iteration",
    )(solution, residual, sensitivity, sampling, g)
    alpha, beta = alpha[0], beta[0]
    new_residual = residual - alpha * applied
    return solution + alpha * residual, new_residual, new_residual + beta * residual


def solution(mesh):
    n, m = mesh.shape["gy"], mesh.shape["gz"]
    field = P(None, "gz", "gy", None)
    return jax.shard_map(
        functools.partial(body, n, m),
        mesh=mesh,
        in_specs=(field, field, P(None, None, "gz", "gy", None), P()),
        out_specs=(field, field, field),
        check_vma=False,
    )
```

```python
import functools

import jax
import jax.numpy as jnp
import ml_dtypes
import numpy as np
from jax import lax
from jax.experimental import pallas as pl
from jax.experimental.pallas import tpu as pltpu
from jax.sharding import PartitionSpec as P

TV_EPS = 0.1
TV_WEIGHT = 0.1
TIKHONOV = 0.1
MESH = pl.DeviceIdType.MESH
F32 = jnp.float32
BF16 = jnp.bfloat16
LANES = 128
NX = 4


def split(x):
    high = x.astype(BF16)
    return high, (x - high.astype(F32)).astype(BF16)


def dot(a, b):
    return jnp.dot(a, b, preferred_element_type=F32)


def dot3(ah, al, bh, bl):
    return dot(ah, bh) + (dot(ah, bl) + dot(al, bh))


def fold(x):
    parts = [
        x[r : r + 8, c : c + LANES] for r in range(0, x.shape[0], 8) for c in range(0, x.shape[1], LANES)
    ]
    return functools.reduce(jnp.add, parts)


def total(x):
    return jnp.sum(jnp.sum(x, axis=0, keepdims=True), axis=1, keepdims=True)


def interleave(a, b):
    parts = []
    for i in range(a.shape[1] // LANES):
        parts += [a[:, i * LANES : (i + 1) * LANES], b[:, i * LANES : (i + 1) * LANES]]
    return jnp.concatenate(parts, axis=1)


def part_of(v, i):
    return jnp.concatenate([v[:, (2 * b + i) * LANES : (2 * b + i + 1) * LANES] for b in range(v.shape[1] // LANES // 2)], axis=1)


def kernel(
    n, m, sol_in, res_in, sens_in, samp_in, g_in,
    out_app, out_alpha, out_beta,
    sol, res, sens, sbuf, relay, srecv, xrel, xall, vh, vl, yacc, yh, yl, samp, g,
    part, pair, tot, gath, fin, image, smooth, local, local_in,
    hz, hy_s, hy, qz_s, qz, qy_s, qy, ps1_s, ps1, ps2_s, ps2,
    csem, xls, xlr, zs, zr, xrs, xrr, xzs, xar, ms, os,
    prs, prr, gs, gr, fs, fr, hs, hr, ls, lr, p1s, p1r, p2s, p2r,
):
    y = lax.axis_index("gy")
    w = lax.axis_index("gz")
    z, core = y // 2, lax.rem(y, 2)
    x, yy = w // NX, lax.rem(w, NX)
    nz = n // 2
    slab, rows, cols = res.shape[1:]
    sib = 1 - core
    pos = (x, yy)
    odd = lax.rem(z, 2)
    lp = (1 - odd) * x + odd * yy
    sp = z // 2
    l = 2 * lp + core
    line = 2 * NX

    def dev(j, p, z_, core_):
        return (2 * z_ + core_, NX * x + p if j else NX * p + yy)

    def on_line(p, z_, core_):
        return (2 * z_ + core_, (1 - odd) * (NX * p + yy) + odd * (NX * x + p))

    def at_y(t):
        return (t, w)

    def at_z(t):
        return (y, t)

    other = (yy, x)

    def around(t):
        return lax.rem(t + 4 * NX, NX)

    def shift(j):
        return sp + other[j] + 2 * j

    def rows_at(k):
        return around(sp - x - yy - 2 * odd - k)

    def remote(src, dst, ssem, rsem, device):
        return pltpu.make_async_remote_copy(
            src_ref=src, dst_ref=dst, send_sem=ssem, recv_sem=rsem, device_id=device, device_id_type=MESH
        )

    def loop(lo, hi, f):
        def step(i, c):
            f(i)
            return c

        lax.fori_loop(lo, hi, step, 0)

    loads = [
        pltpu.make_async_copy(a, b, csem.at[i])
        for i, (a, b) in enumerate([(sens_in, sens), (res_in, res), (sol_in, sol), (g_in, g), (samp_in, samp)])
    ]
    for c in loads:
        c.start()

    barrier = pltpu.get_barrier_semaphore()

    def hail(device):
        pl.semaphore_signal(barrier, inc=1, device_id=device, device_id_type=MESH)

    loop(1, n, lambda k: hail(at_y(lax.rem(y + k, n))))
    loop(1, m, lambda k: hail(at_z(lax.rem(w + k, m))))
    for j in range(slab):
        loop(1, NX, lambda k: hail(dev(j, lax.rem(pos[j] + k, NX), z, sib)))
        hail(dev(j, around(pos[j] - shift(j)), slab * pos[j] + j, core))

    def from_self(j):
        return jnp.logical_and(around(shift(j)) == 0, slab * pos[j] + j == z)

    def widen(c):
        for j in range(slab):
            sbuf[c, j, 0] = sens[0, c, j].astype(F32)
            sbuf[c, j, 1] = sens[1, c, j].astype(F32)

    loads[0].wait()
    loop(0, line, widen)
    loads[1].wait()
    loads[2].wait()

    up_y, down_y = lax.rem(y + 1, n), lax.rem(y + n - 1, n)
    up_z, down_z = lax.rem(w + 1, m), lax.rem(w + m - 1, m)
    for f, field in enumerate((sol, res)):
        for p in range(2):
            for s in range(slab):
                i = f * 2 * slab + p * slab + s
                hy_s[i : i + 1, :] = field[p, s, 0:1, :]

    pl.semaphore_wait(barrier, n + m - 2 + slab * NX)

    def pass_on(src, j, t):
        zt = slab * (t // 2) + j
        slot = 2 * z + lax.rem(t, 2)
        cp = remote(src, srecv.at[slot], zs.at[line * j + t], zr.at[slot], dev(0, x, zt, core))
        return zt, slot, cp

    def forward_maps(src, j, t):
        zt, slot, cp = pass_on(src, j, t)

        @pl.when(zt != z)
        def _():
            cp.start()

        @pl.when(zt == z)
        def _():
            srecv[slot] = src[...]

    def maps_over(j, p, c):
        t = 2 * p + c
        me = 2 * pos[j] + core
        return remote(sbuf.at[t, j], relay.at[j, me], xls.at[line * j + t], xlr.at[line * j + me], dev(j, p, z, c))

    def hops(j, k):
        return around(shift(j) + k) != 0

    def send_step(k):
        for j in range(slab):
            @pl.when(hops(j, k))
            def _():
                maps_over(j, around(pos[j] - shift(j) - k), core).start()

        for j in range(slab):
            maps_over(j, around(pos[j] - shift(j) - k), sib).start()

    send_step(0)

    def moved(j):
        return around(shift(j)) != 0

    def res_over(j):
        return remote(res.at[:, j], xrel.at[j], xrs.at[j], xrr.at[j], dev(j, around(pos[j] - shift(j)), z, core))

    for j in range(slab):
        @pl.when(moved(j))
        def _():
            res_over(j).start()

        @pl.when(jnp.logical_not(moved(j)))
        def _():
            xrel[j] = res[:, j]

    halo1 = [
        remote(sol.at[:, 0], hz.at[0], hs.at[0], hr.at[0], at_z(down_z)),
        remote(res.at[:, 0], hz.at[1], hs.at[1], hr.at[1], at_z(down_z)),
        remote(hy_s, hy, hs.at[2], hr.at[2], at_y(down_y)),
    ]
    def relay_maps(j, p, c):
        t = 2 * p + c
        remote(sbuf.at[t, j], relay.at[j, t], xls.at[line * j + t], xlr.at[line * j + t], dev(j, p, z, c)).wait_recv()
        forward_maps(relay.at[j, t], j, t)

    def relay_step(k):
        for j in range(slab):
            @pl.when(hops(j, k))
            def _():
                relay_maps(j, around(pos[j] + shift(j) + k), core)

            @pl.when(jnp.logical_not(hops(j, k)))
            def _():
                t = 2 * pos[j] + core
                forward_maps(sbuf.at[t, j], j, t)

        for j in range(slab):
            relay_maps(j, around(pos[j] + shift(j) + k), sib)

    relay_step(0)
    send_step(1)

    def forward_res(j):
        zt = slab * around(pos[j] + shift(j)) + j
        return zt, remote(xrel.at[j], xall.at[y], xzs.at[j], xar.at[y], dev(0, x, zt, core))

    for j in range(slab):
        @pl.when(moved(j))
        def _():
            res_over(j).wait_recv()

        zt, cp = forward_res(j)

        @pl.when(zt != z)
        def _():
            cp.start()

        @pl.when(zt == z)
        def _():
            xall[y] = xrel[j]

    for h in halo1:
        h.start()
    relay_step(1)
    send_step(2)

    first = 2 * rows_at(0)

    def hand(slot, i, k):
        p = around(lp + k)
        return remote(xall.at[slot], xall.at[slot], ms.at[i * NX + k], xar.at[slot], on_line(p, z, core))

    def to_other(zz):
        slot = 2 * zz + core
        return remote(xall.at[slot], xall.at[slot], os.at[zz], xar.at[slot], on_line(lp, z, sib))

    for i in range(nz // NX):
        zz = first + i
        slot = 2 * zz + core

        @pl.when(zz != z)
        def _():
            remote(xrel.at[0], xall.at[slot], xzs.at[0], xar.at[slot], dev(0, x, zz, core)).wait_recv()

        for k in range(1, NX):
            hand(slot, i, k).start()
        to_other(zz).start()

    for k in range(2, NX):
        relay_step(k)
        if k + 1 < NX:
            send_step(k + 1)

    for h in halo1:
        h.wait_recv()
    row = lax.broadcasted_iota(jnp.int32, (rows, cols), 0)
    col = lax.broadcasted_iota(jnp.int32, (rows, cols), 1)
    keep_y = jnp.logical_or(row < rows - 1, y < n - 1)
    keep_z = jnp.full((rows, cols), w, jnp.int32) < m - 1

    def ahead(f, field, p, s):
        v = field[p, s]
        dx = jnp.where(col == cols - 1, 0.0, pltpu.roll(v, cols - 1, 1) - v)
        i = f * 2 * slab + p * slab + s
        nxt = jnp.where(row == rows - 1, jnp.broadcast_to(hy[i : i + 1, :], (rows, cols)), pltpu.roll(v, rows - 1, 0))
        dy = jnp.where(keep_y, nxt - v, 0.0)
        if s + 1 < slab:
            dz = field[p, s + 1] - v
        else:
            dz = jnp.where(keep_z, hz[f, p] - v, 0.0)
        return dx, dy, dz

    qy_s[...] = jnp.zeros_like(qy_s)
    for s in range(slab):
        sq = jnp.zeros((rows, cols), F32)
        for p in range(2):
            for d in ahead(0, sol, p, s):
                sq = sq + d * d
        weight = 1.0 / jnp.sqrt(sq + TV_EPS * TV_EPS)
        for p in range(2):
            dx, dy, dz = (weight * d for d in ahead(1, res, p, s))
            before_x = jnp.where(col == 0, 0.0, pltpu.roll(dx, 1, 1))
            before_y = jnp.where(row == 0, 0.0, pltpu.roll(dy, 1, 0))
            here = (before_x - dx) + (before_y - dy) - dz
            if s > 0:
                here = here + qz_s[p]
            smooth[p, s] = here
            qz_s[p] = dz
            i = p * slab + s
            qy_s[i : i + 1, :] = dy[rows - 1 : rows, :]
    halo2 = [
        remote(qz_s, qz, hs.at[3], hr.at[3], at_z(up_z)),
        remote(qy_s, qy, hs.at[4], hr.at[4], at_y(up_y)),
    ]
    for h in halo2:
        h.start()

    for k in range(1, NX):
        for i in range(nz // NX):
            zz = 2 * rows_at(k) + i
            slot = 2 * zz + core
            remote(xall.at[slot], xall.at[slot], ms.at[0], xar.at[slot], on_line(around(lp + k), z, core)).wait_recv()
            to_other(zz).start()

    per = 4
    tile = per * rows
    groups = n // per

    def ready(s):
        zz = s // 2

        @pl.when(zz != z)
        def _():
            remote(relay.at[0, 0], srecv.at[s], zs.at[0], zr.at[s], dev(0, x, zz, core)).wait_recv()

        @pl.when(lax.rem(s, 2) == sib)
        def _():
            remote(xall.at[s], xall.at[s], os.at[0], xar.at[s], on_line(lp, z, sib)).wait_recv()

    at_zero = jnp.full((rows, cols), w, jnp.int32) > 0
    at_top = jnp.logical_and(row == 0, y > 0)

    def local_over(j):
        there = dev(j, around(pos[j] - shift(j)), slab * pos[j] + j, core)
        return remote(local.at[j], local_in.at[odd], ls.at[j], lr.at[odd], there)

    def send_local():
        for h in halo2:
            h.wait_recv()
        for p in range(2):
            for s in range(slab):
                i = p * slab + s
                v = smooth[p, s] + jnp.where(at_top, jnp.broadcast_to(qy[i : i + 1, :], (rows, cols)), 0.0)
                if s == 0:
                    v = v + jnp.where(at_zero, qz[p], 0.0)
                local[s, p] = TIKHONOV * res[p, s] - TV_WEIGHT * v
        for j in range(slab):
            @pl.when(jnp.logical_not(from_self(j)))
            def _():
                local_over(j).start()

            @pl.when(from_self(j))
            def _():
                local_in[odd] = local[j]

    full = n * rows
    scale = 1.0 / (full * cols)
    yacc[...] = jnp.zeros_like(yacc)
    loads[3].wait()
    loads[4].wait()

    def forward(i):
        q = rows_at(i)
        last = i == groups - 1

        @pl.when(last)
        def _():
            send_local()

        for t in range(per):
            ready(q * per + t)
        block = []
        for t in range(per):
            sr, si = srecv[q * per + t, 0], srecv[q * per + t, 1]
            xr, xi = xall[q * per + t, 0], xall[q * per + t, 1]
            block.append(interleave(sr * xr - si * xi, -(sr * xi + si * xr)))
        ah, al = split(jnp.concatenate(block, axis=0))
        v = dot3(ah, al, g[0], g[1])
        vh[:tile], vl[:tile] = split(part_of(v, 0))
        vh[tile:], vl[tile:] = split(-part_of(v, 1))

        def rows_tile(t):
            at = pl.ds(pl.multiple_of(2 * t * tile, 2 * tile), 2 * tile)
            k = pl.ds(pl.multiple_of(2 * q * tile, 2 * tile), 2 * tile)
            v = yacc[at] + dot3(g[0, at, k], g[1, at, k], vh[...], vl[...])

            @pl.when(jnp.logical_not(last))
            def _():
                yacc[at] = v

            @pl.when(last)
            def _():
                taken = samp[pl.ds(pl.multiple_of(t * tile, tile), tile)].astype(F32) * scale
                yh[at], yl[at] = split(v * jnp.concatenate([taken, -taken], axis=0))

        loop(0, groups, rows_tile)

    loop(0, groups, forward)

    def to_sib(zz):
        return remote(part.at[2 * zz + sib], pair.at[zz], prs.at[zz], prr.at[zz], on_line(lp, z, sib))

    def to_adder(zz):
        t = around(lp + rows_at(0) - zz // 2)
        i = lax.rem(zz, 2)
        return t, remote(tot.at[zz], gath.at[i, lp], gs.at[zz], gr.at[NX * i + lp], on_line(t, z, core))

    def add_pair(zz):
        to_sib(zz).wait_recv()
        tot[zz] = part[2 * zz + core] + pair[zz]
        t, cp = to_adder(zz)

        @pl.when(t != lp)
        def _():
            cp.start()

    def home(i):
        zz = first + i
        return zz, remote(fin.at[i], image.at[odd], fs.at[i], fr.at[odd], on_line(sp, zz, core))

    def add_line(i, sums):
        zz = first + i
        v = tot[zz]
        for k in range(1, NX):
            t = around(lp + k)
            remote(tot.at[zz], gath.at[i, t], gs.at[zz], gr.at[NX * i + t], on_line(t, z, core)).wait_recv()
            v = v + gath[i, t]

        @pl.when(jnp.logical_not(jnp.logical_and(sp == lp, zz == z)))
        def _():
            remote(local.at[0], local_in.at[i], ls.at[0], lr.at[i], on_line(sp, zz, core)).wait_recv()

        v = v + local_in[i]
        for p in range(2):
            a, r = v[p], xall[2 * zz + core, p]
            for k, term in enumerate((r * r, r * a, a * a)):
                sums[k] = sums[k] + fold(term)
        here = jnp.logical_and(sp == lp, zz == z)

        @pl.when(here)
        def _():
            image[odd] = v

        @pl.when(jnp.logical_not(here))
        def _():
            fin[i] = v

    def block_at(i):
        return rows_at(2 + i - (i // 2) * (2 * i - 1))

    def inverse(i):
        q = block_at(i)
        at = pl.ds(pl.multiple_of(2 * q * tile, 2 * tile), 2 * tile)
        v = dot3(g[0, at], g[1, at], yh[...], yl[...])
        ah, al = split(interleave(v[:tile], -v[tile:]))
        v = dot3(ah, al, g[0], g[1])
        re, im = part_of(v, 0), part_of(v, 1)
        for t in range(per):
            s = q * per + t
            vr, vi = re[t * rows : (t + 1) * rows], im[t * rows : (t + 1) * rows]
            sr, si = srecv[s, 0], srecv[s, 1]
            part[s, 0] = sr * vr + si * vi
            part[s, 1] = sr * vi - si * vr
        for t in range(per // 2):
            to_sib(q * per // 2 + t).start()

        @pl.when(i > 0)
        def _():
            for t in range(per // 2):
                add_pair(block_at(i - 1) * per // 2 + t)

    loop(0, groups, inverse)
    for t in range(per // 2):
        add_pair(first + t)
    sums = [jnp.zeros((8, LANES), F32) for _ in range(3)]
    for i in range(nz // NX):
        add_line(i, sums)
    sums = [total(v) for v in sums]
    lane = lax.broadcasted_iota(jnp.int32, (1, LANES), 1)
    ps1_s[...] = jnp.where(lane == 0, sums[0], jnp.where(lane == 1, sums[1], sums[2]))

    def start_home():
        for i in range(nz // NX):
            zz, cp = home(i)

            @pl.when(jnp.logical_not(jnp.logical_and(sp == lp, zz == z)))
            def _():
                cp.start()

    def wait_home():
        for i in range(nz // NX):
            zz, cp = home(i)

            @pl.when(jnp.logical_not(jnp.logical_and(sp == lp, zz == z)))
            def _():
                cp.wait_send()

    def wait_sends():
        for h in halo1 + halo2:
            h.wait_send()
        for j in range(slab):
            @pl.when(moved(j))
            def _():
                res_over(j).wait_send()

            @pl.when(jnp.logical_not(from_self(j)))
            def _():
                local_over(j).wait_send()

            for k in range(NX):
                @pl.when(hops(j, k))
                def _():
                    maps_over(j, around(pos[j] - shift(j) - k), core).wait_send()

                maps_over(j, around(pos[j] - shift(j) - k), sib).wait_send()

            def sent_maps(t):
                zt, _, cp = pass_on(sbuf.at[0, j], j, t)

                @pl.when(zt != z)
                def _():
                    cp.wait_send()

            loop(0, line, sent_maps)
            zt, cp = forward_res(j)

            @pl.when(zt != z)
            def _():
                cp.wait_send()

        for i in range(nz // NX):
            for k in range(1, NX):
                hand(2 * (first + i) + core, i, k).wait_send()

        def sent_sums(zz):
            to_other(zz).wait_send()
            to_sib(zz).wait_send()
            t, cp = to_adder(zz)

            @pl.when(t != lp)
            def _():
                cp.wait_send()

        loop(0, nz, sent_sums)

    def exchange(send, recv, ssem, rsem, me, size, where, meanwhile):
        recv[me] = send[...]

        def go(k):
            t = lax.rem(me + k, size)
            remote(send, recv.at[me], ssem, rsem, where(t)).start()

        loop(1, size, go)
        for f in meanwhile:
            f()
        others = recv.at[pl.ds(0, size - 1)]
        remote(others, others, ssem, rsem, where(lax.rem(me + 1, size))).wait_recv()
        return functools.reduce(jnp.add, [recv[i] for i in range(size)])

    ps2_s[...] = exchange(ps1_s, ps1, p1s, p1r, y, n, at_y, (start_home, wait_sends))
    sums = exchange(ps2_s, ps2, p2s, p2r, w, m, at_z, (wait_home,))
    norm_old, curvature, applied2 = sums[:, 0:1], sums[:, 1:2], sums[:, 2:3]
    alpha = norm_old / curvature
    norm_new = jnp.maximum(alpha * alpha * applied2 - norm_old, 0.0)
    out_alpha[...] = jnp.broadcast_to(alpha, (1, cols))
    out_beta[...] = jnp.broadcast_to(norm_new / norm_old, (1, cols))

    for s in range(slab):
        @pl.when(jnp.logical_not(from_self(s)))
        def _():
            remote(fin.at[0], image.at[s], fs.at[0], fr.at[s], dev(s, around(pos[s] - shift(s)), slab * pos[s] + s, core)).wait_recv()

        for p in range(2):
            out_app[p, s] = image[s, p]

    for recv, ssem, rsem, size, there in ((ps1, p1s, p1r, n, at_y(up_y)), (ps2, p2s, p2r, m, at_z(up_z))):
        others = recv.at[pl.ds(0, size - 1)]
        remote(others, others, ssem, rsem, there).wait_send()


def matrix(length, rows):
    k = np.arange(length)
    angle = 2.0 * np.pi / length * (np.outer(k, k) % length)
    c, s = np.cos(angle), np.sin(angle)
    g = np.block([[c, s], [-s, c]])
    blocks = length // rows
    order = np.arange(2 * length).reshape(2, blocks, rows).transpose(1, 0, 2).reshape(-1)
    g = g[order][:, order]
    g = g.astype(np.float32)
    h = g.astype(ml_dtypes.bfloat16)
    return np.stack([h, (g - h.astype(np.float32)).astype(ml_dtypes.bfloat16)])


def body(n, m, solution, residual, sensitivity, sampling):
    _, slab, rows, cols = solution.shape
    coils = sensitivity.shape[1]
    full = n * rows
    g = jnp.asarray(matrix(full, LANES))
    vmem = pl.BlockSpec(memory_space=pltpu.VMEM)
    hbm = pl.BlockSpec(memory_space=pl.ANY)
    dma = pltpu.SemaphoreType.DMA
    chunk = (2, rows, cols)

    def f32(*shape):
        return pltpu.VMEM(shape, F32)

    def bf16(*shape):
        return pltpu.VMEM(shape, BF16)

    applied, alpha, beta = pl.pallas_call(
        functools.partial(kernel, n, m),
        out_shape=(jax.ShapeDtypeStruct(solution.shape, F32),) + 2 * (jax.ShapeDtypeStruct((1, cols), F32),),
        in_specs=5 * [hbm],
        out_specs=(vmem, vmem, vmem),
        scratch_shapes=[
            f32(*solution.shape), f32(*residual.shape), bf16(*sensitivity.shape),
            f32(coils, slab, *chunk), f32(slab, 2 * NX, *chunk), f32(n, *chunk), f32(slab, *chunk), f32(n, *chunk),
            bf16(2 * LANES, cols), bf16(2 * LANES, cols), f32(2 * full, cols), bf16(2 * full, cols), bf16(2 * full, cols),
            pltpu.VMEM(sampling.shape, sampling.dtype), bf16(*g.shape),
            f32(n, *chunk), f32(n // 2, *chunk), f32(n // 2, *chunk), f32(n // 2 // NX, NX, *chunk), f32(2, *chunk),
            f32(slab, *chunk), f32(*solution.shape), f32(slab, *chunk), f32(n // 2 // NX, *chunk),
            f32(2, *chunk), f32(8, cols), f32(8, cols), f32(*chunk), f32(*chunk), f32(8, cols), f32(8, cols),
            f32(1, LANES), f32(n, 1, LANES), f32(1, LANES), f32(m, 1, LANES),
            dma((5,)), dma((2 * NX * slab,)), dma((2 * NX * slab,)), dma((2 * NX * slab,)), dma((n,)), dma((slab,)), dma((slab,)),
            dma((slab,)), dma((n,)), dma((n // 2 // NX * NX,)), dma((n // 2,)),
            dma((n // 2,)), dma((n // 2,)), dma((n // 2,)), dma((n // 2,)), dma((n // 2 // NX,)), dma((slab,)),
            dma((5,)), dma((5,)), dma((slab,)), dma((n // 2 // NX,)), dma, dma, dma, dma,
        ],
        compiler_params=pltpu.CompilerParams(
            collective_id=0, has_side_effects=True, vmem_limit_bytes=56 * 1024 * 1024
        ),
        name="iteration",
    )(solution, residual, sensitivity, sampling, g)
    alpha, beta = alpha[0], beta[0]
    new_residual = residual - alpha * applied
    return solution + alpha * residual, new_residual, new_residual + beta * residual


def solution(mesh):
    n, m = mesh.shape["gy"], mesh.shape["gz"]
    field = P(None, "gz", "gy", None)
    return jax.shard_map(
        functools.partial(body, n, m),
        mesh=mesh,
        in_specs=(field, field, P(None, None, "gz", "gy", None), P()),
        out_specs=(field, field, field),
        check_vma=False,
    )
```

```python
import functools

import jax
import jax.numpy as jnp
import ml_dtypes
import numpy as np
from jax import lax
from jax.experimental import pallas as pl
from jax.experimental.pallas import tpu as pltpu
from jax.sharding import PartitionSpec as P

TV_EPS = 0.1
TV_WEIGHT = 0.1
TIKHONOV = 0.1
MESH = pl.DeviceIdType.MESH
F32 = jnp.float32
BF16 = jnp.bfloat16
LANES = 128
NX = 4


def split(x):
    high = x.astype(BF16)
    return high, (x - high.astype(F32)).astype(BF16)


def dot(a, b):
    return jnp.dot(a, b, preferred_element_type=F32)


def dot3(ah, al, bh, bl):
    return dot(ah, bh) + (dot(ah, bl) + dot(al, bh))


def fold(x):
    parts = [
        x[r : r + 8, c : c + LANES] for r in range(0, x.shape[0], 8) for c in range(0, x.shape[1], LANES)
    ]
    return functools.reduce(jnp.add, parts)


def total(x):
    return jnp.sum(jnp.sum(x, axis=0, keepdims=True), axis=1, keepdims=True)


def interleave(a, b):
    parts = []
    for i in range(a.shape[1] // LANES):
        parts += [a[:, i * LANES : (i + 1) * LANES], b[:, i * LANES : (i + 1) * LANES]]
    return jnp.concatenate(parts, axis=1)


def part_of(v, i):
    return jnp.concatenate([v[:, (2 * b + i) * LANES : (2 * b + i + 1) * LANES] for b in range(v.shape[1] // LANES // 2)], axis=1)


def kernel(
    n, m, sol_in, res_in, sens_in, samp_in, g_in,
    out_app, out_alpha, out_beta,
    sol, res, sens, sbuf, relay, srecv, xrel, xall, vh, vl, yacc, yh, yl, samp, g,
    part, pair, tot, gath, fin, image, smooth, local, local_in,
    hz, hy_s, hy, qz_s, qz, qy_s, qy, ps1_s, ps1, ps2_s, ps2,
    csem, xls, xlr, zs, zr, xrs, xrr, xzs, xar, ms, os,
    prs, prr, gs, gr, fs, fr, hs, hr, ls, lr, p1s, p1r, p2s, p2r,
):
    y = lax.axis_index("gy")
    w = lax.axis_index("gz")
    z, core = y // 2, lax.rem(y, 2)
    x, yy = w // NX, lax.rem(w, NX)
    nz = n // 2
    slab, rows, cols = res.shape[1:]
    sib = 1 - core
    pos = (x, yy)
    odd = lax.rem(z, 2)
    lp = (1 - odd) * x + odd * yy
    sp = z // 2
    l = 2 * lp + core
    line = 2 * NX

    def dev(j, p, z_, core_):
        return (2 * z_ + core_, NX * x + p if j else NX * p + yy)

    def on_line(p, z_, core_):
        return (2 * z_ + core_, (1 - odd) * (NX * p + yy) + odd * (NX * x + p))

    def at_y(t):
        return (t, w)

    def at_z(t):
        return (y, t)

    other = (yy, x)

    def around(t):
        return lax.rem(t + 4 * NX, NX)

    def shift(j):
        return sp + other[j] + 2 * j

    def rows_at(k):
        return around(sp - x - yy - 2 * odd - k)

    def remote(src, dst, ssem, rsem, device):
        return pltpu.make_async_remote_copy(
            src_ref=src, dst_ref=dst, send_sem=ssem, recv_sem=rsem, device_id=device, device_id_type=MESH
        )

    def loop(lo, hi, f):
        def step(i, c):
            f(i)
            return c

        lax.fori_loop(lo, hi, step, 0)

    loads = [
        pltpu.make_async_copy(a, b, csem.at[i])
        for i, (a, b) in enumerate([(sens_in, sens), (res_in, res), (sol_in, sol), (g_in, g), (samp_in, samp)])
    ]
    for c in loads:
        c.start()

    barrier = pltpu.get_barrier_semaphore()

    def hail(device):
        pl.semaphore_signal(barrier, inc=1, device_id=device, device_id_type=MESH)

    loop(1, n, lambda k: hail(at_y(lax.rem(y + k, n))))
    loop(1, m, lambda k: hail(at_z(lax.rem(w + k, m))))
    for j in range(slab):
        loop(1, NX, lambda k: hail(dev(j, lax.rem(pos[j] + k, NX), z, sib)))
        hail(dev(j, around(pos[j] - shift(j)), slab * pos[j] + j, core))

    def from_self(j):
        return jnp.logical_and(around(shift(j)) == 0, slab * pos[j] + j == z)

    def widen(c):
        for j in range(slab):
            sbuf[c, j, 0] = sens[0, c, j].astype(F32)
            sbuf[c, j, 1] = sens[1, c, j].astype(F32)

    loads[0].wait()
    loop(0, line, widen)
    loads[1].wait()

    up_y, down_y = lax.rem(y + 1, n), lax.rem(y + n - 1, n)
    up_z, down_z = lax.rem(w + 1, m), lax.rem(w + m - 1, m)
    pl.semaphore_wait(barrier, n + m - 2 + slab * NX)

    def pass_on(src, j, t):
        zt = slab * (t // 2) + j
        slot = 2 * z + lax.rem(t, 2)
        cp = remote(src, srecv.at[slot], zs.at[line * j + t], zr.at[z], dev(0, x, zt, core))
        return zt, slot, cp

    def pass_both(j, p):
        zt = slab * p + j
        both = pl.ds(2 * p, 2)
        cp = remote(relay.at[j, both], srecv.at[pl.ds(2 * z, 2)], zs.at[line * j + 2 * p], zr.at[z], dev(0, x, zt, core))
        return zt, both, cp

    def forward_maps(src, j, t):
        zt, slot, cp = pass_on(src, j, t)

        @pl.when(zt != z)
        def _():
            cp.start()

        @pl.when(zt == z)
        def _():
            srecv[slot] = src[...]

    def maps_over(j, p, c):
        t = 2 * p + c
        me = 2 * pos[j] + core
        return remote(sbuf.at[t, j], relay.at[j, me], xls.at[line * j + t], xlr.at[line * j + me], dev(j, p, z, c))

    for j in range(slab):
        t = 2 * pos[j] + core
        forward_maps(sbuf.at[t, j], j, t)
        maps_over(j, pos[j], sib).start()

    def moved(j):
        return around(shift(j)) != 0

    def res_over(j):
        return remote(res.at[:, j], xrel.at[j], xrs.at[j], xrr.at[j], dev(j, around(pos[j] - shift(j)), z, core))

    for j in range(slab):
        @pl.when(moved(j))
        def _():
            res_over(j).start()

        @pl.when(jnp.logical_not(moved(j)))
        def _():
            xrel[j] = res[:, j]

    steps = [(k, c) for k in range(NX) for c in (core, sib)]

    def hops(j, k):
        return around(shift(j) + k) != 0

    for k, c in steps:
        for j in range(slab):
            @pl.when(hops(j, k))
            def _():
                maps_over(j, around(pos[j] - shift(j) - k), c).start()

    halo1 = [
        remote(sol.at[:, 0], hz.at[0], hs.at[0], hr.at[0], at_z(down_z)),
        remote(res.at[:, 0], hz.at[1], hs.at[1], hr.at[1], at_z(down_z)),
        remote(hy_s, hy, hs.at[2], hr.at[2], at_y(down_y)),
    ]
    loads[2].wait()
    for f, field in enumerate((sol, res)):
        for p in range(2):
            for s in range(slab):
                i = f * 2 * slab + p * slab + s
                hy_s[i : i + 1, :] = field[p, s, 0:1, :]

    for h in halo1:
        h.start()

    def got_maps(j, p, c):
        t = 2 * p + c
        remote(sbuf.at[t, j], relay.at[j, t], xls.at[line * j + t], xlr.at[line * j + t], dev(j, p, z, c)).wait_recv()

    def relay_maps(j, p):
        got_maps(j, p, core)
        got_maps(j, p, sib)
        zt, both, cp = pass_both(j, p)

        @pl.when(zt != z)
        def _():
            cp.start()

        @pl.when(zt == z)
        def _():
            srecv[pl.ds(2 * z, 2)] = relay[j, both]

    for j in range(slab):
        t = 2 * pos[j] + sib
        got_maps(j, pos[j], sib)
        forward_maps(relay.at[j, t], j, t)

    def forward_res(j):
        zt = slab * around(pos[j] + shift(j)) + j
        return zt, remote(xrel.at[j], xall.at[y], xzs.at[j], xar.at[y], dev(0, x, zt, core))

    for j in range(slab):
        @pl.when(moved(j))
        def _():
            res_over(j).wait_recv()

        zt, cp = forward_res(j)

        @pl.when(zt != z)
        def _():
            cp.start()

        @pl.when(zt == z)
        def _():
            xall[y] = xrel[j]

    for k in range(NX):
        for j in range(slab):
            @pl.when(hops(j, k))
            def _():
                relay_maps(j, around(pos[j] + shift(j) + k))

    first = 2 * rows_at(0)

    def hand(slot, i, k):
        p = around(lp + k)
        return remote(xall.at[slot], xall.at[slot], ms.at[i * NX + k], xar.at[slot], on_line(p, z, core))

    def to_other(zz):
        slot = 2 * zz + core
        return remote(xall.at[slot], xall.at[slot], os.at[zz], xar.at[slot], on_line(lp, z, sib))

    for i in range(nz // NX):
        zz = first + i
        slot = 2 * zz + core

        @pl.when(zz != z)
        def _():
            remote(xrel.at[0], xall.at[slot], xzs.at[0], xar.at[slot], dev(0, x, zz, core)).wait_recv()

        for k in range(1, NX):
            hand(slot, i, k).start()
        to_other(zz).start()

    for h in halo1:
        h.wait_recv()
    row = lax.broadcasted_iota(jnp.int32, (rows, cols), 0)
    col = lax.broadcasted_iota(jnp.int32, (rows, cols), 1)
    keep_y = jnp.logical_or(row < rows - 1, y < n - 1)
    keep_z = jnp.full((rows, cols), w, jnp.int32) < m - 1

    def ahead(f, field, p, s):
        v = field[p, s]
        dx = jnp.where(col == cols - 1, 0.0, pltpu.roll(v, cols - 1, 1) - v)
        i = f * 2 * slab + p * slab + s
        nxt = jnp.where(row == rows - 1, jnp.broadcast_to(hy[i : i + 1, :], (rows, cols)), pltpu.roll(v, rows - 1, 0))
        dy = jnp.where(keep_y, nxt - v, 0.0)
        if s + 1 < slab:
            dz = field[p, s + 1] - v
        else:
            dz = jnp.where(keep_z, hz[f, p] - v, 0.0)
        return dx, dy, dz

    qy_s[...] = jnp.zeros_like(qy_s)
    for s in range(slab):
        sq = jnp.zeros((rows, cols), F32)
        for p in range(2):
            for d in ahead(0, sol, p, s):
                sq = sq + d * d
        weight = 1.0 / jnp.sqrt(sq + TV_EPS * TV_EPS)
        for p in range(2):
            dx, dy, dz = (weight * d for d in ahead(1, res, p, s))
            before_x = jnp.where(col == 0, 0.0, pltpu.roll(dx, 1, 1))
            before_y = jnp.where(row == 0, 0.0, pltpu.roll(dy, 1, 0))
            here = (before_x - dx) + (before_y - dy) - dz
            if s > 0:
                here = here + qz_s[p]
            smooth[p, s] = here
            qz_s[p] = dz
            i = p * slab + s
            qy_s[i : i + 1, :] = dy[rows - 1 : rows, :]
    halo2 = [
        remote(qz_s, qz, hs.at[3], hr.at[3], at_z(up_z)),
        remote(qy_s, qy, hs.at[4], hr.at[4], at_y(up_y)),
    ]
    for h in halo2:
        h.start()

    for k in range(1, NX):
        for i in range(nz // NX):
            zz = 2 * rows_at(k) + i
            slot = 2 * zz + core
            remote(xall.at[slot], xall.at[slot], ms.at[0], xar.at[slot], on_line(around(lp + k), z, core)).wait_recv()
            to_other(zz).start()

    per = 4
    tile = per * rows
    groups = n // per

    def ready(zz):
        @pl.when(zz != z)
        def _():
            both = srecv.at[pl.ds(2 * zz, 2)]
            remote(relay.at[0, pl.ds(0, 2)], both, zs.at[0], zr.at[zz], dev(0, x, zz, core)).wait_recv()

        s = 2 * zz + sib
        remote(xall.at[s], xall.at[s], os.at[0], xar.at[s], on_line(lp, z, sib)).wait_recv()

    at_zero = jnp.full((rows, cols), w, jnp.int32) > 0
    at_top = jnp.logical_and(row == 0, y > 0)

    def local_over(j):
        there = dev(j, around(pos[j] - shift(j)), slab * pos[j] + j, core)
        return remote(local.at[j], local_in.at[odd], ls.at[j], lr.at[odd], there)

    def send_local():
        for h in halo2:
            h.wait_recv()
        for p in range(2):
            for s in range(slab):
                i = p * slab + s
                v = smooth[p, s] + jnp.where(at_top, jnp.broadcast_to(qy[i : i + 1, :], (rows, cols)), 0.0)
                if s == 0:
                    v = v + jnp.where(at_zero, qz[p], 0.0)
                local[s, p] = TIKHONOV * res[p, s] - TV_WEIGHT * v
        for j in range(slab):
            @pl.when(jnp.logical_not(from_self(j)))
            def _():
                local_over(j).start()

            @pl.when(from_self(j))
            def _():
                local_in[odd] = local[j]

    full = n * rows
    scale = 1.0 / (full * cols)
    yacc[...] = jnp.zeros_like(yacc)
    loads[3].wait()
    loads[4].wait()

    def forward(i):
        q = rows_at(i)
        last = i == groups - 1

        @pl.when(last)
        def _():
            send_local()

        for t in range(per // 2):
            ready(q * per // 2 + t)
        block = []
        for t in range(per):
            sr, si = srecv[q * per + t, 0], srecv[q * per + t, 1]
            xr, xi = xall[q * per + t, 0], xall[q * per + t, 1]
            block.append(interleave(sr * xr - si * xi, -(sr * xi + si * xr)))
        ah, al = split(jnp.concatenate(block, axis=0))
        v = dot3(ah, al, g[0], g[1])
        vh[:tile], vl[:tile] = split(part_of(v, 0))
        vh[tile:], vl[tile:] = split(-part_of(v, 1))

        def rows_tile(t):
            at = pl.ds(pl.multiple_of(2 * t * tile, 2 * tile), 2 * tile)
            k = pl.ds(pl.multiple_of(2 * q * tile, 2 * tile), 2 * tile)
            v = yacc[at] + dot3(g[0, at, k], g[1, at, k], vh[...], vl[...])

            @pl.when(jnp.logical_not(last))
            def _():
                yacc[at] = v

            @pl.when(last)
            def _():
                taken = samp[pl.ds(pl.multiple_of(t * tile, tile), tile)].astype(F32) * scale
                yh[at], yl[at] = split(v * jnp.concatenate([taken, -taken], axis=0))

        loop(0, groups, rows_tile)

    loop(0, groups, forward)

    def to_sib(zz):
        return remote(part.at[2 * zz + sib], pair.at[zz], prs.at[zz], prr.at[zz], on_line(lp, z, sib))

    def to_adder(zz):
        t = around(lp + rows_at(0) - zz // 2)
        i = lax.rem(zz, 2)
        return t, remote(tot.at[zz], gath.at[i, lp], gs.at[zz], gr.at[NX * i + lp], on_line(t, z, core))

    def add_pair(zz):
        to_sib(zz).wait_recv()
        tot[zz] = part[2 * zz + core] + pair[zz]
        t, cp = to_adder(zz)

        @pl.when(t != lp)
        def _():
            cp.start()

    def home(i):
        zz = first + i
        return zz, remote(fin.at[i], image.at[odd], fs.at[i], fr.at[odd], on_line(sp, zz, core))

    def add_line(i, sums):
        zz = first + i
        v = tot[zz]
        for k in range(1, NX):
            t = around(lp + k)
            remote(tot.at[zz], gath.at[i, t], gs.at[zz], gr.at[NX * i + t], on_line(t, z, core)).wait_recv()
            v = v + gath[i, t]

        @pl.when(jnp.logical_not(jnp.logical_and(sp == lp, zz == z)))
        def _():
            remote(local.at[0], local_in.at[i], ls.at[0], lr.at[i], on_line(sp, zz, core)).wait_recv()

        v = v + local_in[i]
        for p in range(2):
            a, r = v[p], xall[2 * zz + core, p]
            for k, term in enumerate((r * r, r * a, a * a)):
                sums[k] = sums[k] + fold(term)
        here = jnp.logical_and(sp == lp, zz == z)

        @pl.when(here)
        def _():
            image[odd] = v

        @pl.when(jnp.logical_not(here))
        def _():
            fin[i] = v

    def block_at(i):
        return rows_at(2 - i + (i // 2) * (2 * i - 1) - (i // 3) * 4)

    def inverse(i):
        q = block_at(i)
        at = pl.ds(pl.multiple_of(2 * q * tile, 2 * tile), 2 * tile)
        v = dot3(g[0, at], g[1, at], yh[...], yl[...])
        ah, al = split(interleave(v[:tile], -v[tile:]))
        v = dot3(ah, al, g[0], g[1])
        re, im = part_of(v, 0), part_of(v, 1)
        for t in range(per):
            s = q * per + t
            vr, vi = re[t * rows : (t + 1) * rows], im[t * rows : (t + 1) * rows]
            sr, si = srecv[s, 0], srecv[s, 1]
            part[s, 0] = sr * vr + si * vi
            part[s, 1] = sr * vi - si * vr
        for t in range(per // 2):
            to_sib(q * per // 2 + t).start()

        @pl.when(i > 0)
        def _():
            for t in range(per // 2):
                add_pair(block_at(i - 1) * per // 2 + t)

    loop(0, groups, inverse)
    for t in range(per // 2):
        add_pair(first + t)
    sums = [jnp.zeros((8, LANES), F32) for _ in range(3)]
    for i in range(nz // NX):
        add_line(i, sums)
    sums = [total(v) for v in sums]
    lane = lax.broadcasted_iota(jnp.int32, (1, LANES), 1)
    ps1_s[...] = jnp.where(lane == 0, sums[0], jnp.where(lane == 1, sums[1], sums[2]))

    def start_home():
        for i in range(nz // NX):
            zz, cp = home(i)

            @pl.when(jnp.logical_not(jnp.logical_and(sp == lp, zz == z)))
            def _():
                cp.start()

    def wait_home():
        for i in range(nz // NX):
            zz, cp = home(i)

            @pl.when(jnp.logical_not(jnp.logical_and(sp == lp, zz == z)))
            def _():
                cp.wait_send()

    def wait_sends():
        for h in halo1 + halo2:
            h.wait_send()
        for j in range(slab):
            @pl.when(moved(j))
            def _():
                res_over(j).wait_send()

            @pl.when(jnp.logical_not(from_self(j)))
            def _():
                local_over(j).wait_send()

            maps_over(j, pos[j], sib).wait_send()
            for k, c in steps:
                @pl.when(hops(j, k))
                def _():
                    maps_over(j, around(pos[j] - shift(j) - k), c).wait_send()

            for c in (core, sib):
                zt, _, cp = pass_on(sbuf.at[0, j], j, 2 * pos[j] + c)

                @pl.when(zt != z)
                def _():
                    cp.wait_send()

            for k in range(1, NX):
                zt, _, cp = pass_both(j, around(pos[j] + k))

                @pl.when(zt != z)
                def _():
                    cp.wait_send()

            zt, cp = forward_res(j)

            @pl.when(zt != z)
            def _():
                cp.wait_send()

        for i in range(nz // NX):
            for k in range(1, NX):
                hand(2 * (first + i) + core, i, k).wait_send()

        def sent_sums(zz):
            to_other(zz).wait_send()
            to_sib(zz).wait_send()
            t, cp = to_adder(zz)

            @pl.when(t != lp)
            def _():
                cp.wait_send()

        loop(0, nz, sent_sums)

    def exchange(send, recv, ssem, rsem, me, size, where, targets, meanwhile):
        recv[me] = send[...]

        for t in targets:
            remote(send, recv.at[me], ssem, rsem, where(t)).start()

        for f in meanwhile:
            f()
        others = recv.at[pl.ds(0, size - 1)]
        remote(others, others, ssem, rsem, where(lax.rem(me + 1, size))).wait_recv()
        return functools.reduce(jnp.add, [recv[i] for i in range(size)])

    over_z = [2 * lax.rem(z + d, nz) + c for d in (4, 3, 5, 2, 6, 1, 7) for c in (sib, core)] + [2 * z + sib]
    ways = sorted(((a, b) for a in range(NX) for b in range(NX)), key=lambda d: -min(d[0], NX - d[0]) - min(d[1], NX - d[1]))
    over_xy = [NX * around(x + a) + around(yy + b) for a, b in ways[:-1]]
    ps2_s[...] = exchange(ps1_s, ps1, p1s, p1r, y, n, at_y, over_z, (start_home, wait_sends))
    sums = exchange(ps2_s, ps2, p2s, p2r, w, m, at_z, over_xy, (wait_home,))
    norm_old, curvature, applied2 = sums[:, 0:1], sums[:, 1:2], sums[:, 2:3]
    alpha = norm_old / curvature
    norm_new = jnp.maximum(alpha * alpha * applied2 - norm_old, 0.0)
    out_alpha[...] = jnp.broadcast_to(alpha, (1, cols))
    out_beta[...] = jnp.broadcast_to(norm_new / norm_old, (1, cols))

    for s in range(slab):
        @pl.when(jnp.logical_not(from_self(s)))
        def _():
            remote(fin.at[0], image.at[s], fs.at[0], fr.at[s], dev(s, around(pos[s] - shift(s)), slab * pos[s] + s, core)).wait_recv()

        for p in range(2):
            out_app[p, s] = image[s, p]

    for recv, ssem, rsem, size, there in ((ps1, p1s, p1r, n, at_y(up_y)), (ps2, p2s, p2r, m, at_z(up_z))):
        others = recv.at[pl.ds(0, size - 1)]
        remote(others, others, ssem, rsem, there).wait_send()


def matrix(length, rows):
    k = np.arange(length)
    angle = 2.0 * np.pi / length * (np.outer(k, k) % length)
    c, s = np.cos(angle), np.sin(angle)
    g = np.block([[c, s], [-s, c]])
    blocks = length // rows
    order = np.arange(2 * length).reshape(2, blocks, rows).transpose(1, 0, 2).reshape(-1)
    g = g[order][:, order]
    g = g.astype(np.float32)
    h = g.astype(ml_dtypes.bfloat16)
    return np.stack([h, (g - h.astype(np.float32)).astype(ml_dtypes.bfloat16)])


def body(n, m, solution, residual, sensitivity, sampling):
    _, slab, rows, cols = solution.shape
    coils = sensitivity.shape[1]
    full = n * rows
    g = jnp.asarray(matrix(full, LANES))
    vmem = pl.BlockSpec(memory_space=pltpu.VMEM)
    hbm = pl.BlockSpec(memory_space=pl.ANY)
    dma = pltpu.SemaphoreType.DMA
    chunk = (2, rows, cols)

    def f32(*shape):
        return pltpu.VMEM(shape, F32)

    def bf16(*shape):
        return pltpu.VMEM(shape, BF16)

    applied, alpha, beta = pl.pallas_call(
        functools.partial(kernel, n, m),
        out_shape=(jax.ShapeDtypeStruct(solution.shape, F32),) + 2 * (jax.ShapeDtypeStruct((1, cols), F32),),
        in_specs=5 * [hbm],
        out_specs=(vmem, vmem, vmem),
        scratch_shapes=[
            f32(*solution.shape), f32(*residual.shape), bf16(*sensitivity.shape),
            f32(coils, slab, *chunk), f32(slab, 2 * NX, *chunk), f32(n, *chunk), f32(slab, *chunk), f32(n, *chunk),
            bf16(2 * LANES, cols), bf16(2 * LANES, cols), f32(2 * full, cols), bf16(2 * full, cols), bf16(2 * full, cols),
            pltpu.VMEM(sampling.shape, sampling.dtype), bf16(*g.shape),
            f32(n, *chunk), f32(n // 2, *chunk), f32(n // 2, *chunk), f32(n // 2 // NX, NX, *chunk), f32(2, *chunk),
            f32(slab, *chunk), f32(*solution.shape), f32(slab, *chunk), f32(n // 2 // NX, *chunk),
            f32(2, *chunk), f32(8, cols), f32(8, cols), f32(*chunk), f32(*chunk), f32(8, cols), f32(8, cols),
            f32(1, LANES), f32(n, 1, LANES), f32(1, LANES), f32(m, 1, LANES),
            dma((5,)), dma((2 * NX * slab,)), dma((2 * NX * slab,)), dma((2 * NX * slab,)), dma((n // 2,)), dma((slab,)), dma((slab,)),
            dma((slab,)), dma((n,)), dma((n // 2 // NX * NX,)), dma((n // 2,)),
            dma((n // 2,)), dma((n // 2,)), dma((n // 2,)), dma((n // 2,)), dma((n // 2 // NX,)), dma((slab,)),
            dma((5,)), dma((5,)), dma((slab,)), dma((n // 2 // NX,)), dma, dma, dma, dma,
        ],
        compiler_params=pltpu.CompilerParams(
            collective_id=0, has_side_effects=True, vmem_limit_bytes=56 * 1024 * 1024
        ),
        name="iteration",
    )(solution, residual, sensitivity, sampling, g)
    alpha, beta = alpha[0], beta[0]
    new_residual = residual - alpha * applied
    return solution + alpha * residual, new_residual, new_residual + beta * residual


def solution(mesh):
    n, m = mesh.shape["gy"], mesh.shape["gz"]
    field = P(None, "gz", "gy", None)
    return jax.shard_map(
        functools.partial(body, n, m),
        mesh=mesh,
        in_specs=(field, field, P(None, None, "gz", "gy", None), P()),
        out_specs=(field, field, field),
        check_vma=False,
    )
```

```python
import functools

import jax
import jax.numpy as jnp
import ml_dtypes
import numpy as np
from jax import lax
from jax.experimental import pallas as pl
from jax.experimental.pallas import tpu as pltpu
from jax.sharding import PartitionSpec as P

TV_EPS = 0.1
TV_WEIGHT = 0.1
TIKHONOV = 0.1
MESH = pl.DeviceIdType.MESH
F32 = jnp.float32
BF16 = jnp.bfloat16
LANES = 128
NX = 4


def split(x):
    high = x.astype(BF16)
    return high, (x - high.astype(F32)).astype(BF16)


def dot(a, b):
    return jnp.dot(a, b, preferred_element_type=F32)


def dot3(ah, al, bh, bl):
    return dot(ah, bh) + (dot(ah, bl) + dot(al, bh))


def fold(x):
    parts = [
        x[r : r + 8, c : c + LANES] for r in range(0, x.shape[0], 8) for c in range(0, x.shape[1], LANES)
    ]
    return functools.reduce(jnp.add, parts)


def total(x):
    return jnp.sum(jnp.sum(x, axis=0, keepdims=True), axis=1, keepdims=True)


def interleave(a, b):
    parts = []
    for i in range(a.shape[1] // LANES):
        parts += [a[:, i * LANES : (i + 1) * LANES], b[:, i * LANES : (i + 1) * LANES]]
    return jnp.concatenate(parts, axis=1)


def part_of(v, i):
    return jnp.concatenate([v[:, (2 * b + i) * LANES : (2 * b + i + 1) * LANES] for b in range(v.shape[1] // LANES // 2)], axis=1)


def kernel(
    n, m, sol_in, res_in, sens_in, samp_in, g_in,
    out_app, out_alpha, out_beta,
    sol, res, sens, sbuf, relay, srecv, xrel, xall, vh, vl, yacc, yh, yl, samp, g,
    part, pair, tot, gath, fin, smooth, local, local_in,
    hz, hy_s, hy, qz_s, qz, qy_s, qy, ps1_s, ps1, ps2_s, ps2,
    csem, xls, xlr, zs, zr, xrs, xrr, xzs, xar, ms, os,
    prs, prr, gs, gr, fs, fr, hs, hr, ls, lr, p1s, p1r, p2s, p2r,
):
    y = lax.axis_index("gy")
    w = lax.axis_index("gz")
    z, core = y // 2, lax.rem(y, 2)
    x, yy = w // NX, lax.rem(w, NX)
    nz = n // 2
    slab, rows, cols = res.shape[1:]
    sib = 1 - core
    pos = (x, yy)
    odd = lax.rem(z, 2)
    lp = (1 - odd) * x + odd * yy
    sp = z // 2
    l = 2 * lp + core
    line = 2 * NX

    def dev(j, p, z_, core_):
        return (2 * z_ + core_, NX * x + p if j else NX * p + yy)

    def on_line(p, z_, core_):
        return (2 * z_ + core_, (1 - odd) * (NX * p + yy) + odd * (NX * x + p))

    def at_y(t):
        return (t, w)

    def at_z(t):
        return (y, t)

    other = (yy, x)

    def around(t):
        return lax.rem(t + 4 * NX, NX)

    def shift(j):
        return sp + other[j] + 2 * j

    def rows_at(k):
        return around(sp - x - yy - 2 * odd - k)

    def remote(src, dst, ssem, rsem, device):
        return pltpu.make_async_remote_copy(
            src_ref=src, dst_ref=dst, send_sem=ssem, recv_sem=rsem, device_id=device, device_id_type=MESH
        )

    def loop(lo, hi, f):
        def step(i, c):
            f(i)
            return c

        lax.fori_loop(lo, hi, step, 0)

    loads = [
        pltpu.make_async_copy(a, b, csem.at[i])
        for i, (a, b) in enumerate([(sens_in, sens), (res_in, res), (sol_in, sol), (g_in, g), (samp_in, samp)])
    ]
    for c in loads:
        c.start()

    barrier = pltpu.get_barrier_semaphore()

    def hail(device):
        pl.semaphore_signal(barrier, inc=1, device_id=device, device_id_type=MESH)

    loop(1, n, lambda k: hail(at_y(lax.rem(y + k, n))))
    loop(1, m, lambda k: hail(at_z(lax.rem(w + k, m))))
    for j in range(slab):
        loop(1, NX, lambda k: hail(dev(j, lax.rem(pos[j] + k, NX), z, sib)))
        hail(dev(j, around(pos[j] - shift(j)), slab * pos[j] + j, core))

    def from_self(j):
        return jnp.logical_and(around(shift(j)) == 0, slab * pos[j] + j == z)

    def widen(c):
        for j in range(slab):
            sbuf[c, j, 0] = sens[0, c, j].astype(F32)
            sbuf[c, j, 1] = sens[1, c, j].astype(F32)

    loads[0].wait()
    loop(0, line, widen)
    loads[1].wait()

    up_y, down_y = lax.rem(y + 1, n), lax.rem(y + n - 1, n)
    up_z, down_z = lax.rem(w + 1, m), lax.rem(w + m - 1, m)
    pl.semaphore_wait(barrier, n + m - 2 + slab * NX)

    def pass_on(src, j, t):
        zt = slab * (t // 2) + j
        slot = 2 * z + lax.rem(t, 2)
        cp = remote(src, srecv.at[slot], zs.at[line * j + t], zr.at[z], dev(0, x, zt, core))
        return zt, slot, cp

    def pass_both(j, p):
        zt = slab * p + j
        both = pl.ds(2 * p, 2)
        cp = remote(relay.at[j, both], srecv.at[pl.ds(2 * z, 2)], zs.at[line * j + 2 * p], zr.at[z], dev(0, x, zt, core))
        return zt, both, cp

    def forward_maps(src, j, t):
        zt, slot, cp = pass_on(src, j, t)

        @pl.when(zt != z)
        def _():
            cp.start()

        @pl.when(zt == z)
        def _():
            srecv[slot] = src[...]

    def maps_over(j, p, c):
        t = 2 * p + c
        me = 2 * pos[j] + core
        return remote(sbuf.at[t, j], relay.at[j, me], xls.at[line * j + t], xlr.at[line * j + me], dev(j, p, z, c))

    for j in range(slab):
        t = 2 * pos[j] + core
        forward_maps(sbuf.at[t, j], j, t)
        maps_over(j, pos[j], sib).start()

    def moved(j):
        return around(shift(j)) != 0

    def res_over(j):
        return remote(res.at[:, j], xrel.at[j], xrs.at[j], xrr.at[j], dev(j, around(pos[j] - shift(j)), z, core))

    for j in range(slab):
        @pl.when(moved(j))
        def _():
            res_over(j).start()

        @pl.when(jnp.logical_not(moved(j)))
        def _():
            xrel[j] = res[:, j]

    steps = [(k, c) for k in range(NX) for c in (core, sib)]

    def hops(j, k):
        return around(shift(j) + k) != 0

    for k, c in steps:
        for j in range(slab):
            @pl.when(hops(j, k))
            def _():
                maps_over(j, around(pos[j] - shift(j) - k), c).start()

    halo1 = [
        remote(sol.at[:, 0], hz.at[0], hs.at[0], hr.at[0], at_z(down_z)),
        remote(res.at[:, 0], hz.at[1], hs.at[1], hr.at[1], at_z(down_z)),
        remote(hy_s, hy, hs.at[2], hr.at[2], at_y(down_y)),
    ]
    loads[2].wait()
    for f, field in enumerate((sol, res)):
        for p in range(2):
            for s in range(slab):
                i = f * 2 * slab + p * slab + s
                hy_s[i : i + 1, :] = field[p, s, 0:1, :]

    for h in halo1:
        h.start()

    def got_maps(j, p, c):
        t = 2 * p + c
        remote(sbuf.at[t, j], relay.at[j, t], xls.at[line * j + t], xlr.at[line * j + t], dev(j, p, z, c)).wait_recv()

    def relay_maps(j, p):
        got_maps(j, p, core)
        got_maps(j, p, sib)
        zt, both, cp = pass_both(j, p)

        @pl.when(zt != z)
        def _():
            cp.start()

        @pl.when(zt == z)
        def _():
            srecv[pl.ds(2 * z, 2)] = relay[j, both]

    for j in range(slab):
        t = 2 * pos[j] + sib
        got_maps(j, pos[j], sib)
        forward_maps(relay.at[j, t], j, t)

    def forward_res(j):
        zt = slab * around(pos[j] + shift(j)) + j
        return zt, remote(xrel.at[j], xall.at[y], xzs.at[j], xar.at[y], dev(0, x, zt, core))

    for j in range(slab):
        @pl.when(moved(j))
        def _():
            res_over(j).wait_recv()

        zt, cp = forward_res(j)

        @pl.when(zt != z)
        def _():
            cp.start()

        @pl.when(zt == z)
        def _():
            xall[y] = xrel[j]

    for k in range(NX):
        for j in range(slab):
            @pl.when(hops(j, k))
            def _():
                relay_maps(j, around(pos[j] + shift(j) + k))

    for h in halo1:
        h.wait_recv()
    row = lax.broadcasted_iota(jnp.int32, (rows, cols), 0)
    col = lax.broadcasted_iota(jnp.int32, (rows, cols), 1)
    keep_y = jnp.logical_or(row < rows - 1, y < n - 1)
    keep_z = jnp.full((rows, cols), w, jnp.int32) < m - 1

    def ahead(f, field, p, s):
        v = field[p, s]
        dx = jnp.where(col == cols - 1, 0.0, pltpu.roll(v, cols - 1, 1) - v)
        i = f * 2 * slab + p * slab + s
        nxt = jnp.where(row == rows - 1, jnp.broadcast_to(hy[i : i + 1, :], (rows, cols)), pltpu.roll(v, rows - 1, 0))
        dy = jnp.where(keep_y, nxt - v, 0.0)
        if s + 1 < slab:
            dz = field[p, s + 1] - v
        else:
            dz = jnp.where(keep_z, hz[f, p] - v, 0.0)
        return dx, dy, dz

    qy_s[...] = jnp.zeros_like(qy_s)
    for s in range(slab):
        sq = jnp.zeros((rows, cols), F32)
        for p in range(2):
            for d in ahead(0, sol, p, s):
                sq = sq + d * d
        weight = 1.0 / jnp.sqrt(sq + TV_EPS * TV_EPS)
        for p in range(2):
            dx, dy, dz = (weight * d for d in ahead(1, res, p, s))
            before_x = jnp.where(col == 0, 0.0, pltpu.roll(dx, 1, 1))
            before_y = jnp.where(row == 0, 0.0, pltpu.roll(dy, 1, 0))
            here = (before_x - dx) + (before_y - dy) - dz
            if s > 0:
                here = here + qz_s[p]
            smooth[p, s] = here
            qz_s[p] = dz
            i = p * slab + s
            qy_s[i : i + 1, :] = dy[rows - 1 : rows, :]
    halo2 = [
        remote(qz_s, qz, hs.at[3], hr.at[3], at_z(up_z)),
        remote(qy_s, qy, hs.at[4], hr.at[4], at_y(up_y)),
    ]
    for h in halo2:
        h.start()

    first = 2 * rows_at(0)

    def hand(slot, i, k):
        p = around(lp + k)
        return remote(xall.at[slot], xall.at[slot], ms.at[i * NX + k], xar.at[slot], on_line(p, z, core))

    def to_other(zz):
        slot = 2 * zz + core
        return remote(xall.at[slot], xall.at[slot], os.at[zz], xar.at[slot], on_line(lp, z, sib))

    for i in range(nz // NX):
        zz = first + i
        slot = 2 * zz + core

        @pl.when(zz != z)
        def _():
            remote(xrel.at[0], xall.at[slot], xzs.at[0], xar.at[slot], dev(0, x, zz, core)).wait_recv()

        for k in range(1, NX):
            hand(slot, i, k).start()
        to_other(zz).start()

    for k in range(1, NX):
        for i in range(nz // NX):
            zz = 2 * rows_at(k) + i
            slot = 2 * zz + core
            remote(xall.at[slot], xall.at[slot], ms.at[0], xar.at[slot], on_line(around(lp + k), z, core)).wait_recv()
            to_other(zz).start()

    per = 4
    tile = per * rows
    groups = n // per

    def ready(zz):
        @pl.when(zz != z)
        def _():
            both = srecv.at[pl.ds(2 * zz, 2)]
            remote(relay.at[0, pl.ds(0, 2)], both, zs.at[0], zr.at[zz], dev(0, x, zz, core)).wait_recv()

        s = 2 * zz + sib
        remote(xall.at[s], xall.at[s], os.at[0], xar.at[s], on_line(lp, z, sib)).wait_recv()

    at_zero = jnp.full((rows, cols), w, jnp.int32) > 0
    at_top = jnp.logical_and(row == 0, y > 0)

    def local_over(j):
        there = dev(j, around(pos[j] - shift(j)), slab * pos[j] + j, core)
        return remote(local.at[j], local_in.at[odd], ls.at[j], lr.at[odd], there)

    def send_local():
        for h in halo2:
            h.wait_recv()
        for p in range(2):
            for s in range(slab):
                i = p * slab + s
                v = smooth[p, s] + jnp.where(at_top, jnp.broadcast_to(qy[i : i + 1, :], (rows, cols)), 0.0)
                if s == 0:
                    v = v + jnp.where(at_zero, qz[p], 0.0)
                local[s, p] = TIKHONOV * res[p, s] - TV_WEIGHT * v
        for j in range(slab):
            @pl.when(jnp.logical_not(from_self(j)))
            def _():
                local_over(j).start()

            @pl.when(from_self(j))
            def _():
                local_in[odd] = local[j]

    full = n * rows
    scale = 1.0 / (full * cols)
    yacc[...] = jnp.zeros_like(yacc)
    loads[3].wait()
    loads[4].wait()

    def forward(i):
        q = rows_at(i)
        last = i == groups - 1

        @pl.when(last)
        def _():
            send_local()

        for t in range(per // 2):
            ready(q * per // 2 + t)
        block = []
        for t in range(per):
            sr, si = srecv[q * per + t, 0], srecv[q * per + t, 1]
            xr, xi = xall[q * per + t, 0], xall[q * per + t, 1]
            block.append(interleave(sr * xr - si * xi, -(sr * xi + si * xr)))
        ah, al = split(jnp.concatenate(block, axis=0))
        v = dot3(ah, al, g[0], g[1])
        vh[:tile], vl[:tile] = split(part_of(v, 0))
        vh[tile:], vl[tile:] = split(-part_of(v, 1))

        def rows_tile(t):
            at = pl.ds(pl.multiple_of(2 * t * tile, 2 * tile), 2 * tile)
            k = pl.ds(pl.multiple_of(2 * q * tile, 2 * tile), 2 * tile)
            v = yacc[at] + dot3(g[0, at, k], g[1, at, k], vh[...], vl[...])

            @pl.when(jnp.logical_not(last))
            def _():
                yacc[at] = v

            @pl.when(last)
            def _():
                taken = samp[pl.ds(pl.multiple_of(t * tile, tile), tile)].astype(F32) * scale
                yh[at], yl[at] = split(v * jnp.concatenate([taken, -taken], axis=0))

        loop(0, groups, rows_tile)

    loop(0, groups, forward)

    def to_sib(zz):
        return remote(part.at[2 * zz + sib], pair.at[zz], prs.at[zz], prr.at[zz], on_line(lp, z, sib))

    def to_adder(zz):
        t = around(lp + rows_at(0) - zz // 2)
        i = lax.rem(zz, 2)
        return t, remote(tot.at[zz], gath.at[i, lp], gs.at[zz], gr.at[NX * i + lp], on_line(t, z, core))

    def add_pair(zz):
        to_sib(zz).wait_recv()
        tot[zz] = part[2 * zz + core] + pair[zz]
        t, cp = to_adder(zz)

        @pl.when(t != lp)
        def _():
            cp.start()

    def home(i):
        zz = first + i
        return zz, remote(fin.at[i], out_app.at[:, odd], fs.at[i], fr.at[odd], on_line(sp, zz, core))

    def add_line(i, sums):
        zz = first + i
        v = tot[zz]
        for k in range(1, NX):
            t = around(lp + k)
            remote(tot.at[zz], gath.at[i, t], gs.at[zz], gr.at[NX * i + t], on_line(t, z, core)).wait_recv()
            v = v + gath[i, t]

        @pl.when(jnp.logical_not(jnp.logical_and(sp == lp, zz == z)))
        def _():
            remote(local.at[0], local_in.at[i], ls.at[0], lr.at[i], on_line(sp, zz, core)).wait_recv()

        v = v + local_in[i]
        for p in range(2):
            a, r = v[p], xall[2 * zz + core, p]
            for k, term in enumerate((r * r, r * a, a * a)):
                sums[k] = sums[k] + fold(term)
        fin[i] = v

    def block_at(i):
        return rows_at(2 - i + (i // 2) * (2 * i - 1) - (i // 3) * 4)

    def inverse(i):
        q = block_at(i)
        at = pl.ds(pl.multiple_of(2 * q * tile, 2 * tile), 2 * tile)
        v = dot3(g[0, at], g[1, at], yh[...], yl[...])
        ah, al = split(interleave(v[:tile], -v[tile:]))
        v = dot3(ah, al, g[0], g[1])
        re, im = part_of(v, 0), part_of(v, 1)
        for t in range(per):
            s = q * per + t
            vr, vi = re[t * rows : (t + 1) * rows], im[t * rows : (t + 1) * rows]
            sr, si = srecv[s, 0], srecv[s, 1]
            part[s, 0] = sr * vr + si * vi
            part[s, 1] = sr * vi - si * vr
        for t in range(per // 2):
            to_sib(q * per // 2 + t).start()

        @pl.when(i > 0)
        def _():
            for t in range(per // 2):
                add_pair(block_at(i - 1) * per // 2 + t)

    loop(0, groups, inverse)
    for t in range(per // 2):
        add_pair(first + t)
    sums = [jnp.zeros((8, LANES), F32) for _ in range(3)]
    for i in range(nz // NX):
        add_line(i, sums)
    sums = [total(v) for v in sums]
    lane = lax.broadcasted_iota(jnp.int32, (1, LANES), 1)
    ps1_s[...] = jnp.where(lane == 0, sums[0], jnp.where(lane == 1, sums[1], sums[2]))

    def stay(i):
        return pltpu.make_async_copy(fin.at[i], out_app.at[:, odd], csem.at[0])

    def start_home():
        for i in range(nz // NX):
            zz, cp = home(i)

            @pl.when(jnp.logical_not(jnp.logical_and(sp == lp, zz == z)))
            def _():
                cp.start()

            @pl.when(jnp.logical_and(sp == lp, zz == z))
            def _():
                stay(i).start()

    def wait_home():
        for i in range(nz // NX):
            zz, cp = home(i)

            @pl.when(jnp.logical_not(jnp.logical_and(sp == lp, zz == z)))
            def _():
                cp.wait_send()

            @pl.when(jnp.logical_and(sp == lp, zz == z))
            def _():
                stay(i).wait()

    def wait_sends():
        for h in halo1 + halo2:
            h.wait_send()
        for j in range(slab):
            @pl.when(moved(j))
            def _():
                res_over(j).wait_send()

            @pl.when(jnp.logical_not(from_self(j)))
            def _():
                local_over(j).wait_send()

            maps_over(j, pos[j], sib).wait_send()
            for k, c in steps:
                @pl.when(hops(j, k))
                def _():
                    maps_over(j, around(pos[j] - shift(j) - k), c).wait_send()

            for c in (core, sib):
                zt, _, cp = pass_on(sbuf.at[0, j], j, 2 * pos[j] + c)

                @pl.when(zt != z)
                def _():
                    cp.wait_send()

            for k in range(1, NX):
                zt, _, cp = pass_both(j, around(pos[j] + k))

                @pl.when(zt != z)
                def _():
                    cp.wait_send()

            zt, cp = forward_res(j)

            @pl.when(zt != z)
            def _():
                cp.wait_send()

        for i in range(nz // NX):
            for k in range(1, NX):
                hand(2 * (first + i) + core, i, k).wait_send()

        def sent_sums(zz):
            to_other(zz).wait_send()
            to_sib(zz).wait_send()
            t, cp = to_adder(zz)

            @pl.when(t != lp)
            def _():
                cp.wait_send()

        loop(0, nz, sent_sums)

    def exchange(send, recv, ssem, rsem, me, size, where, targets, meanwhile):
        recv[me] = send[...]

        for t in targets:
            remote(send, recv.at[me], ssem, rsem, where(t)).start()

        for f in meanwhile:
            f()
        others = recv.at[pl.ds(0, size - 1)]
        remote(others, others, ssem, rsem, where(lax.rem(me + 1, size))).wait_recv()
        return functools.reduce(jnp.add, [recv[i] for i in range(size)])

    over_z = [2 * lax.rem(z + d, nz) + c for d in (4, 3, 5, 2, 6, 1, 7) for c in (sib, core)] + [2 * z + sib]
    ways = sorted(((a, b) for a in range(NX) for b in range(NX)), key=lambda d: -min(d[0], NX - d[0]) - min(d[1], NX - d[1]))
    over_xy = [NX * around(x + a) + around(yy + b) for a, b in ways[:-1]]
    ps2_s[...] = exchange(ps1_s, ps1, p1s, p1r, y, n, at_y, over_z, (start_home, wait_sends))
    sums = exchange(ps2_s, ps2, p2s, p2r, w, m, at_z, over_xy, (wait_home,))
    norm_old, curvature, applied2 = sums[:, 0:1], sums[:, 1:2], sums[:, 2:3]
    alpha = norm_old / curvature
    norm_new = jnp.maximum(alpha * alpha * applied2 - norm_old, 0.0)
    out_alpha[...] = jnp.broadcast_to(alpha, (1, cols))
    out_beta[...] = jnp.broadcast_to(norm_new / norm_old, (1, cols))

    for s in range(slab):
        @pl.when(jnp.logical_not(from_self(s)))
        def _():
            remote(fin.at[0], out_app.at[:, s], fs.at[0], fr.at[s], dev(s, around(pos[s] - shift(s)), slab * pos[s] + s, core)).wait_recv()

    for recv, ssem, rsem, size, there in ((ps1, p1s, p1r, n, at_y(up_y)), (ps2, p2s, p2r, m, at_z(up_z))):
        others = recv.at[pl.ds(0, size - 1)]
        remote(others, others, ssem, rsem, there).wait_send()


def matrix(length, rows):
    k = np.arange(length)
    angle = 2.0 * np.pi / length * (np.outer(k, k) % length)
    c, s = np.cos(angle), np.sin(angle)
    g = np.block([[c, s], [-s, c]])
    blocks = length // rows
    order = np.arange(2 * length).reshape(2, blocks, rows).transpose(1, 0, 2).reshape(-1)
    g = g[order][:, order]
    g = g.astype(np.float32)
    h = g.astype(ml_dtypes.bfloat16)
    return np.stack([h, (g - h.astype(np.float32)).astype(ml_dtypes.bfloat16)])


def body(n, m, solution, residual, sensitivity, sampling):
    _, slab, rows, cols = solution.shape
    coils = sensitivity.shape[1]
    full = n * rows
    g = jnp.asarray(matrix(full, LANES))
    vmem = pl.BlockSpec(memory_space=pltpu.VMEM)
    hbm = pl.BlockSpec(memory_space=pl.ANY)
    dma = pltpu.SemaphoreType.DMA
    chunk = (2, rows, cols)

    def f32(*shape):
        return pltpu.VMEM(shape, F32)

    def bf16(*shape):
        return pltpu.VMEM(shape, BF16)

    applied, alpha, beta = pl.pallas_call(
        functools.partial(kernel, n, m),
        out_shape=(jax.ShapeDtypeStruct(solution.shape, F32),) + 2 * (jax.ShapeDtypeStruct((1, cols), F32),),
        in_specs=5 * [hbm],
        out_specs=(hbm, vmem, vmem),
        scratch_shapes=[
            f32(*solution.shape), f32(*residual.shape), bf16(*sensitivity.shape),
            f32(coils, slab, *chunk), f32(slab, 2 * NX, *chunk), f32(n, *chunk), f32(slab, *chunk), f32(n, *chunk),
            bf16(2 * LANES, cols), bf16(2 * LANES, cols), f32(2 * full, cols), bf16(2 * full, cols), bf16(2 * full, cols),
            pltpu.VMEM(sampling.shape, sampling.dtype), bf16(*g.shape),
            f32(n, *chunk), f32(n // 2, *chunk), f32(n // 2, *chunk), f32(n // 2 // NX, NX, *chunk), f32(2, *chunk),
            f32(*solution.shape), f32(slab, *chunk), f32(n // 2 // NX, *chunk),
            f32(2, *chunk), f32(8, cols), f32(8, cols), f32(*chunk), f32(*chunk), f32(8, cols), f32(8, cols),
            f32(1, LANES), f32(n, 1, LANES), f32(1, LANES), f32(m, 1, LANES),
            dma((5,)), dma((2 * NX * slab,)), dma((2 * NX * slab,)), dma((2 * NX * slab,)), dma((n // 2,)), dma((slab,)), dma((slab,)),
            dma((slab,)), dma((n,)), dma((n // 2 // NX * NX,)), dma((n // 2,)),
            dma((n // 2,)), dma((n // 2,)), dma((n // 2,)), dma((n // 2,)), dma((n // 2 // NX,)), dma((slab,)),
            dma((5,)), dma((5,)), dma((slab,)), dma((n // 2 // NX,)), dma, dma, dma, dma,
        ],
        compiler_params=pltpu.CompilerParams(
            collective_id=0, has_side_effects=True, vmem_limit_bytes=56 * 1024 * 1024
        ),
        name="iteration",
    )(solution, residual, sensitivity, sampling, g)
    alpha, beta = alpha[0], beta[0]
    new_residual = residual - alpha * applied
    return solution + alpha * residual, new_residual, new_residual + beta * residual


def solution(mesh):
    n, m = mesh.shape["gy"], mesh.shape["gz"]
    field = P(None, "gz", "gy", None)
    return jax.shard_map(
        functools.partial(body, n, m),
        mesh=mesh,
        in_specs=(field, field, P(None, None, "gz", "gy", None), P()),
        out_specs=(field, field, field),
        check_vma=False,
    )
```

```python
import functools

import jax
import jax.numpy as jnp
import ml_dtypes
import numpy as np
from jax import lax
from jax.experimental import pallas as pl
from jax.experimental.pallas import tpu as pltpu
from jax.sharding import PartitionSpec as P

TV_EPS = 0.1
TV_WEIGHT = 0.1
TIKHONOV = 0.1
MESH = pl.DeviceIdType.MESH
F32 = jnp.float32
BF16 = jnp.bfloat16
LANES = 128
NX = 4


def split(x):
    high = x.astype(BF16)
    return high, (x - high.astype(F32)).astype(BF16)


def dot(a, b):
    return jnp.dot(a, b, preferred_element_type=F32)


def dot3(ah, al, bh, bl):
    return dot(ah, bh) + (dot(ah, bl) + dot(al, bh))


def fold(x):
    parts = [
        x[r : r + 8, c : c + LANES] for r in range(0, x.shape[0], 8) for c in range(0, x.shape[1], LANES)
    ]
    return functools.reduce(jnp.add, parts)


def total(x):
    return jnp.sum(jnp.sum(x, axis=0, keepdims=True), axis=1, keepdims=True)


def interleave(a, b):
    parts = []
    for i in range(a.shape[1] // LANES):
        parts += [a[:, i * LANES : (i + 1) * LANES], b[:, i * LANES : (i + 1) * LANES]]
    return jnp.concatenate(parts, axis=1)


def part_of(v, i):
    return jnp.concatenate([v[:, (2 * b + i) * LANES : (2 * b + i + 1) * LANES] for b in range(v.shape[1] // LANES // 2)], axis=1)


def kernel(
    n, m, sol_in, res_in, sens_in, samp_in, g_in,
    out_app, out_alpha, out_beta,
    sol, res, sens, sbuf, relay, srecv, xrel, xall, vh, vl, yacc, yh, yl, samp, g,
    part, pair, tot, gath, fin, smooth, local, local_in,
    hz, hy_s, hy, qz_s, qz, qy_s, qy, ps1_s, ps1, ps2_s, ps2,
    csem, xls, xlr, zs, zr, xrs, xrr, xzs, xar, ms, os,
    prs, prr, gs, gr, fs, fr, hs, hr, ls, lr, p1s, p1r, p2s, p2r,
):
    y = lax.axis_index("gy")
    w = lax.axis_index("gz")
    z, core = y // 2, lax.rem(y, 2)
    x, yy = w // NX, lax.rem(w, NX)
    nz = n // 2
    slab, rows, cols = res.shape[1:]
    sib = 1 - core
    pos = (x, yy)
    odd = lax.rem(z, 2)
    lp = (1 - odd) * x + odd * yy
    sp = z // 2
    l = 2 * lp + core
    line = 2 * NX

    def dev(j, p, z_, core_):
        return (2 * z_ + core_, NX * x + p if j else NX * p + yy)

    def on_line(p, z_, core_):
        return (2 * z_ + core_, (1 - odd) * (NX * p + yy) + odd * (NX * x + p))

    def at_y(t):
        return (t, w)

    def at_z(t):
        return (y, t)

    other = (yy, x)

    def around(t):
        return lax.rem(t + 4 * NX, NX)

    def shift(j):
        return sp + other[j] + 2 * j

    def rows_at(k):
        return around(sp - x - yy - 2 * odd - k)

    def remote(src, dst, ssem, rsem, device):
        return pltpu.make_async_remote_copy(
            src_ref=src, dst_ref=dst, send_sem=ssem, recv_sem=rsem, device_id=device, device_id_type=MESH
        )

    def loop(lo, hi, f):
        def step(i, c):
            f(i)
            return c

        lax.fori_loop(lo, hi, step, 0)

    loads = [
        pltpu.make_async_copy(a, b, csem.at[i])
        for i, (a, b) in enumerate([(sens_in, sens), (res_in, res), (sol_in, sol), (g_in, g), (samp_in, samp)])
    ]
    for c in loads:
        c.start()

    barrier = pltpu.get_barrier_semaphore()

    def hail(device):
        pl.semaphore_signal(barrier, inc=1, device_id=device, device_id_type=MESH)

    loop(1, n, lambda k: hail(at_y(lax.rem(y + k, n))))
    loop(1, m, lambda k: hail(at_z(lax.rem(w + k, m))))
    for j in range(slab):
        loop(1, NX, lambda k: hail(dev(j, lax.rem(pos[j] + k, NX), z, sib)))
        hail(dev(j, around(pos[j] - shift(j)), slab * pos[j] + j, core))

    def from_self(j):
        return jnp.logical_and(around(shift(j)) == 0, slab * pos[j] + j == z)

    def widen(c):
        for j in range(slab):
            sbuf[c, j, 0] = sens[0, c, j].astype(F32)
            sbuf[c, j, 1] = sens[1, c, j].astype(F32)

    loads[0].wait()
    loop(0, line, widen)
    loads[1].wait()

    up_y, down_y = lax.rem(y + 1, n), lax.rem(y + n - 1, n)
    up_z, down_z = lax.rem(w + 1, m), lax.rem(w + m - 1, m)
    pl.semaphore_wait(barrier, n + m - 2 + slab * NX)

    def pass_on(src, j, t):
        zt = slab * (t // 2) + j
        slot = 2 * z + lax.rem(t, 2)
        cp = remote(src, srecv.at[slot], zs.at[line * j + t], zr.at[z], dev(0, x, zt, core))
        return zt, slot, cp

    def pass_both(j, p):
        zt = slab * p + j
        both = pl.ds(2 * p, 2)
        cp = remote(relay.at[j, both], srecv.at[pl.ds(2 * z, 2)], zs.at[line * j + 2 * p], zr.at[z], dev(0, x, zt, core))
        return zt, both, cp

    def forward_maps(src, j, t):
        zt, slot, cp = pass_on(src, j, t)

        @pl.when(zt != z)
        def _():
            cp.start()

        @pl.when(zt == z)
        def _():
            srecv[slot] = src[...]

    def maps_over(j, p, c):
        t = 2 * p + c
        me = 2 * pos[j] + core
        return remote(sbuf.at[t, j], relay.at[j, me], xls.at[line * j + t], xlr.at[line * j + me], dev(j, p, z, c))

    def moved(j):
        return around(shift(j)) != 0

    def res_over(j):
        return remote(res.at[:, j], xrel.at[j], xrs.at[j], xrr.at[j], dev(j, around(pos[j] - shift(j)), z, core))

    for j in range(slab):
        @pl.when(moved(j))
        def _():
            res_over(j).start()

        @pl.when(jnp.logical_not(moved(j)))
        def _():
            xrel[j] = res[:, j]

    for j in range(slab):
        t = 2 * pos[j] + core
        forward_maps(sbuf.at[t, j], j, t)
        maps_over(j, pos[j], sib).start()

    steps = [(k, c) for k in range(NX) for c in (core, sib)]

    def hops(j, k):
        return around(shift(j) + k) != 0

    for k, c in steps:
        for j in range(slab):
            @pl.when(hops(j, k))
            def _():
                maps_over(j, around(pos[j] - shift(j) - k), c).start()

    halo1 = [
        remote(sol.at[:, 0], hz.at[0], hs.at[0], hr.at[0], at_z(down_z)),
        remote(res.at[:, 0], hz.at[1], hs.at[1], hr.at[1], at_z(down_z)),
        remote(hy_s, hy, hs.at[2], hr.at[2], at_y(down_y)),
    ]
    loads[2].wait()
    for f, field in enumerate((sol, res)):
        for p in range(2):
            for s in range(slab):
                i = f * 2 * slab + p * slab + s
                hy_s[i : i + 1, :] = field[p, s, 0:1, :]

    for h in halo1:
        h.start()

    def got_maps(j, p, c):
        t = 2 * p + c
        remote(sbuf.at[t, j], relay.at[j, t], xls.at[line * j + t], xlr.at[line * j + t], dev(j, p, z, c)).wait_recv()

    def relay_maps(j, p):
        got_maps(j, p, core)
        got_maps(j, p, sib)
        zt, both, cp = pass_both(j, p)

        @pl.when(zt != z)
        def _():
            cp.start()

        @pl.when(zt == z)
        def _():
            srecv[pl.ds(2 * z, 2)] = relay[j, both]

    def forward_res(j):
        zt = slab * around(pos[j] + shift(j)) + j
        return zt, remote(xrel.at[j], xall.at[y], xzs.at[j], xar.at[y], dev(0, x, zt, core))

    for j in range(slab):
        @pl.when(moved(j))
        def _():
            res_over(j).wait_recv()

        zt, cp = forward_res(j)

        @pl.when(zt != z)
        def _():
            cp.start()

        @pl.when(zt == z)
        def _():
            xall[y] = xrel[j]

    for j in range(slab):
        t = 2 * pos[j] + sib
        got_maps(j, pos[j], sib)
        forward_maps(relay.at[j, t], j, t)

    for k in range(NX):
        for j in range(slab):
            @pl.when(hops(j, k))
            def _():
                relay_maps(j, around(pos[j] + shift(j) + k))

    for h in halo1:
        h.wait_recv()
    row = lax.broadcasted_iota(jnp.int32, (rows, cols), 0)
    col = lax.broadcasted_iota(jnp.int32, (rows, cols), 1)
    keep_y = jnp.logical_or(row < rows - 1, y < n - 1)
    keep_z = jnp.full((rows, cols), w, jnp.int32) < m - 1

    def ahead(f, field, p, s):
        v = field[p, s]
        dx = jnp.where(col == cols - 1, 0.0, pltpu.roll(v, cols - 1, 1) - v)
        i = f * 2 * slab + p * slab + s
        nxt = jnp.where(row == rows - 1, jnp.broadcast_to(hy[i : i + 1, :], (rows, cols)), pltpu.roll(v, rows - 1, 0))
        dy = jnp.where(keep_y, nxt - v, 0.0)
        if s + 1 < slab:
            dz = field[p, s + 1] - v
        else:
            dz = jnp.where(keep_z, hz[f, p] - v, 0.0)
        return dx, dy, dz

    qy_s[...] = jnp.zeros_like(qy_s)
    for s in range(slab):
        sq = jnp.zeros((rows, cols), F32)
        for p in range(2):
            for d in ahead(0, sol, p, s):
                sq = sq + d * d
        weight = 1.0 / jnp.sqrt(sq + TV_EPS * TV_EPS)
        for p in range(2):
            dx, dy, dz = (weight * d for d in ahead(1, res, p, s))
            before_x = jnp.where(col == 0, 0.0, pltpu.roll(dx, 1, 1))
            before_y = jnp.where(row == 0, 0.0, pltpu.roll(dy, 1, 0))
            here = (before_x - dx) + (before_y - dy) - dz
            if s > 0:
                here = here + qz_s[p]
            smooth[p, s] = here
            qz_s[p] = dz
            i = p * slab + s
            qy_s[i : i + 1, :] = dy[rows - 1 : rows, :]
    halo2 = [
        remote(qz_s, qz, hs.at[3], hr.at[3], at_z(up_z)),
        remote(qy_s, qy, hs.at[4], hr.at[4], at_y(up_y)),
    ]
    for h in halo2:
        h.start()

    first = 2 * rows_at(0)

    def hand(slot, i, k):
        p = around(lp + k)
        return remote(xall.at[slot], xall.at[slot], ms.at[i * NX + k], xar.at[slot], on_line(p, z, core))

    def to_other(zz):
        slot = 2 * zz + core
        return remote(xall.at[slot], xall.at[slot], os.at[zz], xar.at[slot], on_line(lp, z, sib))

    for i in range(nz // NX):
        zz = first + i
        slot = 2 * zz + core

        @pl.when(zz != z)
        def _():
            remote(xrel.at[0], xall.at[slot], xzs.at[0], xar.at[slot], dev(0, x, zz, core)).wait_recv()

        for k in range(1, NX):
            hand(slot, i, k).start()
        to_other(zz).start()

    for k in range(1, NX):
        for i in range(nz // NX):
            zz = 2 * rows_at(k) + i
            slot = 2 * zz + core
            remote(xall.at[slot], xall.at[slot], ms.at[0], xar.at[slot], on_line(around(lp + k), z, core)).wait_recv()
            to_other(zz).start()

    per = 4
    tile = per * rows
    groups = n // per

    def ready(zz):
        @pl.when(zz != z)
        def _():
            both = srecv.at[pl.ds(2 * zz, 2)]
            remote(relay.at[0, pl.ds(0, 2)], both, zs.at[0], zr.at[zz], dev(0, x, zz, core)).wait_recv()

        s = 2 * zz + sib
        remote(xall.at[s], xall.at[s], os.at[0], xar.at[s], on_line(lp, z, sib)).wait_recv()

    at_zero = jnp.full((rows, cols), w, jnp.int32) > 0
    at_top = jnp.logical_and(row == 0, y > 0)

    def local_over(j):
        there = dev(j, around(pos[j] - shift(j)), slab * pos[j] + j, core)
        return remote(local.at[j], local_in.at[odd], ls.at[j], lr.at[odd], there)

    def send_local():
        for h in halo2:
            h.wait_recv()
        for p in range(2):
            for s in range(slab):
                i = p * slab + s
                v = smooth[p, s] + jnp.where(at_top, jnp.broadcast_to(qy[i : i + 1, :], (rows, cols)), 0.0)
                if s == 0:
                    v = v + jnp.where(at_zero, qz[p], 0.0)
                local[s, p] = TIKHONOV * res[p, s] - TV_WEIGHT * v
        for j in range(slab):
            @pl.when(jnp.logical_not(from_self(j)))
            def _():
                local_over(j).start()

            @pl.when(from_self(j))
            def _():
                local_in[odd] = local[j]

    full = n * rows
    scale = 1.0 / (full * cols)
    yacc[...] = jnp.zeros_like(yacc)
    loads[3].wait()
    loads[4].wait()

    def forward(i):
        q = rows_at(i)
        last = i == groups - 1

        @pl.when(last)
        def _():
            send_local()

        for t in range(per // 2):
            ready(q * per // 2 + t)
        block = []
        for t in range(per):
            sr, si = srecv[q * per + t, 0], srecv[q * per + t, 1]
            xr, xi = xall[q * per + t, 0], xall[q * per + t, 1]
            block.append(interleave(sr * xr - si * xi, -(sr * xi + si * xr)))
        ah, al = split(jnp.concatenate(block, axis=0))
        v = dot3(ah, al, g[0], g[1])
        vh[:tile], vl[:tile] = split(part_of(v, 0))
        vh[tile:], vl[tile:] = split(-part_of(v, 1))

        def rows_tile(t):
            at = pl.ds(pl.multiple_of(2 * t * tile, 2 * tile), 2 * tile)
            k = pl.ds(pl.multiple_of(2 * q * tile, 2 * tile), 2 * tile)
            v = yacc[at] + dot3(g[0, at, k], g[1, at, k], vh[...], vl[...])

            @pl.when(jnp.logical_not(last))
            def _():
                yacc[at] = v

            @pl.when(last)
            def _():
                taken = samp[pl.ds(pl.multiple_of(t * tile, tile), tile)].astype(F32) * scale
                yh[at], yl[at] = split(v * jnp.concatenate([taken, -taken], axis=0))

        loop(0, groups, rows_tile)

    loop(0, groups, forward)

    def to_sib(zz):
        return remote(part.at[2 * zz + sib], pair.at[zz], prs.at[zz], prr.at[zz], on_line(lp, z, sib))

    def to_adder(zz):
        t = around(lp + rows_at(0) - zz // 2)
        i = lax.rem(zz, 2)
        return t, remote(tot.at[zz], gath.at[i, lp], gs.at[zz], gr.at[NX * i + lp], on_line(t, z, core))

    def add_pair(zz):
        to_sib(zz).wait_recv()
        tot[zz] = part[2 * zz + core] + pair[zz]
        t, cp = to_adder(zz)

        @pl.when(t != lp)
        def _():
            cp.start()

    def home(i):
        zz = first + i
        return zz, remote(fin.at[i], out_app.at[:, odd], fs.at[i], fr.at[odd], on_line(sp, zz, core))

    def add_line(i, sums):
        zz = first + i
        v = tot[zz]
        for k in range(1, NX):
            t = around(lp + k)
            remote(tot.at[zz], gath.at[i, t], gs.at[zz], gr.at[NX * i + t], on_line(t, z, core)).wait_recv()
            v = v + gath[i, t]

        @pl.when(jnp.logical_not(jnp.logical_and(sp == lp, zz == z)))
        def _():
            remote(local.at[0], local_in.at[i], ls.at[0], lr.at[i], on_line(sp, zz, core)).wait_recv()

        v = v + local_in[i]
        for p in range(2):
            a, r = v[p], xall[2 * zz + core, p]
            for k, term in enumerate((r * r, r * a, a * a)):
                sums[k] = sums[k] + fold(term)
        fin[i] = v

    def block_at(i):
        return rows_at(2 - i + (i // 2) * (2 * i - 1) - (i // 3) * 4)

    def inverse(i):
        q = block_at(i)
        at = pl.ds(pl.multiple_of(2 * q * tile, 2 * tile), 2 * tile)
        v = dot3(g[0, at], g[1, at], yh[...], yl[...])
        ah, al = split(interleave(v[:tile], -v[tile:]))
        v = dot3(ah, al, g[0], g[1])
        re, im = part_of(v, 0), part_of(v, 1)
        for t in range(per):
            s = q * per + t
            vr, vi = re[t * rows : (t + 1) * rows], im[t * rows : (t + 1) * rows]
            sr, si = srecv[s, 0], srecv[s, 1]
            part[s, 0] = sr * vr + si * vi
            part[s, 1] = sr * vi - si * vr
        for t in range(per // 2):
            to_sib(q * per // 2 + t).start()

        @pl.when(i > 0)
        def _():
            for t in range(per // 2):
                add_pair(block_at(i - 1) * per // 2 + t)

    loop(0, groups, inverse)
    for t in range(per // 2):
        add_pair(first + t)
    sums = [jnp.zeros((8, LANES), F32) for _ in range(3)]
    for i in range(nz // NX):
        add_line(i, sums)
    sums = [total(v) for v in sums]
    lane = lax.broadcasted_iota(jnp.int32, (1, LANES), 1)
    ps1_s[...] = jnp.where(lane == 0, sums[0], jnp.where(lane == 1, sums[1], sums[2]))

    def stay(i):
        return pltpu.make_async_copy(fin.at[i], out_app.at[:, odd], csem.at[0])

    def start_home():
        for i in range(nz // NX):
            zz, cp = home(i)

            @pl.when(jnp.logical_not(jnp.logical_and(sp == lp, zz == z)))
            def _():
                cp.start()

            @pl.when(jnp.logical_and(sp == lp, zz == z))
            def _():
                stay(i).start()

    def wait_home():
        for i in range(nz // NX):
            zz, cp = home(i)

            @pl.when(jnp.logical_not(jnp.logical_and(sp == lp, zz == z)))
            def _():
                cp.wait_send()

            @pl.when(jnp.logical_and(sp == lp, zz == z))
            def _():
                stay(i).wait()

    def wait_sends():
        for h in halo1 + halo2:
            h.wait_send()
        for j in range(slab):
            @pl.when(moved(j))
            def _():
                res_over(j).wait_send()

            @pl.when(jnp.logical_not(from_self(j)))
            def _():
                local_over(j).wait_send()

            maps_over(j, pos[j], sib).wait_send()
            for k, c in steps:
                @pl.when(hops(j, k))
                def _():
                    maps_over(j, around(pos[j] - shift(j) - k), c).wait_send()

            for c in (core, sib):
                zt, _, cp = pass_on(sbuf.at[0, j], j, 2 * pos[j] + c)

                @pl.when(zt != z)
                def _():
                    cp.wait_send()

            for k in range(1, NX):
                zt, _, cp = pass_both(j, around(pos[j] + k))

                @pl.when(zt != z)
                def _():
                    cp.wait_send()

            zt, cp = forward_res(j)

            @pl.when(zt != z)
            def _():
                cp.wait_send()

        for i in range(nz // NX):
            for k in range(1, NX):
                hand(2 * (first + i) + core, i, k).wait_send()

        def sent_sums(zz):
            to_other(zz).wait_send()
            to_sib(zz).wait_send()
            t, cp = to_adder(zz)

            @pl.when(t != lp)
            def _():
                cp.wait_send()

        loop(0, nz, sent_sums)

    def exchange(send, recv, ssem, rsem, me, size, where, targets, meanwhile):
        recv[me] = send[...]

        for t in targets:
            remote(send, recv.at[me], ssem, rsem, where(t)).start()

        for f in meanwhile:
            f()
        others = recv.at[pl.ds(0, size - 1)]
        remote(others, others, ssem, rsem, where(lax.rem(me + 1, size))).wait_recv()
        return functools.reduce(jnp.add, [recv[i] for i in range(size)])

    over_z = [2 * lax.rem(z + d, nz) + c for d in (4, 3, 5, 2, 6, 1, 7) for c in (sib, core)] + [2 * z + sib]
    ways = sorted(((a, b) for a in range(NX) for b in range(NX)), key=lambda d: -min(d[0], NX - d[0]) - min(d[1], NX - d[1]))
    over_xy = [NX * around(x + a) + around(yy + b) for a, b in ways[:-1]]
    ps2_s[...] = exchange(ps1_s, ps1, p1s, p1r, y, n, at_y, over_z, (start_home, wait_sends))
    sums = exchange(ps2_s, ps2, p2s, p2r, w, m, at_z, over_xy, (wait_home,))
    norm_old, curvature, applied2 = sums[:, 0:1], sums[:, 1:2], sums[:, 2:3]
    alpha = norm_old / curvature
    norm_new = jnp.maximum(alpha * alpha * applied2 - norm_old, 0.0)
    out_alpha[...] = jnp.broadcast_to(alpha, (1, cols))
    out_beta[...] = jnp.broadcast_to(norm_new / norm_old, (1, cols))

    for s in range(slab):
        @pl.when(jnp.logical_not(from_self(s)))
        def _():
            remote(fin.at[0], out_app.at[:, s], fs.at[0], fr.at[s], dev(s, around(pos[s] - shift(s)), slab * pos[s] + s, core)).wait_recv()

    for recv, ssem, rsem, size, there in ((ps1, p1s, p1r, n, at_y(up_y)), (ps2, p2s, p2r, m, at_z(up_z))):
        others = recv.at[pl.ds(0, size - 1)]
        remote(others, others, ssem, rsem, there).wait_send()


def matrix(length, rows):
    k = np.arange(length)
    angle = 2.0 * np.pi / length * (np.outer(k, k) % length)
    c, s = np.cos(angle), np.sin(angle)
    g = np.block([[c, s], [-s, c]])
    blocks = length // rows
    order = np.arange(2 * length).reshape(2, blocks, rows).transpose(1, 0, 2).reshape(-1)
    g = g[order][:, order]
    g = g.astype(np.float32)
    h = g.astype(ml_dtypes.bfloat16)
    return np.stack([h, (g - h.astype(np.float32)).astype(ml_dtypes.bfloat16)])


def body(n, m, solution, residual, sensitivity, sampling):
    _, slab, rows, cols = solution.shape
    coils = sensitivity.shape[1]
    full = n * rows
    g = jnp.asarray(matrix(full, LANES))
    vmem = pl.BlockSpec(memory_space=pltpu.VMEM)
    hbm = pl.BlockSpec(memory_space=pl.ANY)
    dma = pltpu.SemaphoreType.DMA
    chunk = (2, rows, cols)

    def f32(*shape):
        return pltpu.VMEM(shape, F32)

    def bf16(*shape):
        return pltpu.VMEM(shape, BF16)

    applied, alpha, beta = pl.pallas_call(
        functools.partial(kernel, n, m),
        out_shape=(jax.ShapeDtypeStruct(solution.shape, F32),) + 2 * (jax.ShapeDtypeStruct((1, cols), F32),),
        in_specs=5 * [hbm],
        out_specs=(hbm, vmem, vmem),
        scratch_shapes=[
            f32(*solution.shape), f32(*residual.shape), bf16(*sensitivity.shape),
            f32(coils, slab, *chunk), f32(slab, 2 * NX, *chunk), f32(n, *chunk), f32(slab, *chunk), f32(n, *chunk),
            bf16(2 * LANES, cols), bf16(2 * LANES, cols), f32(2 * full, cols), bf16(2 * full, cols), bf16(2 * full, cols),
            pltpu.VMEM(sampling.shape, sampling.dtype), bf16(*g.shape),
            f32(n, *chunk), f32(n // 2, *chunk), f32(n // 2, *chunk), f32(n // 2 // NX, NX, *chunk), f32(2, *chunk),
            f32(*solution.shape), f32(slab, *chunk), f32(n // 2 // NX, *chunk),
            f32(2, *chunk), f32(8, cols), f32(8, cols), f32(*chunk), f32(*chunk), f32(8, cols), f32(8, cols),
            f32(1, LANES), f32(n, 1, LANES), f32(1, LANES), f32(m, 1, LANES),
            dma((5,)), dma((2 * NX * slab,)), dma((2 * NX * slab,)), dma((2 * NX * slab,)), dma((n // 2,)), dma((slab,)), dma((slab,)),
            dma((slab,)), dma((n,)), dma((n // 2 // NX * NX,)), dma((n // 2,)),
            dma((n // 2,)), dma((n // 2,)), dma((n // 2,)), dma((n // 2,)), dma((n // 2 // NX,)), dma((slab,)),
            dma((5,)), dma((5,)), dma((slab,)), dma((n // 2 // NX,)), dma, dma, dma, dma,
        ],
        compiler_params=pltpu.CompilerParams(
            collective_id=0, has_side_effects=True, vmem_limit_bytes=56 * 1024 * 1024
        ),
        name="iteration",
    )(solution, residual, sensitivity, sampling, g)
    alpha, beta = alpha[0], beta[0]
    new_residual = residual - alpha * applied
    return solution + alpha * residual, new_residual, new_residual + beta * residual


def solution(mesh):
    n, m = mesh.shape["gy"], mesh.shape["gz"]
    field = P(None, "gz", "gy", None)
    return jax.shard_map(
        functools.partial(body, n, m),
        mesh=mesh,
        in_specs=(field, field, P(None, None, "gz", "gy", None), P()),
        out_specs=(field, field, field),
        check_vma=False,
    )
```
